32 devices in a mesh: parts: 2 (over y), cells: 4 (over z), blk: 4 (over x, core).
Axes of the slice: x: 2, y: 2, z: 4, core: 2. Of those that a mesh axis runs over, the one named last changes fastest.
Arguments:
- expression: bfloat16 [4096, 4096], P(('parts', 'cells'), 'blk'), parts along dimension 0, may hold values from 0.02 to 36, as said below
- cell_type: int32 [4096], P(('parts', 'cells')), parts along dimension 0, may hold values from 0 to 3, as said below
- size_factor: bfloat16 [4096], P(('parts', 'cells')), parts along dimension 0, may hold values from 0.19921875 to 5
- gene_mean: float32 [8192], P(('parts', 'blk')), parts along dimension 0, may hold values from 0.2 to 3
Outputs:
- correlation: bfloat16 [8, 4096, 4096], P(('parts', 'cells'), 'blk'), parts along dimension 0
The draws below stay inside these ranges and needn't reach their ends.
There are 2 independent parts, one for each index of `parts`. The reference program is written for one: setup_inputs(seed, part) draws one part's arguments, and reference() takes and returns one part's arrays. A program takes and returns all parts, laid end to end along the dimension named above; each array names one. Nothing has to cross between parts.
Inputs may be any that keep to these rules, and one draw needn't show every extreme that they name: `cell_type`: each storage shard of 512 cells in a row holds at most 256 cells of one type and at least one cell of every type; one type has exactly 256 cells in every shard. `expression`: positive levels.
All inputs are finite; a program needn't handle non-finite values.
Results may differ from the reference program's by a relative error of at most 0.0027.
Values may be sent and summed in bfloat16 or wider, within the bound.
No kernel may reach another device: no remote copies, remote signals or barrier semaphores. Data moves between devices by JAX's collectives and lax.ppermute only.
A program may use at most 128 MiB of HBM per device.

```python
import math
import jax
import jax.numpy as jnp
from jax import lax

G = 4096
CELL_DEV = 512
TYPES = 4
CAP = 256
CELLS = 2048


def draw_cell_type(key, part):
    key = jax.random.fold_in(key, 11)
    full_type = jax.random.randint(jax.random.fold_in(key, 1), (), 0, TYPES)
    slot_type = jnp.arange(TYPES * CAP, dtype=jnp.int32) // CAP
    slot_rank = jnp.arange(TYPES * CAP, dtype=jnp.int32) % CAP
    boost = jnp.where(slot_type == full_type, 4 * TYPES * CAP, jnp.where(slot_rank == 0, 2 * TYPES * CAP, 0)).astype(jnp.int32)

    def one_shard(shard_key):
        scores = jax.random.permutation(jax.random.fold_in(shard_key, 1), TYPES * CAP).astype(jnp.int32) + boost
        _, chosen = lax.top_k(scores, CELL_DEV)
        picked = slot_type[chosen]
        return picked[jax.random.permutation(jax.random.fold_in(shard_key, 2), CELL_DEV)]
    shard_keys = jax.random.split(jax.random.fold_in(key, 2), TYPES)
    return jax.vmap(one_shard)(shard_keys).reshape(-1).astype(jnp.int32)


def draw_expression(key, part):
    key = jax.random.fold_in(key, 23)
    base_noise = jnp.clip(jax.random.normal(key, (CELLS, G), jnp.float32), -4.0, 4.0)
    mixed_noise = base_noise + 0.6 * jnp.roll(base_noise, 1, axis=1) + 0.45 * jnp.roll(base_noise, 29, axis=1)
    return jnp.exp(0.35 * mixed_noise).astype(jnp.bfloat16)


def levels(rng, dims, cuts, smallest, high):
    loudness = 1.0
    for axis_at, shards_of in cuts:
        steps = jax.random.uniform(jax.random.fold_in(jax.random.fold_in(rng, 6), axis_at), (shards_of,), jnp.float32, smallest / len(cuts), high / len(cuts))
        loudness = loudness * jnp.repeat(jnp.exp(steps), dims[axis_at] // shards_of).reshape((-1,) + (1,) * (len(dims) - 1 - axis_at))
    return loudness


def setup_inputs(seed: int = 0, part: int = 0) -> dict:
    seeds = jax.random.split(jax.random.key(seed), 5)
    part_splits = jax.random.split(jax.random.fold_in(seeds[4], part), 5)
    expression = draw_expression(jax.random.fold_in(jax.random.fold_in(seeds[4], part), 71), part)
    cell_type = draw_cell_type(jax.random.fold_in(jax.random.fold_in(seeds[4], part), 71), part)
    size_factor = jnp.clip(jnp.exp(math.log(5.0) - 3.2227897 * jax.random.uniform(part_splits[2], (CELLS,), jnp.float32) ** levels(part_splits[2], (CELLS,), ((0, 4),), -0.2, 0.2)), 0.19921875, 5.0).astype(jnp.bfloat16)
    gene_mean = jnp.clip(jnp.exp(math.log(3.0) - 2.7080502 * jax.random.uniform(part_splits[3], (G,), jnp.float32) ** levels(part_splits[3], (G,), ((0, 4),), -0.2, 0.2)), 0.2, 3.0)
    return dict(expression=expression, cell_type=cell_type, size_factor=size_factor, gene_mean=gene_mean)


dispersion = 100.0
epsilon = 1e-05

def standardize(values, factors, gene_mean, is_valid):
    live = is_valid[:, None]
    expected = jnp.where(live, factors[:, None] * gene_mean[None, :], 1.0)
    residual = jnp.where(live, (values.astype(jnp.float32) - expected) / jnp.sqrt(expected + expected * expected / dispersion), 0.0)
    live_count = jnp.sum(is_valid.astype(jnp.float32))
    center = lax.optimization_barrier(jnp.sum(residual, axis=0)) / live_count
    centered = jnp.where(live, residual - center[None, :], 0.0)
    spread = lax.optimization_barrier(jnp.sum(centered * centered, axis=0)) / live_count
    scaled = (centered * lax.rsqrt(spread + epsilon)[None, :]).astype(jnp.bfloat16)
    return (scaled, live_count)

def cross_gram(left_panel, right_panel):
    return lax.dot_general(left_panel, right_panel, (((0,), (0,)), ((), ())), preferred_element_type=jnp.float32)

def reference(expression, cell_type, size_factor, gene_mean):
    slot_rows = TYPES * CAP
    by_type = jnp.argsort(cell_type, stable=True)
    counts = lax.optimization_barrier(jnp.sum((cell_type[:, None] == jnp.arange(TYPES, dtype=jnp.int32)[None, :]).astype(jnp.int32), axis=0))
    starts = (jnp.cumsum(counts) - counts).astype(jnp.int32)
    sorted_expr = jnp.concatenate([expression[by_type], jnp.zeros((slot_rows, G), jnp.bfloat16)], axis=0)
    sorted_factor = jnp.concatenate([size_factor[by_type].astype(jnp.float32), jnp.zeros((slot_rows,), jnp.float32)])

    def one_type(type_index):
        first_row = starts[type_index].astype(jnp.int32)
        values = lax.dynamic_slice_in_dim(sorted_expr, first_row, slot_rows, 0)
        factors = lax.dynamic_slice_in_dim(sorted_factor, first_row, slot_rows, 0)
        is_valid = jnp.arange(slot_rows, dtype=jnp.int32) < counts[type_index].astype(jnp.int32)
        scaled, live_count = standardize(values, factors, gene_mean, is_valid)
        return (cross_gram(scaled, scaled) / live_count).astype(jnp.bfloat16)
    return lax.map(one_type, jnp.arange(TYPES, dtype=jnp.int32))
```

```python
import functools

import jax
import jax.numpy as jnp
from jax import lax
from jax.experimental import pallas as pl
from jax.experimental.pallas import tpu as pltpu
from jax.sharding import PartitionSpec as P

dispersion = 100.0
epsilon = 1e-05
TILE = 16
VMEM = 48 * 1024 * 1024

whole = pl.BlockSpec(memory_space=pltpu.VMEM)


def pack_kernel(types, cap, widths, home_ref, type_ref, factor_ref, expr_ref, *outs):
    rows = expr_ref.shape[0]
    home = home_ref[0]
    kind = type_ref[...]
    rel = jnp.where(kind >= home, kind - home, kind - home + types)
    lines = max(types, 8)
    hot = lax.broadcasted_iota(jnp.int32, (lines, rows), 0) == rel
    hot_f = jnp.where(hot, 1.0, 0.0)
    upper = jnp.where(
        lax.broadcasted_iota(jnp.int32, (rows, rows), 0)
        <= lax.broadcasted_iota(jnp.int32, (rows, rows), 1),
        1.0,
        0.0,
    ).astype(jnp.bfloat16)
    running = jnp.dot(hot_f.astype(jnp.bfloat16), upper, preferred_element_type=jnp.float32)
    rank = jnp.sum(hot_f * running, axis=0, keepdims=True) - 1.0
    slot = rel * cap + rank.astype(jnp.int32)
    factor = jnp.broadcast_to(factor_ref[...].astype(jnp.float32), (TILE, rows)).astype(
        jnp.bfloat16
    )
    values = expr_ref[...]
    for j in range(types):
        place = jnp.where(
            lax.broadcasted_iota(jnp.int32, (cap, rows), 0) + j * cap == slot, 1.0, 0.0
        ).astype(jnp.bfloat16)
        block = jnp.dot(place, values, preferred_element_type=jnp.float32).astype(jnp.bfloat16)
        start = 0
        for k, width in enumerate(widths):
            outs[k * types + j][0:cap, :] = block[:, start : start + width]
            start += width
        line = lax.dot_general(
            factor, place, (((1,), (1,)), ((), ())), preferred_element_type=jnp.float32
        )
        row = lax.broadcasted_iota(jnp.int32, (TILE, 1), 0)
        width = widths[0]
        tail = jnp.zeros((TILE, min(width, cap)), jnp.float32)
        for i in range(pl.cdiv(cap, width)):
            tail = jnp.where(row == i, line[:, i * width : min((i + 1) * width, cap)], tail)
        outs[j][cap : cap + TILE, 0 : min(width, cap)] = tail.astype(jnp.bfloat16)


def pack(types, cap, widths, home, cell_type, size_factor, expression):
    rows = expression.shape[0]
    shapes = [
        jax.ShapeDtypeStruct((cap + (TILE if k == 0 else 0), width), jnp.bfloat16)
        for k, width in enumerate(widths)
        for _ in range(types)
    ]
    flat = pl.pallas_call(
        functools.partial(pack_kernel, types, cap, widths),
        out_shape=shapes,
        in_specs=[pl.BlockSpec(memory_space=pltpu.SMEM), whole, whole, whole],
        out_specs=[whole] * len(shapes),
        compiler_params=pltpu.CompilerParams(vmem_limit_bytes=VMEM),
        cost_estimate=pl.CostEstimate(
            flops=2 * types * cap * rows * expression.shape[1],
            bytes_accessed=3 * types * cap * expression.shape[1],
            transcendentals=0,
        ),
        name="pack",
    )(home, cell_type.reshape(1, rows), size_factor.reshape(1, rows), expression)
    return [flat[k * types : (k + 1) * types] for k in range(len(widths))]


def standardize_kernel(types, cap, lead, separate, mean_ref, *refs):
    blocks = refs[:types]
    tails = refs[types : 2 * types] if separate else blocks
    base = 0 if separate else cap
    refs = refs[2 * types :] if separate else refs[types:]
    scaled_ref, turned_ref, count_ref, work = refs
    mean = mean_ref[...]
    width = mean.shape[1]
    piece = min(lead, cap)
    total = jnp.zeros((1, width), jnp.float32)
    count = jnp.zeros((1, 1), jnp.float32)
    alive = []
    for j in range(types):
        column = jnp.zeros((cap, 1), jnp.float32)
        for i in range(pl.cdiv(cap, lead)):
            line = tails[j][base : base + TILE, 0:piece].astype(jnp.float32)[i : i + 1, :]
            diagonal = (
                lax.broadcasted_iota(jnp.int32, (cap, piece), 0)
                == lax.broadcasted_iota(jnp.int32, (cap, piece), 1) + i * lead
            )
            column += jnp.sum(jnp.where(diagonal, line, 0.0), axis=1, keepdims=True)
        live = column > 0.0
        alive.append(live)
        count += jnp.sum(jnp.where(live, 1.0, 0.0), axis=0, keepdims=True)
        expected = jnp.where(live, column * mean, 1.0)
        values = blocks[j][0:cap, :].astype(jnp.float32)
        residual = jnp.where(
            live,
            (values - expected) * lax.rsqrt(expected + expected * expected * (1.0 / dispersion)),
            0.0,
        )
        work[j * cap : (j + 1) * cap, :] = residual
        total += jnp.sum(residual, axis=0, keepdims=True)
    center = total / count
    square = jnp.zeros((1, width), jnp.float32)
    for j in range(types):
        centered = jnp.where(alive[j], work[j * cap : (j + 1) * cap, :] - center, 0.0)
        work[j * cap : (j + 1) * cap, :] = centered
        square += jnp.sum(centered * centered, axis=0, keepdims=True)
    scale = lax.rsqrt(square / count + epsilon)
    for j in range(types):
        scaled = work[j * cap : (j + 1) * cap, :] * scale
        scaled_ref[j * cap : (j + 1) * cap, :] = scaled.astype(jnp.bfloat16)
        work[j * cap : (j + 1) * cap, :] = scaled
    turned_ref[...] = jnp.transpose(work[...]).astype(jnp.bfloat16)
    count_ref[...] = jnp.broadcast_to(count, count_ref.shape)


def standardize(types, cap, lead, mean, blocks, first):
    width = mean.shape[1]
    separate = first is not blocks
    slots = types * cap
    specs = [whole] * (1 + types)
    args = [mean, *blocks]
    if separate:
        specs += [pl.BlockSpec((TILE, lead), lambda i: (cap // TILE, 0))] * types
        args += list(first)
    return pl.pallas_call(
        functools.partial(standardize_kernel, types, cap, lead, separate),
        grid=(1,),
        out_shape=[
            jax.ShapeDtypeStruct((slots, width), jnp.bfloat16),
            jax.ShapeDtypeStruct((width, slots), jnp.bfloat16),
            jax.ShapeDtypeStruct((8, 128), jnp.float32),
        ],
        in_specs=specs,
        out_specs=[whole] * 3,
        scratch_shapes=[pltpu.VMEM((slots, width), jnp.float32)],
        compiler_params=pltpu.CompilerParams(vmem_limit_bytes=VMEM),
        cost_estimate=pl.CostEstimate(
            flops=20 * slots * width,
            bytes_accessed=6 * slots * width,
            transcendentals=slots * width,
        ),
        name="standardize",
    )(*args)


def gram_kernel(parts, panels, aliased, place_ref, count_ref, *refs):
    left = refs[:parts]
    right = refs[parts : parts + panels]
    out_ref = refs[parts + panels + (1 if aliased else 0)]
    inverse = 1.0 / count_ref[0:1, 0:1]
    step = pl.program_id(0)
    for j in range(panels):

        @pl.when(step == j)
        def _(j=j):
            start = 0
            for piece in left:
                size = piece.shape[0]
                product = jnp.dot(piece[...], right[j][...], preferred_element_type=jnp.float32)
                out_ref[0, start : start + size, :] = (product * inverse).astype(jnp.bfloat16)
                start += size


def gram(shape, places, count, left, right, before):
    rows, columns = shape[1:]
    width = right[0].shape[1]
    slots = right[0].shape[0]
    aliased = before is not None
    args = [places, count, *left, *right] + ([before] if aliased else [])
    hold = pl.BlockSpec(memory_space=pltpu.VMEM)
    specs = [hold] * (1 + len(left) + len(right))
    specs += [pl.BlockSpec(memory_space=pl.ANY)] if aliased else []
    return pl.pallas_call(
        functools.partial(gram_kernel, len(left), len(right), aliased),
        grid_spec=pltpu.PrefetchScalarGridSpec(
            num_scalar_prefetch=1,
            grid=(len(right),),
            in_specs=specs,
            out_specs=pl.BlockSpec((1, rows, width), lambda i, place: (0, 0, place[i])),
        ),
        out_shape=jax.ShapeDtypeStruct(shape, jnp.bfloat16),
        input_output_aliases={len(args) - 1: 0} if aliased else {},
        compiler_params=pltpu.CompilerParams(vmem_limit_bytes=VMEM),
        cost_estimate=pl.CostEstimate(
            flops=2 * slots * rows * width * len(right),
            bytes_accessed=2 * (slots + rows) * width * len(right) + 2 * slots * rows,
            transcendentals=0,
        ),
        name="gram",
    )(*args)


def shards(expression, cell_type, size_factor, gene_mean):
    types = lax.axis_size("cells")
    blocks = lax.axis_size("blk")
    shard_rows, panel = expression.shape
    cap = 2 * shard_rows // types
    width = 256
    widths = [width] * (panel // width)
    chunks = len(widths)
    home = lax.axis_index("cells").astype(jnp.int32)
    me = lax.axis_index("blk").astype(jnp.int32)
    cores = 2
    chips = blocks // cores

    packed = pack(types, cap, widths, home[None], cell_type, size_factor, expression)

    def shift(block, by):
        return lax.ppermute(block, "cells", [(s, (s + by) % types) for s in range(types)])

    def across(panel_, by):
        return lax.ppermute(panel_, "blk", [(b, (b + by * cores) % blocks) for b in range(blocks)])

    def sibling(panel_):
        return lax.ppermute(panel_, "blk", [(b, b ^ 1) for b in range(blocks)])

    arrived = [
        [packed[k][0]] + [shift(packed[k][j], j) for j in range(1, types)] for k in range(chunks)
    ]
    mean = gene_mean.reshape(1, panel)
    left, panels, count = [], [], None
    for k in range(chunks):
        own, turned, count = standardize(
            types, cap, width, mean[:, k * width : (k + 1) * width], arrived[k], arrived[0]
        )
        left.append(turned)
        near = [own] + [across(own, d) for d in range(1, chips)]
        panels.append(near + [sibling(p) for p in near])

    out = None
    shape = (1, panel, panel * blocks)
    for k in range(chunks):
        sources = [(me + blocks - d * cores) % blocks for d in range(chips)]
        sources += [s ^ 1 for s in sources]
        places = jnp.stack(sources) * chunks + k
        out = gram(shape, places.astype(jnp.int32), count, left, panels[k], out)
    return out


def solution(mesh):
    placed = (
        P(("parts", "cells"), "blk"),
        P(("parts", "cells")),
        P(("parts", "cells")),
        P(("parts", "blk")),
    )
    return jax.shard_map(
        shards,
        mesh=mesh,
        in_specs=placed,
        out_specs=P(("parts", "cells"), "blk", None),
        check_vma=False,
    )
```

```python
import functools

import jax
import jax.numpy as jnp
from jax import lax
from jax.experimental import pallas as pl
from jax.experimental.pallas import tpu as pltpu
from jax.sharding import PartitionSpec as P

dispersion = 100.0
epsilon = 1e-05
TILE = 16
VMEM = 24 * 1024 * 1024

brief = pl.CostEstimate(flops=1024, bytes_accessed=1024, transcendentals=0)
whole = pl.BlockSpec(memory_space=pltpu.VMEM)


def pack_kernel(types, cap, widths, home_ref, type_ref, factor_ref, expr_ref, *outs):
    rows = expr_ref.shape[0]
    home = home_ref[0]
    kind = type_ref[...]
    rel = jnp.bitwise_xor(kind, home)
    lines = max(types, 8)
    hot = lax.broadcasted_iota(jnp.int32, (lines, rows), 0) == rel
    hot_f = jnp.where(hot, 1.0, 0.0)
    upper = jnp.where(
        lax.broadcasted_iota(jnp.int32, (rows, rows), 0)
        <= lax.broadcasted_iota(jnp.int32, (rows, rows), 1),
        1.0,
        0.0,
    ).astype(jnp.bfloat16)
    running = jnp.dot(hot_f.astype(jnp.bfloat16), upper, preferred_element_type=jnp.float32)
    rank = jnp.sum(hot_f * running, axis=0, keepdims=True) - 1.0
    slot = rel * cap + rank.astype(jnp.int32)
    factor = jnp.broadcast_to(factor_ref[...].astype(jnp.float32), (TILE, rows)).astype(
        jnp.bfloat16
    )
    values = expr_ref[...]
    for j in range(types):
        place = jnp.where(
            lax.broadcasted_iota(jnp.int32, (cap, rows), 0) + j * cap == slot, 1.0, 0.0
        ).astype(jnp.bfloat16)
        block = jnp.dot(place, values, preferred_element_type=jnp.float32).astype(jnp.bfloat16)
        start = 0
        for k, width in enumerate(widths):
            outs[k * types + j][0:cap, :] = block[:, start : start + width]
            start += width
        line = lax.dot_general(
            factor, place, (((1,), (1,)), ((), ())), preferred_element_type=jnp.float32
        )
        row = lax.broadcasted_iota(jnp.int32, (TILE, 1), 0)
        width = widths[0]
        tail = jnp.zeros((TILE, min(width, cap)), jnp.float32)
        for i in range(pl.cdiv(cap, width)):
            tail = jnp.where(row == i, line[:, i * width : min((i + 1) * width, cap)], tail)
        outs[j][cap : cap + TILE, 0 : min(width, cap)] = tail.astype(jnp.bfloat16)


def pack(types, cap, widths, home, cell_type, size_factor, expression):
    rows = expression.shape[0]
    shapes = [
        jax.ShapeDtypeStruct((cap + (TILE if k == 0 else 0), width), jnp.bfloat16)
        for k, width in enumerate(widths)
        for _ in range(types)
    ]
    flat = pl.pallas_call(
        functools.partial(pack_kernel, types, cap, widths),
        out_shape=shapes,
        in_specs=[pl.BlockSpec(memory_space=pltpu.SMEM), whole, whole, whole],
        out_specs=[whole] * len(shapes),
        compiler_params=pltpu.CompilerParams(vmem_limit_bytes=VMEM),
        cost_estimate=brief,
        name="pack",
    )(home, cell_type.reshape(1, rows), size_factor.reshape(1, rows), expression)
    return [flat[k * types : (k + 1) * types] for k in range(len(widths))]


def standardize_kernel(types, cap, lead, separate, mean_ref, *refs):
    blocks = refs[:types]
    tails = refs[types : 2 * types] if separate else blocks
    base = 0 if separate else cap
    refs = refs[2 * types :] if separate else refs[types:]
    scaled_ref, turned_ref, count_ref, work = refs
    mean = mean_ref[...]
    width = mean.shape[1]
    piece = min(lead, cap)
    total = jnp.zeros((1, width), jnp.float32)
    count = jnp.zeros((1, 1), jnp.float32)
    alive = []
    for j in range(types):
        column = jnp.zeros((cap, 1), jnp.float32)
        for i in range(pl.cdiv(cap, lead)):
            line = tails[j][base : base + TILE, 0:piece].astype(jnp.float32)[i : i + 1, :]
            diagonal = (
                lax.broadcasted_iota(jnp.int32, (cap, piece), 0)
                == lax.broadcasted_iota(jnp.int32, (cap, piece), 1) + i * lead
            )
            column += jnp.sum(jnp.where(diagonal, line, 0.0), axis=1, keepdims=True)
        live = column > 0.0
        alive.append(live)
        count += jnp.sum(jnp.where(live, 1.0, 0.0), axis=0, keepdims=True)
        expected = jnp.where(live, column * mean, 1.0)
        values = blocks[j][0:cap, :].astype(jnp.float32)
        residual = jnp.where(
            live,
            (values - expected) * lax.rsqrt(expected + expected * expected * (1.0 / dispersion)),
            0.0,
        )
        work[j * cap : (j + 1) * cap, :] = residual
        total += jnp.sum(residual, axis=0, keepdims=True)
    center = total / count
    square = jnp.zeros((1, width), jnp.float32)
    for j in range(types):
        centered = jnp.where(alive[j], work[j * cap : (j + 1) * cap, :] - center, 0.0)
        work[j * cap : (j + 1) * cap, :] = centered
        square += jnp.sum(centered * centered, axis=0, keepdims=True)
    scale = lax.rsqrt(square / count + epsilon)
    for j in range(types):
        scaled = work[j * cap : (j + 1) * cap, :] * scale
        scaled_ref[j * cap : (j + 1) * cap, :] = scaled.astype(jnp.bfloat16)
        work[j * cap : (j + 1) * cap, :] = scaled
    turned_ref[...] = jnp.transpose(work[...]).astype(jnp.bfloat16)
    count_ref[...] = jnp.broadcast_to(count, count_ref.shape)


def standardize(types, cap, lead, mean, blocks, first):
    width = mean.shape[1]
    separate = first is not blocks
    slots = types * cap
    specs = [whole] * (1 + types)
    args = [mean, *blocks]
    if separate:
        specs += [pl.BlockSpec((TILE, lead), lambda i: (cap // TILE, 0))] * types
        args += list(first)
    return pl.pallas_call(
        functools.partial(standardize_kernel, types, cap, lead, separate),
        grid=(1,),
        out_shape=[
            jax.ShapeDtypeStruct((slots, width), jnp.bfloat16),
            jax.ShapeDtypeStruct((width, slots), jnp.bfloat16),
            jax.ShapeDtypeStruct((8, 128), jnp.float32),
        ],
        in_specs=specs,
        out_specs=[whole] * 3,
        scratch_shapes=[pltpu.VMEM((slots, width), jnp.float32)],
        compiler_params=pltpu.CompilerParams(vmem_limit_bytes=VMEM),
        cost_estimate=brief,
        name="standardize",
    )(*args)


def gram_kernel(parts, panels, aliased, place_ref, count_ref, *refs):
    pieces = refs[:parts]
    right = refs[parts : parts + panels]
    out_ref, left = refs[parts + panels + (1 if aliased else 0) :]
    inverse = 1.0 / count_ref[0:1, 0:1]
    step = pl.program_id(0)

    @pl.when(step == 0)
    def _():
        start = 0
        for piece in pieces:
            left[start : start + piece.shape[0], :] = piece[...]
            start += piece.shape[0]

    for j in range(panels):

        @pl.when(step == j)
        def _(j=j):
            product = jnp.dot(left[...], right[j][...], preferred_element_type=jnp.float32)
            out_ref[0] = (product * inverse).astype(jnp.bfloat16)


def gram(shape, places, count, left, right, before):
    rows = shape[1]
    slots, width = right[0].shape
    aliased = before is not None
    args = [places, count, *left, *right] + ([before] if aliased else [])
    specs = [whole] * (1 + len(left) + len(right))
    specs += [pl.BlockSpec(memory_space=pl.ANY)] if aliased else []
    return pl.pallas_call(
        functools.partial(gram_kernel, len(left), len(right), aliased),
        grid_spec=pltpu.PrefetchScalarGridSpec(
            num_scalar_prefetch=1,
            grid=(len(right),),
            in_specs=specs,
            out_specs=pl.BlockSpec((1, rows, width), lambda i, place: (0, 0, place[i])),
            scratch_shapes=[pltpu.VMEM((rows, slots), jnp.bfloat16)],
        ),
        out_shape=jax.ShapeDtypeStruct(shape, jnp.bfloat16),
        input_output_aliases={len(args) - 1: 0} if aliased else {},
        compiler_params=pltpu.CompilerParams(vmem_limit_bytes=VMEM),
        cost_estimate=brief,
        name="gram",
    )(*args)


def after(value, *others):
    return lax.optimization_barrier((value, *others))[0]


def shards(expression, cell_type, size_factor, gene_mean):
    types = lax.axis_size("cells")
    blocks = lax.axis_size("blk")
    shard_rows, panel = expression.shape
    cap = 2 * shard_rows // types
    assert types & (types - 1) == 0
    width = 256
    widths = [width] * (panel // width)
    chunks = len(widths)
    home = lax.axis_index("cells").astype(jnp.int32)
    me = lax.axis_index("blk").astype(jnp.int32)
    cores = 2
    chips = blocks // cores
    window = 3

    packed = pack(types, cap, widths, home[None], cell_type, size_factor, expression)

    def swap(block, by):
        return lax.ppermute(block, "cells", [(s, s ^ by) for s in range(types)])

    def across(panel_, by):
        return lax.ppermute(panel_, "blk", [(b, (b + by * cores) % blocks) for b in range(blocks)])

    def sibling(panel_):
        return lax.ppermute(panel_, "blk", [(b, b ^ 1) for b in range(blocks)])

    mean = gene_mean.reshape(1, panel)
    order = sorted(range(1, types), key=lambda j: (j == types - 1, -j))
    flights, first = [], None
    left, own, near, far, far_near = [], [], [], [], []
    for k in range(chunks):
        arrived = [packed[k][0]] + [None] * (types - 1)
        for j in order:
            waits = flights[-window:][:1] if len(flights) >= window else []
            if j == order[-1] and k >= 2:
                waits = waits + far[k - 2]
            arrived[j] = swap(after(packed[k][j], *waits) if waits else packed[k][j], j)
            flights.append(arrived[j])
        if k >= 2:
            far_near.append([sibling(got) for got in far[k - 2]])
        done = near[-1:] + (far_near[-1] if k >= 2 else [])
        if done:
            arrived[0] = after(arrived[0], *done)
        first = first or arrived
        scaled, turned, count = standardize(
            types, cap, width, mean[:, k * width : (k + 1) * width], arrived, first
        )
        left.append(turned)
        own.append(scaled)
        far.append([across(scaled, d) for d in range(1, chips)])
        near.append(sibling(scaled))

    column = lambda source, k: source * chunks + k
    distant = [(me + blocks - d * cores) % blocks for d in range(1, chips)]
    shape = (1, panel, panel * blocks)

    def far_panels(k):
        panels, places = [], []
        for source, got, other in zip(distant, far[k], far_near[k]):
            panels += [got, other]
            places += [column(source, k), column(source ^ 1, k)]
        return panels, places

    panels, places = [], []
    for k in range(chunks):
        panels += [own[k], near[k]]
        places += [column(me, k), column(me ^ 1, k)]
    for k in range(chunks - 2):
        more, at = far_panels(k)
        panels += more
        places += at
    late = max(chunks - 2, 0)
    panels[0] = after(panels[0], *far[late])
    far_near.append([sibling(got) for got in far[late]])
    out = gram(shape, jnp.stack(places).astype(jnp.int32), count, left, panels, None)
    for k in range(late, chunks):
        if k > late:
            far_near.append([sibling(after(got, out)) for got in far[k]])
        panels, places = far_panels(k)
        out = gram(shape, jnp.stack(places).astype(jnp.int32), count, left, panels, out)
    return out


def solution(mesh):
    placed = (
        P(("parts", "cells"), "blk"),
        P(("parts", "cells")),
        P(("parts", "cells")),
        P(("parts", "blk")),
    )
    return jax.shard_map(
        shards,
        mesh=mesh,
        in_specs=placed,
        out_specs=P(("parts", "cells"), "blk", None),
        check_vma=False,
    )
```

```python
import functools

import jax
import jax.numpy as jnp
from jax import lax
from jax.experimental import pallas as pl
from jax.experimental.pallas import tpu as pltpu
from jax.sharding import PartitionSpec as P

dispersion = 100.0
epsilon = 1e-05
TILE = 16
VMEM = 16 * 1024 * 1024

brief = pl.CostEstimate(flops=1024, bytes_accessed=1024, transcendentals=0)
lengthy = pl.CostEstimate(flops=2 * 10**10, bytes_accessed=1024, transcendentals=0)
whole = pl.BlockSpec(memory_space=pltpu.VMEM)
anywhere = pl.BlockSpec(memory_space=pl.ANY)


def pack_kernel(types, cap, widths, home_ref, type_ref, factor_ref, expr_ref, *outs):
    rows = expr_ref.shape[0]
    home = home_ref[0]
    kind = type_ref[...]
    rel = jnp.bitwise_xor(kind, home)
    lines = max(types, 8)
    hot = lax.broadcasted_iota(jnp.int32, (lines, rows), 0) == rel
    hot_f = jnp.where(hot, 1.0, 0.0)
    upper = jnp.where(
        lax.broadcasted_iota(jnp.int32, (rows, rows), 0)
        <= lax.broadcasted_iota(jnp.int32, (rows, rows), 1),
        1.0,
        0.0,
    ).astype(jnp.bfloat16)
    running = jnp.dot(hot_f.astype(jnp.bfloat16), upper, preferred_element_type=jnp.float32)
    rank = jnp.sum(hot_f * running, axis=0, keepdims=True) - 1.0
    slot = rel * cap + rank.astype(jnp.int32)
    factor = jnp.broadcast_to(factor_ref[...].astype(jnp.float32), (TILE, rows)).astype(
        jnp.bfloat16
    )
    values = expr_ref[...]
    for j in range(types):
        place = jnp.where(
            lax.broadcasted_iota(jnp.int32, (cap, rows), 0) + j * cap == slot, 1.0, 0.0
        ).astype(jnp.bfloat16)
        block = jnp.dot(place, values, preferred_element_type=jnp.float32).astype(jnp.bfloat16)
        start = 0
        for k, width in enumerate(widths):
            outs[k * types + j][0:cap, :] = block[:, start : start + width]
            start += width
        line = lax.dot_general(
            factor, place, (((1,), (1,)), ((), ())), preferred_element_type=jnp.float32
        )
        row = lax.broadcasted_iota(jnp.int32, (TILE, 1), 0)
        width = widths[0]
        tail = jnp.zeros((TILE, min(width, cap)), jnp.float32)
        for i in range(pl.cdiv(cap, width)):
            tail = jnp.where(row == i, line[:, i * width : min((i + 1) * width, cap)], tail)
        outs[j][cap : cap + TILE, 0 : min(width, cap)] = tail.astype(jnp.bfloat16)


def pack(types, cap, widths, home, cell_type, size_factor, expression):
    rows = expression.shape[0]
    shapes = [
        jax.ShapeDtypeStruct((cap + (TILE if k == 0 else 0), width), jnp.bfloat16)
        for k, width in enumerate(widths)
        for _ in range(types)
    ]
    flat = pl.pallas_call(
        functools.partial(pack_kernel, types, cap, widths),
        out_shape=shapes,
        in_specs=[pl.BlockSpec(memory_space=pltpu.SMEM), whole, whole, whole],
        out_specs=[whole] * len(shapes),
        compiler_params=pltpu.CompilerParams(vmem_limit_bytes=VMEM),
        cost_estimate=brief,
        name="pack",
    )(home, cell_type.reshape(1, rows), size_factor.reshape(1, rows), expression)
    return [flat[k * types : (k + 1) * types] for k in range(len(widths))]


def standardize_kernel(types, cap, lead, separate, chunk, mean_ref, *refs):
    blocks = refs[:types]
    tails = refs[types : 2 * types] if separate else blocks
    base = 0 if separate else cap
    refs = refs[2 * types :] if separate else refs[types:]
    scaled_ref, all_ref, turned_ref, count_ref, work, turned, sems = refs[-7:]
    mean = mean_ref[...]
    width = mean.shape[1]
    piece = min(lead, cap)
    total = jnp.zeros((1, width), jnp.float32)
    count = jnp.zeros((1, 1), jnp.float32)
    alive = []
    for j in range(types):
        column = jnp.zeros((cap, 1), jnp.float32)
        for i in range(pl.cdiv(cap, lead)):
            line = tails[j][base : base + TILE, 0:piece].astype(jnp.float32)[i : i + 1, :]
            diagonal = (
                lax.broadcasted_iota(jnp.int32, (cap, piece), 0)
                == lax.broadcasted_iota(jnp.int32, (cap, piece), 1) + i * lead
            )
            column += jnp.sum(jnp.where(diagonal, line, 0.0), axis=1, keepdims=True)
        live = column > 0.0
        alive.append(live)
        count += jnp.sum(jnp.where(live, 1.0, 0.0), axis=0, keepdims=True)
        expected = jnp.where(live, column * mean, 1.0)
        values = blocks[j][0:cap, :].astype(jnp.float32)
        residual = jnp.where(
            live,
            (values - expected) * lax.rsqrt(expected + expected * expected * (1.0 / dispersion)),
            0.0,
        )
        work[j * cap : (j + 1) * cap, :] = residual
        total += jnp.sum(residual, axis=0, keepdims=True)
    center = total / count
    square = jnp.zeros((1, width), jnp.float32)
    for j in range(types):
        centered = jnp.where(alive[j], work[j * cap : (j + 1) * cap, :] - center, 0.0)
        work[j * cap : (j + 1) * cap, :] = centered
        square += jnp.sum(centered * centered, axis=0, keepdims=True)
    scale = lax.rsqrt(square / count + epsilon)
    for j in range(types):
        scaled = work[j * cap : (j + 1) * cap, :] * scale
        scaled_ref[j * cap : (j + 1) * cap, :] = scaled.astype(jnp.bfloat16)
        work[j * cap : (j + 1) * cap, :] = scaled
    slots = types * cap
    rows = pl.ds(chunk * slots, slots)
    scaled_copy = pltpu.make_async_copy(scaled_ref, all_ref.at[rows, :], sems.at[0])
    scaled_copy.start()
    turned[...] = jnp.transpose(work[...]).astype(jnp.bfloat16)
    rows = pl.ds(chunk * width, width)
    turned_copy = pltpu.make_async_copy(turned, turned_ref.at[rows, :], sems.at[1])
    turned_copy.start()
    scaled_copy.wait()
    turned_copy.wait()
    count_ref[...] = jnp.broadcast_to(count, count_ref.shape)


def standardize(types, cap, lead, mean, chunk, chunks, blocks, first, before):
    width = mean.shape[1]
    separate = first is not blocks
    slots = types * cap
    specs = [whole] * (1 + types)
    args = [mean, *blocks]
    if separate:
        specs += [pl.BlockSpec((TILE, lead), lambda i: (cap // TILE, 0))] * types
        args += list(first)
    aliases = {}
    if before is not None:
        aliases = {len(args): 1, len(args) + 1: 2}
        specs += [anywhere] * 2
        args += list(before)
    return pl.pallas_call(
        functools.partial(standardize_kernel, types, cap, lead, separate, chunk),
        grid=(1,),
        out_shape=[
            jax.ShapeDtypeStruct((slots, width), jnp.bfloat16),
            jax.ShapeDtypeStruct((chunks * slots, width), jnp.bfloat16),
            jax.ShapeDtypeStruct((chunks * width, slots), jnp.bfloat16),
            jax.ShapeDtypeStruct((8, 128), jnp.float32),
        ],
        in_specs=specs,
        out_specs=[whole, anywhere, anywhere, whole],
        scratch_shapes=[
            pltpu.VMEM((slots, width), jnp.float32),
            pltpu.VMEM((width, slots), jnp.bfloat16),
            pltpu.SemaphoreType.DMA((2,)),
        ],
        input_output_aliases=aliases,
        compiler_params=pltpu.CompilerParams(vmem_limit_bytes=VMEM),
        cost_estimate=lengthy,
        name="standardize",
    )(*args)


def gram_kernel(spots, arrays, place_ref, count_ref, left_ref, *refs):
    sources = refs[:arrays]
    out_ref, left, panel, tile, left_sem, panel_sem, tile_sem = refs[-7:]
    slots, width = panel.shape[1:]
    panels = len(spots)
    inverse = 1.0 / count_ref[0:1, 0:1]

    def fetch(j):
        source, row = spots[j]
        block = sources[source].at[pl.ds(row, slots), :]
        return pltpu.make_async_copy(block, panel.at[j % 2], panel_sem.at[j % 2])

    def store(j):
        column = pl.multiple_of(place_ref[j] * width, width)
        return pltpu.make_async_copy(
            tile.at[j % 2], out_ref.at[0, :, pl.ds(column, width)], tile_sem.at[j % 2]
        )

    fetch(0).start()
    left_copy = pltpu.make_async_copy(left_ref, left, left_sem)
    left_copy.start()
    left_copy.wait()
    for j in range(panels):
        if j + 1 < panels:
            fetch(j + 1).start()
        fetch(j).wait()
        if j >= 2:
            store(j - 2).wait()
        product = jnp.dot(left[...], panel[j % 2], preferred_element_type=jnp.float32)
        tile[j % 2] = (product * inverse).astype(jnp.bfloat16)
        store(j).start()
    for j in range(max(panels - 2, 0), panels):
        store(j).wait()


def gram(shape, places, count, left, right, before, cost):
    rows, slots = left.shape
    width = right[0].shape[1]
    spots = [
        (i, row) for i, panels in enumerate(right) for row in range(0, panels.shape[0], slots)
    ]
    args = [jnp.stack(places).astype(jnp.int32), count, left, *right]
    args += [] if before is None else [before]
    specs = [pl.BlockSpec(memory_space=pltpu.SMEM), whole] + [anywhere] * (len(args) - 2)
    return pl.pallas_call(
        functools.partial(gram_kernel, spots, len(right)),
        in_specs=specs,
        out_specs=anywhere,
        out_shape=jax.ShapeDtypeStruct(shape, jnp.bfloat16),
        scratch_shapes=[
            pltpu.VMEM((rows, slots), jnp.bfloat16),
            pltpu.VMEM((2, slots, width), jnp.bfloat16),
            pltpu.VMEM((2, rows, width), jnp.bfloat16),
            pltpu.SemaphoreType.DMA,
            pltpu.SemaphoreType.DMA((2,)),
            pltpu.SemaphoreType.DMA((2,)),
        ],
        input_output_aliases={} if before is None else {len(args) - 1: 0},
        compiler_params=pltpu.CompilerParams(vmem_limit_bytes=VMEM),
        cost_estimate=cost,
        name="gram",
    )(*args)


def after(value, *others):
    return lax.optimization_barrier((value, *others))[0]


def shards(expression, cell_type, size_factor, gene_mean):
    types = lax.axis_size("cells")
    blocks = lax.axis_size("blk")
    shard_rows, panel = expression.shape
    cap = 2 * shard_rows // types
    assert types & (types - 1) == 0
    width = 256
    widths = [width] * (panel // width)
    chunks = len(widths)
    home = lax.axis_index("cells").astype(jnp.int32)
    me = lax.axis_index("blk").astype(jnp.int32)
    cores = 2
    chips = blocks // cores
    window = 3

    packed = pack(types, cap, widths, home[None], cell_type, size_factor, expression)

    def swap(block, by):
        return lax.ppermute(block, "cells", [(s, s ^ by) for s in range(types)])

    def across(panel_, by):
        return lax.ppermute(panel_, "blk", [(b, (b + by * cores) % blocks) for b in range(blocks)])

    def side(name, panel_, *waits):
        with jax.named_scope(name):
            return lax.ppermute(after(panel_, *waits), "blk", [(b, b ^ 1) for b in range(blocks)])

    mean = gene_mean.reshape(1, panel)
    order = sorted(range(1, types), key=lambda j: (j == 1, j))
    left, own, far, before = None, None, [], None
    first = None
    for k in range(chunks):
        arrived = [packed[k][0]] + [None] * (types - 1)
        for j in order:
            block = packed[k][j]
            if k:
                block = after(block, before[j])
            with jax.named_scope(f"cells_{j}_chunk_{k}"):
                arrived[j] = swap(block, j)
        before = list(arrived)
        waits = far[k - 2] if k >= 2 else []
        if waits:
            arrived[0] = after(arrived[0], *waits)
        first = first or arrived
        piece = mean[:, k * width : (k + 1) * width]
        scaled, own, left, count = standardize(
            types, cap, width, piece, k, chunks, arrived, first, (own, left) if k else None
        )
        with jax.named_scope(f"far_{k}"):
            far.append([across(scaled, d) for d in range(1, chips)])

    column = lambda source, k: source * chunks + k
    distant = [(me + blocks - d * cores) % blocks for d in range(1, chips)]
    shape = (1, panel, panel * blocks)

    last = chunks - 1
    there = sum(far[:last], [])
    near = side("near", own)
    far_near = [side(f"far_near_{i}", p, own, *there) for i, p in enumerate(there)]
    places = [column(me, k) for k in range(chunks)]
    out = gram(shape, places, count, left, [own], None, lengthy)
    places = [column(me ^ 1, k) for k in range(chunks)]
    places += [column(source, k) for k in range(last) for source in distant]
    places += [column(source ^ 1, k) for k in range(last) for source in distant]
    out = gram(shape, places, count, left, [near, *there, *far_near], out, brief)
    far_near = [side(f"far_near_last_{i}", p, out) for i, p in enumerate(far[last])]
    places = [column(source, last) for source in distant]
    places += [column(source ^ 1, last) for source in distant]
    return gram(shape, places, count, left, [*far[last], *far_near], out, brief)


def solution(mesh):
    placed = (
        P(("parts", "cells"), "blk"),
        P(("parts", "cells")),
        P(("parts", "cells")),
        P(("parts", "blk")),
    )
    return jax.shard_map(
        shards,
        mesh=mesh,
        in_specs=placed,
        out_specs=P(("parts", "cells"), "blk", None),
        check_vma=False,
    )
```

```python
import functools

import jax
import jax.numpy as jnp
from jax import lax
from jax.experimental import pallas as pl
from jax.experimental.pallas import tpu as pltpu
from jax.sharding import PartitionSpec as P

dispersion = 100.0
epsilon = 1e-05
TILE = 16
VMEM = 16 * 1024 * 1024

brief = pl.CostEstimate(flops=1024, bytes_accessed=1024, transcendentals=0)
lengthy = pl.CostEstimate(flops=2 * 10**10, bytes_accessed=1024, transcendentals=0)
whole = pl.BlockSpec(memory_space=pltpu.VMEM)
anywhere = pl.BlockSpec(memory_space=pl.ANY)


def pack_kernel(types, cap, widths, home_ref, type_ref, factor_ref, expr_ref, *outs):
    rows = expr_ref.shape[0]
    home = home_ref[0]
    kind = type_ref[...]
    rel = jnp.bitwise_xor(kind, home)
    lines = max(types, 8)
    hot = lax.broadcasted_iota(jnp.int32, (lines, rows), 0) == rel
    hot_f = jnp.where(hot, 1.0, 0.0)
    upper = jnp.where(
        lax.broadcasted_iota(jnp.int32, (rows, rows), 0)
        <= lax.broadcasted_iota(jnp.int32, (rows, rows), 1),
        1.0,
        0.0,
    ).astype(jnp.bfloat16)
    running = jnp.dot(hot_f.astype(jnp.bfloat16), upper, preferred_element_type=jnp.float32)
    rank = jnp.sum(hot_f * running, axis=0, keepdims=True) - 1.0
    slot = rel * cap + rank.astype(jnp.int32)
    factor = jnp.broadcast_to(factor_ref[...].astype(jnp.float32), (TILE, rows)).astype(
        jnp.bfloat16
    )
    values = expr_ref[...]
    for j in range(types):
        place = jnp.where(
            lax.broadcasted_iota(jnp.int32, (cap, rows), 0) + j * cap == slot, 1.0, 0.0
        ).astype(jnp.bfloat16)
        block = jnp.dot(place, values, preferred_element_type=jnp.float32).astype(jnp.bfloat16)
        start = 0
        for k, width in enumerate(widths):
            outs[k * types + j][0:cap, :] = block[:, start : start + width]
            start += width
        line = lax.dot_general(
            factor, place, (((1,), (1,)), ((), ())), preferred_element_type=jnp.float32
        )
        row = lax.broadcasted_iota(jnp.int32, (TILE, 1), 0)
        width = widths[0]
        tail = jnp.zeros((TILE, min(width, cap)), jnp.float32)
        for i in range(pl.cdiv(cap, width)):
            tail = jnp.where(row == i, line[:, i * width : min((i + 1) * width, cap)], tail)
        outs[j][cap : cap + TILE, 0 : min(width, cap)] = tail.astype(jnp.bfloat16)


def pack(types, cap, widths, home, cell_type, size_factor, expression):
    rows = expression.shape[0]
    shapes = [
        jax.ShapeDtypeStruct((cap + (TILE if k == 0 else 0), width), jnp.bfloat16)
        for k, width in enumerate(widths)
        for _ in range(types)
    ]
    flat = pl.pallas_call(
        functools.partial(pack_kernel, types, cap, widths),
        out_shape=shapes,
        in_specs=[pl.BlockSpec(memory_space=pltpu.SMEM), whole, whole, whole],
        out_specs=[whole] * len(shapes),
        compiler_params=pltpu.CompilerParams(vmem_limit_bytes=VMEM),
        cost_estimate=brief,
        name="pack",
    )(home, cell_type.reshape(1, rows), size_factor.reshape(1, rows), expression)
    return [flat[k * types : (k + 1) * types] for k in range(len(widths))]


def standardize_kernel(types, cap, lead, separate, chunk, mean_ref, *refs):
    blocks = refs[:types]
    tails = refs[types : 2 * types] if separate else blocks
    base = 0 if separate else cap
    refs = refs[2 * types :] if separate else refs[types:]
    scaled_ref, all_ref, turned_ref, count_ref, work, turned, sems = refs[-7:]
    mean = mean_ref[...]
    width = mean.shape[1]
    piece = min(lead, cap)
    total = jnp.zeros((1, width), jnp.float32)
    count = jnp.zeros((1, 1), jnp.float32)
    alive = []
    for j in range(types):
        column = jnp.zeros((cap, 1), jnp.float32)
        for i in range(pl.cdiv(cap, lead)):
            line = tails[j][base : base + TILE, 0:piece].astype(jnp.float32)[i : i + 1, :]
            diagonal = (
                lax.broadcasted_iota(jnp.int32, (cap, piece), 0)
                == lax.broadcasted_iota(jnp.int32, (cap, piece), 1) + i * lead
            )
            column += jnp.sum(jnp.where(diagonal, line, 0.0), axis=1, keepdims=True)
        live = column > 0.0
        alive.append(live)
        count += jnp.sum(jnp.where(live, 1.0, 0.0), axis=0, keepdims=True)
        expected = jnp.where(live, column * mean, 1.0)
        values = blocks[j][0:cap, :].astype(jnp.float32)
        residual = jnp.where(
            live,
            (values - expected) * lax.rsqrt(expected + expected * expected * (1.0 / dispersion)),
            0.0,
        )
        work[j * cap : (j + 1) * cap, :] = residual
        total += jnp.sum(residual, axis=0, keepdims=True)
    center = total / count
    square = jnp.zeros((1, width), jnp.float32)
    for j in range(types):
        centered = jnp.where(alive[j], work[j * cap : (j + 1) * cap, :] - center, 0.0)
        work[j * cap : (j + 1) * cap, :] = centered
        square += jnp.sum(centered * centered, axis=0, keepdims=True)
    scale = lax.rsqrt(square / count + epsilon)
    for j in range(types):
        scaled = work[j * cap : (j + 1) * cap, :] * scale
        scaled_ref[j * cap : (j + 1) * cap, :] = scaled.astype(jnp.bfloat16)
        work[j * cap : (j + 1) * cap, :] = scaled
    slots = types * cap
    rows = pl.ds(chunk * slots, slots)
    scaled_copy = pltpu.make_async_copy(scaled_ref, all_ref.at[rows, :], sems.at[0])
    scaled_copy.start()
    turned[...] = jnp.transpose(work[...]).astype(jnp.bfloat16)
    rows = pl.ds(chunk * width, width)
    turned_copy = pltpu.make_async_copy(turned, turned_ref.at[rows, :], sems.at[1])
    turned_copy.start()
    scaled_copy.wait()
    turned_copy.wait()
    count_ref[...] = jnp.broadcast_to(count, count_ref.shape)


def standardize(types, cap, lead, mean, chunk, chunks, blocks, first, before):
    width = mean.shape[1]
    separate = first is not blocks
    slots = types * cap
    specs = [whole] * (1 + types)
    args = [mean, *blocks]
    if separate:
        specs += [pl.BlockSpec((TILE, lead), lambda i: (cap // TILE, 0))] * types
        args += list(first)
    aliases = {}
    if before is not None:
        aliases = {len(args): 1, len(args) + 1: 2}
        specs += [anywhere] * 2
        args += list(before)
    return pl.pallas_call(
        functools.partial(standardize_kernel, types, cap, lead, separate, chunk),
        grid=(1,),
        out_shape=[
            jax.ShapeDtypeStruct((slots, width), jnp.bfloat16),
            jax.ShapeDtypeStruct((chunks * slots, width), jnp.bfloat16),
            jax.ShapeDtypeStruct((chunks * width, slots), jnp.bfloat16),
            jax.ShapeDtypeStruct((8, 128), jnp.float32),
        ],
        in_specs=specs,
        out_specs=[whole, anywhere, anywhere, whole],
        scratch_shapes=[
            pltpu.VMEM((slots, width), jnp.float32),
            pltpu.VMEM((width, slots), jnp.bfloat16),
            pltpu.SemaphoreType.DMA((2,)),
        ],
        input_output_aliases=aliases,
        compiler_params=pltpu.CompilerParams(vmem_limit_bytes=VMEM),
        cost_estimate=lengthy,
        name="standardize",
    )(*args)


def gram_kernel(groups, arrays, strip, place_ref, count_ref, left_ref, *refs):
    sources = refs[:arrays]
    out_ref, panel, tile, panel_sem, tile_sem = refs[-5:]
    rows, slots = left_ref.shape
    inverse = 1.0 / count_ref[0:1, 0:1]

    def fetch(g):
        copies, column = [], 0
        for source, row, width in groups[g]:
            copies.append(
                pltpu.make_async_copy(
                    sources[source].at[pl.ds(row, slots), :],
                    panel.at[g % 2, :, pl.ds(column, width)],
                    panel_sem.at[g % 2, len(copies)],
                )
            )
            column += width
        return copies, column

    for copy in fetch(0)[0]:
        copy.start()
    stores = []
    for g in range(len(groups)):
        if g + 1 < len(groups):
            for copy in fetch(g + 1)[0]:
                copy.start()
        copies, columns = fetch(g)
        for copy in copies:
            copy.wait()
        place = pl.multiple_of(place_ref[g] * 128, 128)
        for row in range(0, rows, strip):
            slot = len(stores) % 2
            if len(stores) >= 2:
                stores[-2].wait()
            product = jnp.dot(
                left_ref[row : row + strip, :],
                panel[g % 2, :, 0:columns],
                preferred_element_type=jnp.float32,
            )
            tile[slot, :, 0:columns] = (product * inverse).astype(jnp.bfloat16)
            stores.append(
                pltpu.make_async_copy(
                    tile.at[slot, :, pl.ds(0, columns)],
                    out_ref.at[0, pl.ds(row, strip), pl.ds(place, columns)],
                    tile_sem.at[slot],
                )
            )
            stores[-1].start()
    for store in stores[-2:]:
        store.wait()


def gram(shape, count, left, groups, before, cost):
    rows, slots = left.shape
    strip = min(rows, 256)
    places = jnp.stack([place for place, _ in groups]) // 128
    arrays, layout = [], []
    for _, panels in groups:
        layout.append([])
        for array, index in panels:
            if not any(array is other for other in arrays):
                arrays.append(array)
            source = [array is other for other in arrays].index(True)
            layout[-1].append((source, index * slots, array.shape[1]))
    most = max(len(panels) for panels in layout)
    widest = max(sum(width for _, _, width in panels) for panels in layout)
    args = [places.astype(jnp.int32), count, left, *arrays]
    args += [] if before is None else [before]
    specs = [pl.BlockSpec(memory_space=pltpu.SMEM), whole, whole] + [anywhere] * (len(args) - 3)
    return pl.pallas_call(
        functools.partial(gram_kernel, layout, len(arrays), strip),
        in_specs=specs,
        out_specs=anywhere,
        out_shape=jax.ShapeDtypeStruct(shape, jnp.bfloat16),
        scratch_shapes=[
            pltpu.VMEM((2, slots, widest), jnp.bfloat16),
            pltpu.VMEM((2, strip, widest), jnp.bfloat16),
            pltpu.SemaphoreType.DMA((2, most)),
            pltpu.SemaphoreType.DMA((2,)),
        ],
        input_output_aliases={} if before is None else {len(args) - 1: 0},
        compiler_params=pltpu.CompilerParams(vmem_limit_bytes=VMEM),
        cost_estimate=cost,
        name="gram",
    )(*args)


def after(value, *others):
    return lax.optimization_barrier((value, *others))[0]


def shards(expression, cell_type, size_factor, gene_mean):
    types = lax.axis_size("cells")
    blocks = lax.axis_size("blk")
    shard_rows, panel = expression.shape
    cap = 2 * shard_rows // types
    assert types & (types - 1) == 0
    width = 256
    widths = [width] * (panel // width)
    chunks = len(widths)
    home = lax.axis_index("cells").astype(jnp.int32)
    me = lax.axis_index("blk").astype(jnp.int32)
    cores = 2
    chips = blocks // cores
    window = 3

    packed = pack(types, cap, widths, home[None], cell_type, size_factor, expression)

    def swap(block, by):
        return lax.ppermute(block, "cells", [(s, s ^ by) for s in range(types)])

    def across(panel_, by):
        return lax.ppermute(panel_, "blk", [(b, (b + by * cores) % blocks) for b in range(blocks)])

    def side(name, panel_, *waits):
        with jax.named_scope(name):
            return lax.ppermute(after(panel_, *waits), "blk", [(b, b ^ 1) for b in range(blocks)])

    mean = gene_mean.reshape(1, panel)
    order = sorted(range(1, types), key=lambda j: (j == 1, j))
    left, own, far, before = None, None, [], None
    first = None
    for k in range(chunks):
        arrived = [packed[k][0]] + [None] * (types - 1)
        for j in order:
            block = packed[k][j]
            if k:
                block = after(block, before[j])
            with jax.named_scope(f"cells_{j}_chunk_{k}"):
                arrived[j] = swap(block, j)
        before = list(arrived)
        waits = far[k - 2] if k >= 2 else []
        if waits:
            arrived[0] = after(arrived[0], *waits)
        first = first or arrived
        piece = mean[:, k * width : (k + 1) * width]
        scaled, own, left, count = standardize(
            types, cap, width, piece, k, chunks, arrived, first, (own, left) if k else None
        )
        with jax.named_scope(f"far_{k}"):
            far.append([across(scaled, d) for d in range(1, chips)])

    distant = [(me + blocks - d * cores) % blocks for d in range(1, chips)]
    shape = (1, panel, panel * blocks)

    last = chunks - 1
    near = side("near", own)
    far_near = [
        [side(f"far_near_{k}", p, own, *far[last - 1]) for p in far[k]] for k in range(last)
    ]
    groups = [(me * panel, [(own, k) for k in range(chunks)])]
    out = gram(shape, count, left, groups, None, lengthy)
    groups = [((me ^ 1) * panel, [(near, k) for k in range(chunks)])]
    for d, source in enumerate(distant):
        groups.append((source * panel, [(far[k][d], 0) for k in range(last)]))
        groups.append(((source ^ 1) * panel, [(far_near[k][d], 0) for k in range(last)]))
    out = gram(shape, count, left, groups, out, brief)
    far_near = [side(f"far_near_{last}", p, out) for p in far[last]]
    edge = last * width
    groups = [(source * panel + edge, [(p, 0)]) for source, p in zip(distant, far[last])]
    out = gram(shape, count, left, groups, out, brief)
    groups = [((source ^ 1) * panel + edge, [(p, 0)]) for source, p in zip(distant, far_near)]
    return gram(shape, count, left, groups, out, brief)


def solution(mesh):
    placed = (
        P(("parts", "cells"), "blk"),
        P(("parts", "cells")),
        P(("parts", "cells")),
        P(("parts", "blk")),
    )
    return jax.shard_map(
        shards,
        mesh=mesh,
        in_specs=placed,
        out_specs=P(("parts", "cells"), "blk", None),
        check_vma=False,
    )
```

```python
import functools

import jax
import jax.numpy as jnp
from jax import lax
from jax.experimental import pallas as pl
from jax.experimental.pallas import tpu as pltpu
from jax.sharding import PartitionSpec as P

dispersion = 100.0
epsilon = 1e-05
TILE = 16
VMEM = 16 * 1024 * 1024

brief = pl.CostEstimate(flops=1024, bytes_accessed=1024, transcendentals=0)
lengthy = pl.CostEstimate(flops=2 * 10**10, bytes_accessed=1024, transcendentals=0)
whole = pl.BlockSpec(memory_space=pltpu.VMEM)
anywhere = pl.BlockSpec(memory_space=pl.ANY)


def pack_kernel(types, cap, widths, home_ref, type_ref, factor_ref, expr_ref, *outs):
    rows = expr_ref.shape[0]
    home = home_ref[0]
    kind = type_ref[...].reshape(1, rows)
    rel = jnp.bitwise_xor(kind, home)
    lines = max(types, 8)
    hot = lax.broadcasted_iota(jnp.int32, (lines, rows), 0) == rel
    hot_f = jnp.where(hot, 1.0, 0.0)
    upper = jnp.where(
        lax.broadcasted_iota(jnp.int32, (rows, rows), 0)
        <= lax.broadcasted_iota(jnp.int32, (rows, rows), 1),
        1.0,
        0.0,
    ).astype(jnp.bfloat16)
    running = jnp.dot(hot_f.astype(jnp.bfloat16), upper, preferred_element_type=jnp.float32)
    rank = jnp.sum(hot_f * running, axis=0, keepdims=True) - 1.0
    slot = rel * cap + rank.astype(jnp.int32)
    factor = factor_ref[...].astype(jnp.float32).reshape(1, rows)
    factor = jnp.broadcast_to(factor, (TILE, rows)).astype(jnp.bfloat16)
    values = expr_ref[...]
    for j in range(types):
        place = jnp.where(
            lax.broadcasted_iota(jnp.int32, (cap, rows), 0) + j * cap == slot, 1.0, 0.0
        ).astype(jnp.bfloat16)
        block = jnp.dot(place, values, preferred_element_type=jnp.float32).astype(jnp.bfloat16)
        start = 0
        for k, width in enumerate(widths):
            outs[k * types + j][0:cap, :] = block[:, start : start + width]
            start += width
        line = lax.dot_general(
            factor, place, (((1,), (1,)), ((), ())), preferred_element_type=jnp.float32
        )
        row = lax.broadcasted_iota(jnp.int32, (TILE, 1), 0)
        width = widths[0]
        tail = jnp.zeros((TILE, min(width, cap)), jnp.float32)
        for i in range(pl.cdiv(cap, width)):
            tail = jnp.where(row == i, line[:, i * width : min((i + 1) * width, cap)], tail)
        outs[j][cap : cap + TILE, 0 : min(width, cap)] = tail.astype(jnp.bfloat16)


def pack(types, cap, widths, home, cell_type, size_factor, expression):
    rows = expression.shape[0]
    shapes = [
        jax.ShapeDtypeStruct((cap + (TILE if k == 0 else 0), width), jnp.bfloat16)
        for k, width in enumerate(widths)
        for _ in range(types)
    ]
    flat = pl.pallas_call(
        functools.partial(pack_kernel, types, cap, widths),
        out_shape=shapes,
        in_specs=[pl.BlockSpec(memory_space=pltpu.SMEM), whole, whole, whole],
        out_specs=[whole] * len(shapes),
        compiler_params=pltpu.CompilerParams(vmem_limit_bytes=VMEM),
        cost_estimate=brief,
        name="pack",
    )(home, cell_type, size_factor, expression)
    return [flat[k * types : (k + 1) * types] for k in range(len(widths))]


def standardize_kernel(types, cap, lead, separate, chunk, mean_ref, *refs):
    blocks = refs[:types]
    tails = refs[types : 2 * types] if separate else blocks
    base = 0 if separate else cap
    refs = refs[2 * types :] if separate else refs[types:]
    scaled_ref, turned_ref, count_ref, all_ref, work, turned, sems = refs[-7:]
    mean = mean_ref[...]
    width = mean.shape[1]
    piece = min(lead, cap)
    total = jnp.zeros((1, width), jnp.float32)
    count = jnp.zeros((1, 1), jnp.float32)
    alive = []
    for j in range(types):
        column = jnp.zeros((cap, 1), jnp.float32)
        for i in range(pl.cdiv(cap, lead)):
            line = tails[j][base : base + TILE, 0:piece].astype(jnp.float32)[i : i + 1, :]
            diagonal = (
                lax.broadcasted_iota(jnp.int32, (cap, piece), 0)
                == lax.broadcasted_iota(jnp.int32, (cap, piece), 1) + i * lead
            )
            column += jnp.sum(jnp.where(diagonal, line, 0.0), axis=1, keepdims=True)
        live = column > 0.0
        alive.append(live)
        count += jnp.sum(jnp.where(live, 1.0, 0.0), axis=0, keepdims=True)
        expected = jnp.where(live, column * mean, 1.0)
        values = blocks[j][0:cap, :].astype(jnp.float32)
        residual = jnp.where(
            live,
            (values - expected) * lax.rsqrt(expected + expected * expected * (1.0 / dispersion)),
            0.0,
        )
        work[j * cap : (j + 1) * cap, :] = residual
        total += jnp.sum(residual, axis=0, keepdims=True)
    center = total / count
    square = jnp.zeros((1, width), jnp.float32)
    for j in range(types):
        centered = jnp.where(alive[j], work[j * cap : (j + 1) * cap, :] - center, 0.0)
        work[j * cap : (j + 1) * cap, :] = centered
        square += jnp.sum(centered * centered, axis=0, keepdims=True)
    scale = lax.rsqrt(square / count + epsilon)
    for j in range(types):
        scaled = work[j * cap : (j + 1) * cap, :] * scale
        scaled_ref[j * cap : (j + 1) * cap, :] = scaled.astype(jnp.bfloat16)
        work[j * cap : (j + 1) * cap, :] = scaled
    slots = types * cap
    rows = pl.ds(chunk * slots, slots)
    copies = [pltpu.make_async_copy(scaled_ref, all_ref.at[rows, :], sems.at[0])]
    copies[0].start()
    turned[...] = jnp.transpose(work[...]).astype(jnp.bfloat16)
    rows = pl.ds(chunk * width, width)
    copies.append(pltpu.make_async_copy(turned, turned_ref.at[rows, :], sems.at[1]))
    copies[-1].start()
    for copy in copies:
        copy.wait()
    count_ref[...] = jnp.broadcast_to(count, count_ref.shape)


def standardize(types, cap, lead, mean, chunk, chunks, blocks, first, left, own):
    width = mean.shape[1]
    separate = first is not blocks
    slots = types * cap
    specs = [whole] * (1 + types)
    args = [mean, *blocks]
    if separate:
        specs += [pl.BlockSpec((TILE, lead), lambda i: (cap // TILE, 0))] * types
        args += list(first)
    shapes = [
        jax.ShapeDtypeStruct((slots, width), jnp.bfloat16),
        jax.ShapeDtypeStruct((chunks * width, slots), jnp.bfloat16),
        jax.ShapeDtypeStruct((8, 128), jnp.float32),
        jax.ShapeDtypeStruct((chunks * slots, width), jnp.bfloat16),
    ]
    aliases = {}
    for value, output in ((left, 1), (own, 3)):
        if value is not None:
            aliases[len(args)] = output
            specs.append(anywhere)
            args.append(value)
    return pl.pallas_call(
        functools.partial(standardize_kernel, types, cap, lead, separate, chunk),
        grid=(1,),
        out_shape=shapes,
        in_specs=specs,
        out_specs=[whole, anywhere, whole, anywhere],
        scratch_shapes=[
            pltpu.VMEM((slots, width), jnp.float32),
            pltpu.VMEM((width, slots), jnp.bfloat16),
            pltpu.SemaphoreType.DMA((2,)),
        ],
        input_output_aliases=aliases,
        compiler_params=pltpu.CompilerParams(vmem_limit_bytes=VMEM),
        cost_estimate=lengthy,
        name="standardize",
    )(*args)


def gram_kernel(groups, spans, arrays, strip, place_ref, count_ref, left_ref, *refs):
    sources = refs[:arrays]
    out_ref, panel, tile, panel_sem, tile_sem = refs[-5:]
    slots = left_ref.shape[1]
    inverse = 1.0 / count_ref[0:1, 0:1]

    def fetch(g):
        copies, column = [], 0
        for source, row, width in groups[g]:
            copies.append(
                pltpu.make_async_copy(
                    sources[source].at[pl.ds(row, slots), :],
                    panel.at[g % 2, :, pl.ds(column, width)],
                    panel_sem.at[g % 2, len(copies)],
                )
            )
            column += width
        return copies, column

    for copy in fetch(0)[0]:
        copy.start()
    stores = []
    for g in range(len(groups)):
        if g + 1 < len(groups):
            for copy in fetch(g + 1)[0]:
                copy.start()
        copies, columns = fetch(g)
        for copy in copies:
            copy.wait()
        place = pl.multiple_of(place_ref[g] * 128, 128)
        for row in range(*spans[g], strip):
            slot = len(stores) % 2
            if len(stores) >= 2:
                stores[-2].wait()
            product = jnp.dot(
                left_ref[row : row + strip, :],
                panel[g % 2, :, 0:columns],
                preferred_element_type=jnp.float32,
            )
            tile[slot, :, 0:columns] = (product * inverse).astype(jnp.bfloat16)
            stores.append(
                pltpu.make_async_copy(
                    tile.at[slot, :, pl.ds(0, columns)],
                    out_ref.at[0, pl.ds(row, strip), pl.ds(place, columns)],
                    tile_sem.at[slot],
                )
            )
            stores[-1].start()
    for store in stores[-2:]:
        store.wait()


def gram(shape, count, left, groups, before, cost):
    rows, slots = left.shape
    strip = min(rows, 256)
    spans = [span for span, _, _ in groups]
    places = jnp.stack([place for _, place, _ in groups]) // 128
    arrays, layout = [], []
    for _, _, panels in groups:
        layout.append([])
        for array, index in panels:
            if not any(array is other for other in arrays):
                arrays.append(array)
            source = [array is other for other in arrays].index(True)
            layout[-1].append((source, index * slots, array.shape[1]))
    most = max(len(panels) for panels in layout)
    widest = max(sum(width for _, _, width in panels) for panels in layout)
    args = [places.astype(jnp.int32), count, left, *arrays]
    args += [] if before is None else [before]
    specs = [pl.BlockSpec(memory_space=pltpu.SMEM), whole, whole] + [anywhere] * (len(args) - 3)
    return pl.pallas_call(
        functools.partial(gram_kernel, layout, spans, len(arrays), strip),
        in_specs=specs,
        out_specs=anywhere,
        out_shape=jax.ShapeDtypeStruct(shape, jnp.bfloat16),
        scratch_shapes=[
            pltpu.VMEM((2, slots, widest), jnp.bfloat16),
            pltpu.VMEM((2, strip, widest), jnp.bfloat16),
            pltpu.SemaphoreType.DMA((2, most)),
            pltpu.SemaphoreType.DMA((2,)),
        ],
        input_output_aliases={} if before is None else {len(args) - 1: 0},
        compiler_params=pltpu.CompilerParams(vmem_limit_bytes=VMEM),
        cost_estimate=cost,
        name="gram",
    )(*args)


def after(value, *others):
    return lax.optimization_barrier((value, *others))[0]


def shards(expression, cell_type, size_factor, gene_mean):
    types = lax.axis_size("cells")
    blocks = lax.axis_size("blk")
    shard_rows, panel = expression.shape
    cap = 2 * shard_rows // types
    assert types & (types - 1) == 0
    width = 256
    widths = [width] * (panel // width)
    chunks = len(widths)
    home = lax.axis_index("cells").astype(jnp.int32)
    me = lax.axis_index("blk").astype(jnp.int32)
    cores = 2
    chips = blocks // cores
    window = 3

    packed = pack(types, cap, widths, home[None], cell_type, size_factor, expression)

    def swap(block, by):
        return lax.ppermute(block, "cells", [(s, s ^ by) for s in range(types)])

    def across(panel_, by):
        return lax.ppermute(panel_, "blk", [(b, (b + by * cores) % blocks) for b in range(blocks)])

    def side(name, panel_, *waits):
        with jax.named_scope(name):
            return lax.ppermute(after(panel_, *waits), "blk", [(b, b ^ 1) for b in range(blocks)])

    mean = gene_mean.reshape(1, panel)
    order = sorted(range(1, types), key=lambda j: (j == 1, j))
    distant = [(me + blocks - d * cores) % blocks for d in range(1, chips)]
    shape = (1, panel, panel * blocks)
    early, last = 2, chunks - 1
    upper, lower, every = (0, early * width), (early * width, panel), (0, panel)
    left, own, out, far, before = None, None, None, [], None
    for k in range(chunks):
        arrived = [packed[k][0]] + [None] * (types - 1)
        for j in order:
            block = packed[k][j]
            if k:
                block = after(block, before[j], *([out] if k == early + 1 and j != 1 else []))
            with jax.named_scope(f"cells_{j}_chunk_{k}"):
                arrived[j] = swap(block, j)
        before = list(arrived)
        waits = far[k - 2] if k >= 2 else []
        if k == early:
            groups = [
                (upper, me * panel, [(own, i) for i in range(early)]),
            ]
            groups += [
                (upper, source * panel, [(p, 0)]) for source, p in zip(distant, far[0])
            ]
            out = gram(shape, count, left, groups, None, brief)
            waits = waits + [out]
        if waits:
            arrived[0] = after(arrived[0], *waits)
        if k == 0:
            first = arrived
        piece = mean[:, k * width : (k + 1) * width]
        scaled, left, count, own = standardize(
            types, cap, width, piece, k, chunks, arrived, first, left, own
        )
        with jax.named_scope(f"far_{k}"):
            far.append([across(scaled, d) for d in range(1, chips)])

    near = side("near", own)
    far_near = [
        [side(f"far_near_{k}", p, own, *far[last - 1]) for p in far[k]]
        for k in range(max(last - 1, 1))
    ]
    edge = early * width
    groups = []
    if out is not None:
        rest = [(own, i) for i in range(early, chunks)]
        groups.append((upper, me * panel + edge, rest))
        groups.append((lower, me * panel, [(own, i) for i in range(chunks)]))
    else:
        groups.append((every, me * panel, [(own, i) for i in range(chunks)]))
    out = gram(shape, count, left, groups, out, lengthy)
    begun = lower if chunks > early else every
    groups = [
        (every, (me ^ 1) * panel, [(near, i) for i in range(chunks)]),
    ]
    for d, source in enumerate(distant):
        groups.append((begun, source * panel, [(far[0][d], 0)]))
        if last > 1:
            panels = [(far[k][d], 0) for k in range(1, last)]
            groups.append((every, source * panel + width, panels))
        panels = [(got[d], 0) for got in far_near]
        groups.append((every, (source ^ 1) * panel, panels))
    out = gram(shape, count, left, groups, out, brief)
    start = len(far_near)
    far_near = [
        [side(f"far_near_{k}", p, out) for p in far[k]] for k in range(start, chunks)
    ]
    edge = last * width
    groups = [(every, source * panel + edge, [(p, 0)]) for source, p in zip(distant, far[last])]
    out = gram(shape, count, left, groups, out, brief)
    edge = start * width
    groups = [
        (every, (source ^ 1) * panel + edge, [(got[d], 0) for got in far_near])
        for d, source in enumerate(distant)
    ]
    return gram(shape, count, left, groups, out, brief)


def solution(mesh):
    placed = (
        P(("parts", "cells"), "blk"),
        P(("parts", "cells")),
        P(("parts", "cells")),
        P(("parts", "blk")),
    )
    return jax.shard_map(
        shards,
        mesh=mesh,
        in_specs=placed,
        out_specs=P(("parts", "cells"), "blk", None),
        check_vma=False,
    )
```

```python
import functools

import jax
import jax.numpy as jnp
from jax import lax
from jax.experimental import pallas as pl
from jax.experimental.pallas import tpu as pltpu
from jax.sharding import PartitionSpec as P

dispersion = 100.0
epsilon = 1e-05
TILE = 16
VMEM = 16 * 1024 * 1024

brief = pl.CostEstimate(flops=1024, bytes_accessed=1024, transcendentals=0)
lengthy = pl.CostEstimate(flops=2 * 10**10, bytes_accessed=1024, transcendentals=0)
whole = pl.BlockSpec(memory_space=pltpu.VMEM)
anywhere = pl.BlockSpec(memory_space=pl.ANY)


def pack_kernel(types, cap, widths, type_ref, factor_ref, expr_ref, *outs):
    rows = expr_ref.shape[0]
    home = lax.axis_index("cells")
    kind = type_ref[...].reshape(1, rows)
    rel = jnp.bitwise_xor(kind, home)
    lines = max(types, 8)
    hot = lax.broadcasted_iota(jnp.int32, (lines, rows), 0) == rel
    hot_f = jnp.where(hot, 1.0, 0.0)
    upper = jnp.where(
        lax.broadcasted_iota(jnp.int32, (rows, rows), 0)
        <= lax.broadcasted_iota(jnp.int32, (rows, rows), 1),
        1.0,
        0.0,
    ).astype(jnp.bfloat16)
    running = jnp.dot(hot_f.astype(jnp.bfloat16), upper, preferred_element_type=jnp.float32)
    rank = jnp.sum(hot_f * running, axis=0, keepdims=True) - 1.0
    slot = rel * cap + rank.astype(jnp.int32)
    factor = factor_ref[...].astype(jnp.float32).reshape(1, rows)
    factor = jnp.broadcast_to(factor, (TILE, rows)).astype(jnp.bfloat16)
    values = expr_ref[...]
    for j in range(types):
        place = jnp.where(
            lax.broadcasted_iota(jnp.int32, (cap, rows), 0) + j * cap == slot, 1.0, 0.0
        ).astype(jnp.bfloat16)
        block = jnp.dot(place, values, preferred_element_type=jnp.float32).astype(jnp.bfloat16)
        start = 0
        for k, width in enumerate(widths):
            outs[k * types + j][0:cap, :] = block[:, start : start + width]
            start += width
        line = lax.dot_general(
            factor, place, (((1,), (1,)), ((), ())), preferred_element_type=jnp.float32
        )
        row = lax.broadcasted_iota(jnp.int32, (TILE, 1), 0)
        width = widths[0]
        tail = jnp.zeros((TILE, min(width, cap)), jnp.float32)
        for i in range(pl.cdiv(cap, width)):
            tail = jnp.where(row == i, line[:, i * width : min((i + 1) * width, cap)], tail)
        outs[j][cap : cap + TILE, 0 : min(width, cap)] = tail.astype(jnp.bfloat16)


def pack(types, cap, widths, cell_type, size_factor, expression):
    rows = expression.shape[0]
    shapes = [
        jax.ShapeDtypeStruct((cap + (TILE if k == 0 else 0), width), jnp.bfloat16)
        for k, width in enumerate(widths)
        for _ in range(types)
    ]
    flat = pl.pallas_call(
        functools.partial(pack_kernel, types, cap, widths),
        out_shape=shapes,
        in_specs=[whole] * 3,
        out_specs=[whole] * len(shapes),
        compiler_params=pltpu.CompilerParams(vmem_limit_bytes=VMEM),
        cost_estimate=brief,
        name="pack",
    )(cell_type, size_factor, expression)
    return [flat[k * types : (k + 1) * types] for k in range(len(widths))]


def standardize_kernel(types, cap, lead, separate, chunk, mean_ref, *refs):
    blocks = refs[:types]
    tails = refs[types : 2 * types] if separate else blocks
    base = 0 if separate else cap
    refs = refs[2 * types :] if separate else refs[types:]
    scaled_ref, turned_ref, count_ref, all_ref, work, turned, sems = refs[-7:]
    width = work.shape[1]
    mean = mean_ref[:, chunk * width : (chunk + 1) * width]
    piece = min(lead, cap)
    total = jnp.zeros((1, width), jnp.float32)
    count = jnp.zeros((1, 1), jnp.float32)
    alive = []
    for j in range(types):
        column = jnp.zeros((cap, 1), jnp.float32)
        for i in range(pl.cdiv(cap, lead)):
            line = tails[j][base : base + TILE, 0:piece].astype(jnp.float32)[i : i + 1, :]
            diagonal = (
                lax.broadcasted_iota(jnp.int32, (cap, piece), 0)
                == lax.broadcasted_iota(jnp.int32, (cap, piece), 1) + i * lead
            )
            column += jnp.sum(jnp.where(diagonal, line, 0.0), axis=1, keepdims=True)
        live = column > 0.0
        alive.append(live)
        count += jnp.sum(jnp.where(live, 1.0, 0.0), axis=0, keepdims=True)
        expected = jnp.where(live, column * mean, 1.0)
        values = blocks[j][0:cap, :].astype(jnp.float32)
        residual = jnp.where(
            live,
            (values - expected) * lax.rsqrt(expected + expected * expected * (1.0 / dispersion)),
            0.0,
        )
        work[j * cap : (j + 1) * cap, :] = residual
        total += jnp.sum(residual, axis=0, keepdims=True)
    center = total / count
    square = jnp.zeros((1, width), jnp.float32)
    for j in range(types):
        centered = jnp.where(alive[j], work[j * cap : (j + 1) * cap, :] - center, 0.0)
        work[j * cap : (j + 1) * cap, :] = centered
        square += jnp.sum(centered * centered, axis=0, keepdims=True)
    scale = lax.rsqrt(square / count + epsilon)
    for j in range(types):
        scaled = work[j * cap : (j + 1) * cap, :] * scale
        scaled_ref[j * cap : (j + 1) * cap, :] = scaled.astype(jnp.bfloat16)
        work[j * cap : (j + 1) * cap, :] = scaled
    slots = types * cap
    rows = pl.ds(chunk * slots, slots)
    copies = [pltpu.make_async_copy(scaled_ref, all_ref.at[rows, :], sems.at[0])]
    copies[0].start()
    turned[...] = jnp.transpose(work[...]).astype(jnp.bfloat16)
    rows = pl.ds(chunk * width, width)
    copies.append(pltpu.make_async_copy(turned, turned_ref.at[rows, :], sems.at[1]))
    copies[-1].start()
    for copy in copies:
        copy.wait()
    count_ref[...] = jnp.broadcast_to(count, count_ref.shape)


def standardize(types, cap, lead, width, mean, chunk, blocks, first, left, own):
    chunks = mean.shape[1] // width
    separate = first is not blocks
    slots = types * cap
    specs = [whole] * (1 + types)
    args = [mean, *blocks]
    if separate:
        specs += [pl.BlockSpec((TILE, lead), lambda i: (cap // TILE, 0))] * types
        args += list(first)
    shapes = [
        jax.ShapeDtypeStruct((slots, width), jnp.bfloat16),
        jax.ShapeDtypeStruct((chunks * width, slots), jnp.bfloat16),
        jax.ShapeDtypeStruct((8, 128), jnp.float32),
        jax.ShapeDtypeStruct((chunks * slots, width), jnp.bfloat16),
    ]
    aliases = {}
    for value, output in ((left, 1), (own, 3)):
        if value is not None:
            aliases[len(args)] = output
            specs.append(anywhere)
            args.append(value)
    return pl.pallas_call(
        functools.partial(standardize_kernel, types, cap, lead, separate, chunk),
        grid=(1,),
        out_shape=shapes,
        in_specs=specs,
        out_specs=[whole, anywhere, whole, anywhere],
        scratch_shapes=[
            pltpu.VMEM((slots, width), jnp.float32),
            pltpu.VMEM((width, slots), jnp.bfloat16),
            pltpu.SemaphoreType.DMA((2,)),
        ],
        input_output_aliases=aliases,
        compiler_params=pltpu.CompilerParams(vmem_limit_bytes=VMEM),
        cost_estimate=lengthy,
        name="standardize",
    )(*args)


def gram_kernel(blocks, cores, items, count_ref, left_ref, *refs):
    out_ref, tile, sems = refs[-3:]
    rows, slots = left_ref.shape
    width = tile.shape[2]
    inverse = 1.0 / count_ref[0:1, 0:1]
    me = lax.axis_index("blk")
    stores = []
    for source, index, chip, flip, chunk in items:
        slot = len(stores) % 2
        if len(stores) >= 2:
            stores[-2].wait()
        product = jnp.dot(
            left_ref[...],
            refs[source][index * slots : (index + 1) * slots, :],
            preferred_element_type=jnp.float32,
        )
        tile[slot] = (product * inverse).astype(jnp.bfloat16)
        owner = lax.rem(me + (blocks - chip * cores), blocks)
        owner = jnp.bitwise_xor(owner, flip)
        column = pl.multiple_of(owner * rows + chunk * width, 128)
        stores.append(
            pltpu.make_async_copy(
                tile.at[slot], out_ref.at[0, :, pl.ds(column, width)], sems.at[slot]
            )
        )
        stores[-1].start()
    for store in stores[-2:]:
        store.wait()


def gram(blocks, cores, count, left, panels, before, cost):
    rows, slots = left.shape
    arrays, items = [], []
    for array, index, *owner in panels:
        if not any(array is other for other in arrays):
            arrays.append(array)
        items.append(([array is other for other in arrays].index(True), index, *owner))
    width = arrays[0].shape[1]
    args = [count, left, *arrays]
    specs = [whole] * len(args)
    if before is not None:
        args.append(before)
        specs.append(anywhere)
    return pl.pallas_call(
        functools.partial(gram_kernel, blocks, cores, items),
        in_specs=specs,
        out_specs=anywhere,
        out_shape=jax.ShapeDtypeStruct((1, rows, rows * blocks), jnp.bfloat16),
        scratch_shapes=[
            pltpu.VMEM((2, rows, width), jnp.bfloat16),
            pltpu.SemaphoreType.DMA((2,)),
        ],
        input_output_aliases={} if before is None else {len(args) - 1: 0},
        compiler_params=pltpu.CompilerParams(vmem_limit_bytes=VMEM),
        cost_estimate=cost,
        name="gram",
    )(*args)


def after(value, *others):
    return lax.optimization_barrier((value, *others))[0]


def shards(expression, cell_type, size_factor, gene_mean):
    types = lax.axis_size("cells")
    blocks = lax.axis_size("blk")
    shard_rows, panel = expression.shape
    cap = 2 * shard_rows // types
    assert types & (types - 1) == 0
    width = 256
    widths = [width] * (panel // width)
    chunks = len(widths)
    cores = 2
    chips = blocks // cores
    window = 3

    packed = pack(types, cap, widths, cell_type, size_factor, expression)

    def swap(block, by):
        return lax.ppermute(block, "cells", [(s, s ^ by) for s in range(types)])

    def across(panel_, by):
        return lax.ppermute(panel_, "blk", [(b, (b + by * cores) % blocks) for b in range(blocks)])

    def side(name, panel_, *waits):
        with jax.named_scope(name):
            return lax.ppermute(after(panel_, *waits), "blk", [(b, b ^ 1) for b in range(blocks)])

    mean = gene_mean.reshape(1, panel)
    order = sorted(range(1, types), key=lambda j: (j == 1, j))
    left, own, far, before = None, None, [], None
    for k in range(chunks):
        arrived = [packed[k][0]] + [None] * (types - 1)
        for j in order:
            block = packed[k][j]
            if k:
                block = after(block, before[j])
            with jax.named_scope(f"cells_{j}_chunk_{k}"):
                arrived[j] = swap(block, j)
        before = list(arrived)
        if k >= 2:
            arrived[0] = after(arrived[0], *far[k - 2])
        if k == 0:
            first = arrived
        scaled, left, count, own = standardize(
            types, cap, width, width, mean, k, arrived, first, left, own
        )
        with jax.named_scope(f"far_{k}"):
            far.append([across(scaled, d) for d in range(1, chips)])

    multiply = functools.partial(gram, blocks, cores, count, left)
    last = chunks - 1
    near = side("near", own)
    far_near = [
        [side(f"far_near_{k}", p, own, *far[last - 1]) for p in far[k]] for k in range(last)
    ]
    out = multiply([(own, k, 0, 0, k) for k in range(chunks)], None, lengthy)
    panels = [(near, k, 0, 1, k) for k in range(chunks)]
    for flip, group in ((0, far), (1, far_near)):
        panels += [(p, 0, d, flip, k) for k in range(last) for d, p in enumerate(group[k], 1)]
    out = multiply(panels, out, brief)
    far_near = [side(f"far_near_{last}", p, out) for p in far[last]]
    out = multiply([(p, 0, d, 0, last) for d, p in enumerate(far[last], 1)], out, brief)
    return multiply([(p, 0, d, 1, last) for d, p in enumerate(far_near, 1)], out, brief)


def solution(mesh):
    placed = (
        P(("parts", "cells"), "blk"),
        P(("parts", "cells")),
        P(("parts", "cells")),
        P(("parts", "blk")),
    )
    return jax.shard_map(
        shards,
        mesh=mesh,
        in_specs=placed,
        out_specs=P(("parts", "cells"), "blk", None),
        check_vma=False,
    )
```

```python
import functools

import jax
import jax.numpy as jnp
from jax import lax
from jax.experimental import pallas as pl
from jax.experimental.pallas import tpu as pltpu
from jax.sharding import PartitionSpec as P

dispersion = 100.0
epsilon = 1e-05
TILE = 16
VMEM = 16 * 1024 * 1024

brief = pl.CostEstimate(flops=1024, bytes_accessed=1024, transcendentals=0)
lengthy = pl.CostEstimate(flops=2 * 10**10, bytes_accessed=1024, transcendentals=0)
whole = pl.BlockSpec(memory_space=pltpu.VMEM)
anywhere = pl.BlockSpec(memory_space=pl.ANY)


def pack_kernel(types, cap, widths, type_ref, factor_ref, expr_ref, *outs):
    rows = expr_ref.shape[0]
    home = lax.axis_index("cells")
    kind = type_ref[...].reshape(1, rows)
    rel = jnp.bitwise_xor(kind, home)
    lines = max(types, 8)
    hot = lax.broadcasted_iota(jnp.int32, (lines, rows), 0) == rel
    hot_f = jnp.where(hot, 1.0, 0.0)
    upper = jnp.where(
        lax.broadcasted_iota(jnp.int32, (rows, rows), 0)
        <= lax.broadcasted_iota(jnp.int32, (rows, rows), 1),
        1.0,
        0.0,
    ).astype(jnp.bfloat16)
    running = jnp.dot(hot_f.astype(jnp.bfloat16), upper, preferred_element_type=jnp.float32)
    rank = jnp.sum(hot_f * running, axis=0, keepdims=True) - 1.0
    slot = rel * cap + rank.astype(jnp.int32)
    factor = factor_ref[...].astype(jnp.float32).reshape(1, rows)
    factor = jnp.broadcast_to(factor, (TILE, rows)).astype(jnp.bfloat16)
    values = expr_ref[...]
    for j in range(types):
        place = jnp.where(
            lax.broadcasted_iota(jnp.int32, (cap, rows), 0) + j * cap == slot, 1.0, 0.0
        ).astype(jnp.bfloat16)
        block = jnp.dot(place, values, preferred_element_type=jnp.float32).astype(jnp.bfloat16)
        start = 0
        for k, width in enumerate(widths):
            outs[k * types + j][0:cap, :] = block[:, start : start + width]
            start += width
        line = lax.dot_general(
            factor, place, (((1,), (1,)), ((), ())), preferred_element_type=jnp.float32
        )
        row = lax.broadcasted_iota(jnp.int32, (TILE, 1), 0)
        width = widths[0]
        tail = jnp.zeros((TILE, min(width, cap)), jnp.float32)
        for i in range(pl.cdiv(cap, width)):
            tail = jnp.where(row == i, line[:, i * width : min((i + 1) * width, cap)], tail)
        outs[j][cap : cap + TILE, 0 : min(width, cap)] = tail.astype(jnp.bfloat16)


def pack(types, cap, widths, cell_type, size_factor, expression):
    rows = expression.shape[0]
    shapes = [
        jax.ShapeDtypeStruct((cap + (TILE if k == 0 else 0), width), jnp.bfloat16)
        for k, width in enumerate(widths)
        for _ in range(types)
    ]
    flat = pl.pallas_call(
        functools.partial(pack_kernel, types, cap, widths),
        out_shape=shapes,
        in_specs=[whole] * 3,
        out_specs=[whole] * len(shapes),
        compiler_params=pltpu.CompilerParams(vmem_limit_bytes=VMEM),
        cost_estimate=brief,
        name="pack",
    )(cell_type, size_factor, expression)
    return [flat[k * types : (k + 1) * types] for k in range(len(widths))]


def standardize_kernel(types, cap, lead, separate, chunk, mean_ref, *refs):
    blocks = refs[:types]
    tails = refs[types : 2 * types] if separate else blocks
    base = 0 if separate else cap
    refs = refs[2 * types :] if separate else refs[types:]
    scaled_ref, turned_ref, count_ref, all_ref, work, turned, sems = refs[-7:]
    width = work.shape[1]
    mean = mean_ref[:, chunk * width : (chunk + 1) * width]
    piece = min(lead, cap)
    total = jnp.zeros((1, width), jnp.float32)
    count = jnp.zeros((1, 1), jnp.float32)
    alive = []
    for j in range(types):
        column = jnp.zeros((cap, 1), jnp.float32)
        for i in range(pl.cdiv(cap, lead)):
            line = tails[j][base : base + TILE, 0:piece].astype(jnp.float32)[i : i + 1, :]
            diagonal = (
                lax.broadcasted_iota(jnp.int32, (cap, piece), 0)
                == lax.broadcasted_iota(jnp.int32, (cap, piece), 1) + i * lead
            )
            column += jnp.sum(jnp.where(diagonal, line, 0.0), axis=1, keepdims=True)
        live = column > 0.0
        alive.append(live)
        count += jnp.sum(jnp.where(live, 1.0, 0.0), axis=0, keepdims=True)
        expected = jnp.where(live, column * mean, 1.0)
        values = blocks[j][0:cap, :].astype(jnp.float32)
        residual = jnp.where(
            live,
            (values - expected) * lax.rsqrt(expected + expected * expected * (1.0 / dispersion)),
            0.0,
        )
        work[j * cap : (j + 1) * cap, :] = residual
        total += jnp.sum(residual, axis=0, keepdims=True)
    center = total / count
    square = jnp.zeros((1, width), jnp.float32)
    for j in range(types):
        centered = jnp.where(alive[j], work[j * cap : (j + 1) * cap, :] - center, 0.0)
        work[j * cap : (j + 1) * cap, :] = centered
        square += jnp.sum(centered * centered, axis=0, keepdims=True)
    scale = lax.rsqrt(square / count + epsilon)
    for j in range(types):
        scaled = work[j * cap : (j + 1) * cap, :] * scale
        scaled_ref[j * cap : (j + 1) * cap, :] = scaled.astype(jnp.bfloat16)
        work[j * cap : (j + 1) * cap, :] = scaled
    slots = types * cap
    columns = pl.ds(chunk * width, width)
    copies = [pltpu.make_async_copy(scaled_ref, all_ref.at[:, columns], sems.at[0])]
    copies[0].start()
    turned[...] = jnp.transpose(work[...]).astype(jnp.bfloat16)
    copies.append(pltpu.make_async_copy(turned, turned_ref.at[columns, :], sems.at[1]))
    copies[-1].start()
    for copy in copies:
        copy.wait()
    count_ref[...] = jnp.broadcast_to(count, count_ref.shape)


def standardize(types, cap, lead, width, mean, chunk, blocks, first, left, own):
    chunks = mean.shape[1] // width
    separate = first is not blocks
    slots = types * cap
    specs = [whole] * (1 + types)
    args = [mean, *blocks]
    if separate:
        specs += [pl.BlockSpec((TILE, lead), lambda i: (cap // TILE, 0))] * types
        args += list(first)
    shapes = [
        jax.ShapeDtypeStruct((slots, width), jnp.bfloat16),
        jax.ShapeDtypeStruct((chunks * width, slots), jnp.bfloat16),
        jax.ShapeDtypeStruct((8, 128), jnp.float32),
        jax.ShapeDtypeStruct((slots, chunks * width), jnp.bfloat16),
    ]
    aliases = {}
    for value, output in ((left, 1), (own, 3)):
        if value is not None:
            aliases[len(args)] = output
            specs.append(anywhere)
            args.append(value)
    return pl.pallas_call(
        functools.partial(standardize_kernel, types, cap, lead, separate, chunk),
        grid=(1,),
        out_shape=shapes,
        in_specs=specs,
        out_specs=[whole, anywhere, whole, anywhere],
        scratch_shapes=[
            pltpu.VMEM((slots, width), jnp.float32),
            pltpu.VMEM((width, slots), jnp.bfloat16),
            pltpu.SemaphoreType.DMA((2,)),
        ],
        input_output_aliases=aliases,
        compiler_params=pltpu.CompilerParams(vmem_limit_bytes=VMEM),
        cost_estimate=lengthy,
        name="standardize",
    )(*args)


def gram_kernel(blocks, cores, strip, groups, arrays, count_ref, left_ref, *refs):
    sources = refs[:arrays]
    out_ref, joined, tile, join_sems, sems = refs[-5:]
    rows, slots = left_ref.shape
    inverse = 1.0 / count_ref[0:1, 0:1]
    me = lax.axis_index("blk")

    joins, column = [], 0
    for panels, _ in groups:
        joins.append([])
        if len(panels) > 1:
            for index in panels:
                width = sources[index].shape[1]
                spot = joined.at[:, pl.ds(column, width)]
                joins[-1].append((column, sources[index], spot))
                column += width
    sent = 0
    for parts in joins:
        for _, source, spot in parts:
            pltpu.make_async_copy(source, spot, join_sems.at[sent]).start()
            sent += 1
    stores, sent = [], 0
    for (panels, (chip, flip, first)), parts in zip(groups, joins):
        for _, source, spot in parts:
            pltpu.make_async_copy(source, spot, join_sems.at[sent]).wait()
            sent += 1
        width = sum(sources[index].shape[1] for index in panels)
        owner = lax.rem(me + (blocks - chip * cores), blocks)
        owner = jnp.bitwise_xor(owner, flip)
        column = pl.multiple_of(owner * rows + first, 128)
        for row in range(0, rows, strip):
            slot = len(stores) % 2
            if len(stores) >= 2:
                stores[-2].wait()
            if parts:
                right = joined[:, parts[0][0] : parts[0][0] + width]
            else:
                right = sources[panels[0]][...]
            product = jnp.dot(
                left_ref[row : row + strip, :], right, preferred_element_type=jnp.float32
            )
            tile[slot, :, 0:width] = (product * inverse).astype(jnp.bfloat16)
            stores.append(
                pltpu.make_async_copy(
                    tile.at[slot, :, pl.ds(0, width)],
                    out_ref.at[0, pl.ds(row, strip), pl.ds(column, width)],
                    sems.at[slot],
                )
            )
            stores[-1].start()
    for store in stores[-2:]:
        store.wait()


def gram(blocks, cores, count, left, groups, before, cost):
    rows, slots = left.shape
    arrays, layout = [], []
    for panels, place in groups:
        layout.append((list(range(len(arrays), len(arrays) + len(panels))), place))
        arrays += panels
    joined = [array for panels, _ in groups if len(panels) > 1 for array in panels]
    widest = max(sum(array.shape[1] for array in panels) for panels, _ in groups)
    strip = min(rows, 256)
    args = [count, left, *arrays]
    specs = [whole] * len(args)
    if before is not None:
        args.append(before)
        specs.append(anywhere)
    return pl.pallas_call(
        functools.partial(gram_kernel, blocks, cores, strip, layout, len(arrays)),
        in_specs=specs,
        out_specs=anywhere,
        out_shape=jax.ShapeDtypeStruct((1, rows, rows * blocks), jnp.bfloat16),
        scratch_shapes=[
            pltpu.VMEM((slots, max(sum(array.shape[1] for array in joined), 128)), jnp.bfloat16),
            pltpu.VMEM((2, strip, widest), jnp.bfloat16),
            pltpu.SemaphoreType.DMA((max(len(joined), 1),)),
            pltpu.SemaphoreType.DMA((2,)),
        ],
        input_output_aliases={} if before is None else {len(args) - 1: 0},
        compiler_params=pltpu.CompilerParams(vmem_limit_bytes=VMEM),
        cost_estimate=cost,
        name="gram",
    )(*args)


def after(value, *others):
    return lax.optimization_barrier((value, *others))[0]


def shards(expression, cell_type, size_factor, gene_mean):
    types = lax.axis_size("cells")
    blocks = lax.axis_size("blk")
    shard_rows, panel = expression.shape
    cap = 2 * shard_rows // types
    assert types & (types - 1) == 0
    width = 256
    widths = [width] * (panel // width)
    chunks = len(widths)
    cores = 2
    chips = blocks // cores
    window = 3

    packed = pack(types, cap, widths, cell_type, size_factor, expression)

    def swap(block, by):
        return lax.ppermute(block, "cells", [(s, s ^ by) for s in range(types)])

    def across(panel_, by):
        return lax.ppermute(panel_, "blk", [(b, (b + by * cores) % blocks) for b in range(blocks)])

    def side(name, panel_, *waits):
        with jax.named_scope(name):
            return lax.ppermute(after(panel_, *waits), "blk", [(b, b ^ 1) for b in range(blocks)])

    mean = gene_mean.reshape(1, panel)
    order = sorted(range(1, types), key=lambda j: (j == 1, j))
    left, own, far, before = None, None, [], None
    for k in range(chunks):
        arrived = [packed[k][0]] + [None] * (types - 1)
        for j in order:
            block = packed[k][j]
            if k:
                block = after(block, before[j])
            with jax.named_scope(f"cells_{j}_chunk_{k}"):
                arrived[j] = swap(block, j)
        before = list(arrived)
        if k >= 2:
            arrived[0] = after(arrived[0], *far[k - 2])
        if k == 0:
            first = arrived
        scaled, left, count, own = standardize(
            types, cap, width, width, mean, k, arrived, first, left, own
        )
        with jax.named_scope(f"far_{k}"):
            far.append([across(scaled, d) for d in range(1, chips)])

    multiply = functools.partial(gram, blocks, cores, count, left)
    last = chunks - 1
    near = side("near", own)
    far_near = [
        [side(f"far_near_{k}", p, own, *far[last - 1]) for p in far[k]] for k in range(last)
    ]
    out = multiply([([own], (0, 0, 0))], None, lengthy)
    groups = [([near], (0, 1, 0))]
    for flip, group in ((0, far), (1, far_near)):
        for d in range(1, chips):
            groups.append(([group[k][d - 1] for k in range(last)], (d, flip, 0)))
    out = multiply(groups, out, brief)
    far_near = [side(f"far_near_{last}", p, out) for p in far[last]]
    edge = last * width
    out = multiply([([p], (d, 0, edge)) for d, p in enumerate(far[last], 1)], out, brief)
    return multiply([([p], (d, 1, edge)) for d, p in enumerate(far_near, 1)], out, brief)


def solution(mesh):
    placed = (
        P(("parts", "cells"), "blk"),
        P(("parts", "cells")),
        P(("parts", "cells")),
        P(("parts", "blk")),
    )
    return jax.shard_map(
        shards,
        mesh=mesh,
        in_specs=placed,
        out_specs=P(("parts", "cells"), "blk", None),
        check_vma=False,
    )
```

```python
import functools

import jax
import jax.numpy as jnp
from jax import lax
from jax.experimental import pallas as pl
from jax.experimental.pallas import tpu as pltpu
from jax.sharding import PartitionSpec as P

dispersion = 100.0
epsilon = 1e-05
TILE = 16
VMEM = 16 * 1024 * 1024

brief = pl.CostEstimate(flops=1024, bytes_accessed=1024, transcendentals=0)
lengthy = pl.CostEstimate(flops=2 * 10**10, bytes_accessed=1024, transcendentals=0)
whole = pl.BlockSpec(memory_space=pltpu.VMEM)
anywhere = pl.BlockSpec(memory_space=pl.ANY)


def pack_kernel(types, cap, widths, type_ref, factor_ref, expr_ref, *outs):
    rows = expr_ref.shape[0]
    home = lax.axis_index("cells")
    kind = type_ref[...].reshape(1, rows)
    rel = jnp.bitwise_xor(kind, home)
    lines = max(types, 8)
    hot = lax.broadcasted_iota(jnp.int32, (lines, rows), 0) == rel
    hot_f = jnp.where(hot, 1.0, 0.0)
    upper = jnp.where(
        lax.broadcasted_iota(jnp.int32, (rows, rows), 0)
        <= lax.broadcasted_iota(jnp.int32, (rows, rows), 1),
        1.0,
        0.0,
    ).astype(jnp.bfloat16)
    running = jnp.dot(hot_f.astype(jnp.bfloat16), upper, preferred_element_type=jnp.float32)
    rank = jnp.sum(hot_f * running, axis=0, keepdims=True) - 1.0
    slot = rel * cap + rank.astype(jnp.int32)
    factor = factor_ref[...].astype(jnp.float32).reshape(1, rows)
    factor = jnp.broadcast_to(factor, (TILE, rows)).astype(jnp.bfloat16)
    values = expr_ref[...]
    for j in range(types):
        place = jnp.where(
            lax.broadcasted_iota(jnp.int32, (cap, rows), 0) + j * cap == slot, 1.0, 0.0
        ).astype(jnp.bfloat16)
        block = jnp.dot(place, values, preferred_element_type=jnp.float32).astype(jnp.bfloat16)
        start = 0
        for k, width in enumerate(widths):
            outs[k * types + j][0:cap, :] = block[:, start : start + width]
            start += width
        line = lax.dot_general(
            factor, place, (((1,), (1,)), ((), ())), preferred_element_type=jnp.float32
        )
        row = lax.broadcasted_iota(jnp.int32, (TILE, 1), 0)
        width = widths[0]
        tail = jnp.zeros((TILE, min(width, cap)), jnp.float32)
        for i in range(pl.cdiv(cap, width)):
            tail = jnp.where(row == i, line[:, i * width : min((i + 1) * width, cap)], tail)
        outs[j][cap : cap + TILE, 0 : min(width, cap)] = tail.astype(jnp.bfloat16)


def pack(types, cap, widths, cell_type, size_factor, expression):
    rows = expression.shape[0]
    shapes = [
        jax.ShapeDtypeStruct((cap + (TILE if k == 0 else 0), width), jnp.bfloat16)
        for k, width in enumerate(widths)
        for _ in range(types)
    ]
    flat = pl.pallas_call(
        functools.partial(pack_kernel, types, cap, widths),
        out_shape=shapes,
        in_specs=[whole] * 3,
        out_specs=[whole] * len(shapes),
        compiler_params=pltpu.CompilerParams(vmem_limit_bytes=VMEM),
        cost_estimate=brief,
        name="pack",
    )(cell_type, size_factor, expression)
    return [flat[k * types : (k + 1) * types] for k in range(len(widths))]


def standardize_kernel(types, cap, lead, separate, chunk, mean_ref, *refs):
    blocks = refs[:types]
    tails = refs[types : 2 * types] if separate else blocks
    base = 0 if separate else cap
    refs = refs[2 * types :] if separate else refs[types:]
    scaled_ref, turned_ref, count_ref, all_ref, work, turned, sems = refs[-7:]
    width = work.shape[1]
    mean = mean_ref[:, chunk * width : (chunk + 1) * width]
    piece = min(lead, cap)
    total = jnp.zeros((1, width), jnp.float32)
    count = jnp.zeros((1, 1), jnp.float32)
    alive = []
    for j in range(types):
        column = jnp.zeros((cap, 1), jnp.float32)
        for i in range(pl.cdiv(cap, lead)):
            line = tails[j][base : base + TILE, 0:piece].astype(jnp.float32)[i : i + 1, :]
            diagonal = (
                lax.broadcasted_iota(jnp.int32, (cap, piece), 0)
                == lax.broadcasted_iota(jnp.int32, (cap, piece), 1) + i * lead
            )
            column += jnp.sum(jnp.where(diagonal, line, 0.0), axis=1, keepdims=True)
        live = column > 0.0
        alive.append(live)
        count += jnp.sum(jnp.where(live, 1.0, 0.0), axis=0, keepdims=True)
        expected = jnp.where(live, column * mean, 1.0)
        values = blocks[j][0:cap, :].astype(jnp.float32)
        residual = jnp.where(
            live,
            (values - expected) * lax.rsqrt(expected + expected * expected * (1.0 / dispersion)),
            0.0,
        )
        work[j * cap : (j + 1) * cap, :] = residual
        total += jnp.sum(residual, axis=0, keepdims=True)
    center = total / count
    square = jnp.zeros((1, width), jnp.float32)
    for j in range(types):
        centered = jnp.where(alive[j], work[j * cap : (j + 1) * cap, :] - center, 0.0)
        work[j * cap : (j + 1) * cap, :] = centered
        square += jnp.sum(centered * centered, axis=0, keepdims=True)
    scale = lax.rsqrt(square / count + epsilon)
    for j in range(types):
        scaled = work[j * cap : (j + 1) * cap, :] * scale
        scaled_ref[j * cap : (j + 1) * cap, :] = scaled.astype(jnp.bfloat16)
        work[j * cap : (j + 1) * cap, :] = scaled
    slots = types * cap
    columns = pl.ds(chunk * width, width)
    copies = [pltpu.make_async_copy(scaled_ref, all_ref.at[:, columns], sems.at[0])]
    copies[0].start()
    turned[...] = jnp.transpose(work[...]).astype(jnp.bfloat16)
    copies.append(pltpu.make_async_copy(turned, turned_ref.at[columns, :], sems.at[1]))
    copies[-1].start()
    for copy in copies:
        copy.wait()
    count_ref[...] = jnp.broadcast_to(count, count_ref.shape)


def standardize(types, cap, lead, width, mean, chunk, blocks, first, left, own):
    chunks = mean.shape[1] // width
    separate = first is not blocks
    slots = types * cap
    specs = [whole] * (1 + types)
    args = [mean, *blocks]
    if separate:
        specs += [pl.BlockSpec((TILE, lead), lambda i: (cap // TILE, 0))] * types
        args += list(first)
    shapes = [
        jax.ShapeDtypeStruct((slots, width), jnp.bfloat16),
        jax.ShapeDtypeStruct((chunks * width, slots), jnp.bfloat16),
        jax.ShapeDtypeStruct((8, 128), jnp.float32),
        jax.ShapeDtypeStruct((slots, chunks * width), jnp.bfloat16),
    ]
    aliases = {}
    for value, output in ((left, 1), (own, 3)):
        if value is not None:
            aliases[len(args)] = output
            specs.append(anywhere)
            args.append(value)
    return pl.pallas_call(
        functools.partial(standardize_kernel, types, cap, lead, separate, chunk),
        grid=(1,),
        out_shape=shapes,
        in_specs=specs,
        out_specs=[whole, anywhere, whole, anywhere],
        scratch_shapes=[
            pltpu.VMEM((slots, width), jnp.float32),
            pltpu.VMEM((width, slots), jnp.bfloat16),
            pltpu.SemaphoreType.DMA((2,)),
        ],
        input_output_aliases=aliases,
        compiler_params=pltpu.CompilerParams(vmem_limit_bytes=VMEM),
        cost_estimate=lengthy,
        name="standardize",
    )(*args)


def gram_kernel(blocks, cores, strip, groups, arrays, count_ref, left_ref, *refs):
    sources = refs[:arrays]
    out_ref, joined, tile, join_sems, sems = refs[-5:]
    rows, slots = left_ref.shape
    inverse = 1.0 / count_ref[0:1, 0:1]
    me = lax.axis_index("blk")

    joins, column = [], 0
    for panels, _ in groups:
        joins.append([])
        if len(panels) > 1:
            for index in panels:
                width = sources[index].shape[1]
                spot = joined.at[:, pl.ds(column, width)]
                joins[-1].append((column, sources[index], spot))
                column += width
    sent = 0
    for parts in joins:
        for _, source, spot in parts:
            pltpu.make_async_copy(source, spot, join_sems.at[sent]).start()
            sent += 1
    stores, sent = [], 0
    for (panels, (chip, flip, first)), parts in zip(groups, joins):
        for _, source, spot in parts:
            pltpu.make_async_copy(source, spot, join_sems.at[sent]).wait()
            sent += 1
        width = sum(sources[index].shape[1] for index in panels)
        owner = lax.rem(me + (blocks - chip * cores), blocks)
        owner = jnp.bitwise_xor(owner, flip)
        column = pl.multiple_of(owner * rows + first, 128)
        for row in range(0, rows, strip):
            slot = len(stores) % 2
            if len(stores) >= 2:
                stores[-2].wait()
            if parts:
                right = joined[:, parts[0][0] : parts[0][0] + width]
            else:
                right = sources[panels[0]][...]
            product = jnp.dot(
                left_ref[row : row + strip, :], right, preferred_element_type=jnp.float32
            )
            tile[slot, :, 0:width] = (product * inverse).astype(jnp.bfloat16)
            stores.append(
                pltpu.make_async_copy(
                    tile.at[slot, :, pl.ds(0, width)],
                    out_ref.at[0, pl.ds(row, strip), pl.ds(column, width)],
                    sems.at[slot],
                )
            )
            stores[-1].start()
    for store in stores[-2:]:
        store.wait()


def gram(blocks, cores, count, left, groups, before, cost):
    rows, slots = left.shape
    arrays, layout = [], []
    for panels, place in groups:
        layout.append((list(range(len(arrays), len(arrays) + len(panels))), place))
        arrays += panels
    joined = [array for panels, _ in groups if len(panels) > 1 for array in panels]
    widest = max(sum(array.shape[1] for array in panels) for panels, _ in groups)
    strip = min(rows, 256 if widest > 512 else 1024)
    args = [count, left, *arrays]
    specs = [whole] * len(args)
    if before is not None:
        args.append(before)
        specs.append(anywhere)
    return pl.pallas_call(
        functools.partial(gram_kernel, blocks, cores, strip, layout, len(arrays)),
        in_specs=specs,
        out_specs=anywhere,
        out_shape=jax.ShapeDtypeStruct((1, rows, rows * blocks), jnp.bfloat16),
        scratch_shapes=[
            pltpu.VMEM((slots, max(sum(array.shape[1] for array in joined), 128)), jnp.bfloat16),
            pltpu.VMEM((2, strip, widest), jnp.bfloat16),
            pltpu.SemaphoreType.DMA((max(len(joined), 1),)),
            pltpu.SemaphoreType.DMA((2,)),
        ],
        input_output_aliases={} if before is None else {len(args) - 1: 0},
        compiler_params=pltpu.CompilerParams(vmem_limit_bytes=VMEM),
        cost_estimate=cost,
        name="gram",
    )(*args)


def after(value, *others):
    return lax.optimization_barrier((value, *others))[0]


def shards(expression, cell_type, size_factor, gene_mean):
    types = lax.axis_size("cells")
    blocks = lax.axis_size("blk")
    shard_rows, panel = expression.shape
    cap = 2 * shard_rows // types
    assert types & (types - 1) == 0
    width = 256
    widths = [width] * (panel // width)
    chunks = len(widths)
    cores = 2
    chips = blocks // cores
    window = 3

    packed = pack(types, cap, widths, cell_type, size_factor, expression)

    def swap(block, by):
        return lax.ppermute(block, "cells", [(s, s ^ by) for s in range(types)])

    def across(panel_, by):
        return lax.ppermute(panel_, "blk", [(b, (b + by * cores) % blocks) for b in range(blocks)])

    def side(name, panel_, *waits):
        with jax.named_scope(name):
            return lax.ppermute(after(panel_, *waits), "blk", [(b, b ^ 1) for b in range(blocks)])

    mean = gene_mean.reshape(1, panel)
    order = sorted(range(1, types), key=lambda j: (j == 1, j))
    left, own, far, before = None, None, [], None
    for k in range(chunks):
        arrived = [packed[k][0]] + [None] * (types - 1)
        for j in order:
            block = packed[k][j]
            if k:
                block = after(block, before[j])
            with jax.named_scope(f"cells_{j}_chunk_{k}"):
                arrived[j] = swap(block, j)
        before = list(arrived)
        if k >= 2:
            arrived[0] = after(arrived[0], *far[k - 2])
        if k == 0:
            first = arrived
        scaled, left, count, own = standardize(
            types, cap, width, width, mean, k, arrived, first, left, own
        )
        with jax.named_scope(f"far_{k}"):
            far.append([across(scaled, d) for d in range(1, chips)])

    multiply = functools.partial(gram, blocks, cores, count, left)
    last = chunks - 1
    late = max(last - 1, 1)
    near = side("near", own)
    far_near = [[side(f"far_near_{k}", p, own) for p in far[k]] for k in range(late)]
    out = multiply([([own], (0, 0, 0))], None, brief)
    groups = [([far[k][d - 1] for k in range(last)], (d, 0, 0)) for d in range(1, chips)]
    out = multiply(groups, out, lengthy)
    groups = [([near], (0, 1, 0))]
    for d in range(1, chips):
        groups.append(([far_near[k][d - 1] for k in range(late)], (d, 1, 0)))
    out = multiply(groups, out, brief)
    far_near = [[side(f"far_near_{k}", p, out) for p in far[k]] for k in range(late, chunks)]
    edge = last * width
    out = multiply([([p], (d, 0, edge)) for d, p in enumerate(far[last], 1)], out, brief)
    edge = late * width
    groups = [([p[d - 1] for p in far_near], (d, 1, edge)) for d in range(1, chips)]
    return multiply(groups, out, brief)


def solution(mesh):
    placed = (
        P(("parts", "cells"), "blk"),
        P(("parts", "cells")),
        P(("parts", "cells")),
        P(("parts", "blk")),
    )
    return jax.shard_map(
        shards,
        mesh=mesh,
        in_specs=placed,
        out_specs=P(("parts", "cells"), "blk", None),
        check_vma=False,
    )
```

```python
import functools

import jax
import jax.numpy as jnp
from jax import lax
from jax.experimental import pallas as pl
from jax.experimental.pallas import tpu as pltpu
from jax.sharding import PartitionSpec as P

dispersion = 100.0
epsilon = 1e-05
TILE = 16
VMEM = 16 * 1024 * 1024

brief = pl.CostEstimate(flops=1024, bytes_accessed=1024, transcendentals=0)
lengthy = pl.CostEstimate(flops=2 * 10**10, bytes_accessed=1024, transcendentals=0)
whole = pl.BlockSpec(memory_space=pltpu.VMEM)
anywhere = pl.BlockSpec(memory_space=pl.ANY)


def pack_kernel(types, cap, widths, type_ref, factor_ref, expr_ref, *outs):
    rows = expr_ref.shape[0]
    home = lax.axis_index("cells")
    kind = type_ref[...].reshape(1, rows)
    rel = jnp.bitwise_xor(kind, home)
    lines = max(types, 8)
    hot = lax.broadcasted_iota(jnp.int32, (lines, rows), 0) == rel
    hot_f = jnp.where(hot, 1.0, 0.0)
    upper = jnp.where(
        lax.broadcasted_iota(jnp.int32, (rows, rows), 0)
        <= lax.broadcasted_iota(jnp.int32, (rows, rows), 1),
        1.0,
        0.0,
    ).astype(jnp.bfloat16)
    running = jnp.dot(hot_f.astype(jnp.bfloat16), upper, preferred_element_type=jnp.float32)
    rank = jnp.sum(hot_f * running, axis=0, keepdims=True) - 1.0
    slot = rel * cap + rank.astype(jnp.int32)
    factor = factor_ref[...].astype(jnp.float32).reshape(1, rows)
    factor = jnp.broadcast_to(factor, (TILE, rows)).astype(jnp.bfloat16)
    values = expr_ref[...]
    for j in range(types):
        place = jnp.where(
            lax.broadcasted_iota(jnp.int32, (cap, rows), 0) + j * cap == slot, 1.0, 0.0
        ).astype(jnp.bfloat16)
        block = jnp.dot(place, values, preferred_element_type=jnp.float32).astype(jnp.bfloat16)
        start = 0
        for k, width in enumerate(widths):
            outs[k * types + j][0:cap, :] = block[:, start : start + width]
            start += width
        line = lax.dot_general(
            factor, place, (((1,), (1,)), ((), ())), preferred_element_type=jnp.float32
        )
        row = lax.broadcasted_iota(jnp.int32, (TILE, 1), 0)
        width = widths[0]
        tail = jnp.zeros((TILE, min(width, cap)), jnp.float32)
        for i in range(pl.cdiv(cap, width)):
            tail = jnp.where(row == i, line[:, i * width : min((i + 1) * width, cap)], tail)
        outs[j][cap : cap + TILE, 0 : min(width, cap)] = tail.astype(jnp.bfloat16)


def pack(types, cap, widths, cell_type, size_factor, expression):
    rows = expression.shape[0]
    shapes = [
        jax.ShapeDtypeStruct((cap + (TILE if k == 0 else 0), width), jnp.bfloat16)
        for k, width in enumerate(widths)
        for _ in range(types)
    ]
    flat = pl.pallas_call(
        functools.partial(pack_kernel, types, cap, widths),
        out_shape=shapes,
        in_specs=[whole] * 3,
        out_specs=[whole] * len(shapes),
        compiler_params=pltpu.CompilerParams(vmem_limit_bytes=VMEM),
        cost_estimate=brief,
        name="pack",
    )(cell_type, size_factor, expression)
    return [flat[k * types : (k + 1) * types] for k in range(len(widths))]


def standardize_kernel(types, cap, lead, separate, chunk, mean_ref, *refs):
    blocks = refs[:types]
    tails = refs[types : 2 * types] if separate else blocks
    base = 0 if separate else cap
    refs = refs[2 * types :] if separate else refs[types:]
    scaled_ref, turned_ref, count_ref, all_ref, work, turned, sems = refs[-7:]
    width = work.shape[1]
    mean = mean_ref[:, chunk * width : (chunk + 1) * width]
    piece = min(lead, cap)
    total = jnp.zeros((1, width), jnp.float32)
    count = jnp.zeros((1, 1), jnp.float32)
    alive = []
    for j in range(types):
        column = jnp.zeros((cap, 1), jnp.float32)
        for i in range(pl.cdiv(cap, lead)):
            line = tails[j][base : base + TILE, 0:piece].astype(jnp.float32)[i : i + 1, :]
            diagonal = (
                lax.broadcasted_iota(jnp.int32, (cap, piece), 0)
                == lax.broadcasted_iota(jnp.int32, (cap, piece), 1) + i * lead
            )
            column += jnp.sum(jnp.where(diagonal, line, 0.0), axis=1, keepdims=True)
        live = column > 0.0
        alive.append(live)
        count += jnp.sum(jnp.where(live, 1.0, 0.0), axis=0, keepdims=True)
        expected = jnp.where(live, column * mean, 1.0)
        values = blocks[j][0:cap, :].astype(jnp.float32)
        residual = jnp.where(
            live,
            (values - expected) * lax.rsqrt(expected + expected * expected * (1.0 / dispersion)),
            0.0,
        )
        work[j * cap : (j + 1) * cap, :] = residual
        total += jnp.sum(residual, axis=0, keepdims=True)
    center = total / count
    square = jnp.zeros((1, width), jnp.float32)
    for j in range(types):
        centered = jnp.where(alive[j], work[j * cap : (j + 1) * cap, :] - center, 0.0)
        work[j * cap : (j + 1) * cap, :] = centered
        square += jnp.sum(centered * centered, axis=0, keepdims=True)
    scale = lax.rsqrt(square / count + epsilon)
    for j in range(types):
        scaled = work[j * cap : (j + 1) * cap, :] * scale
        scaled_ref[j * cap : (j + 1) * cap, :] = scaled.astype(jnp.bfloat16)
        work[j * cap : (j + 1) * cap, :] = scaled
    slots = types * cap
    columns = pl.ds(chunk * width, width)
    copies = [pltpu.make_async_copy(scaled_ref, all_ref.at[:, columns], sems.at[0])]
    copies[0].start()
    turned[...] = jnp.transpose(work[...]).astype(jnp.bfloat16)
    copies.append(pltpu.make_async_copy(turned, turned_ref.at[columns, :], sems.at[1]))
    copies[-1].start()
    for copy in copies:
        copy.wait()
    count_ref[...] = jnp.broadcast_to(count, count_ref.shape)


def standardize(types, cap, lead, width, mean, chunk, blocks, first, left, own):
    chunks = mean.shape[1] // width
    separate = first is not blocks
    slots = types * cap
    specs = [whole] * (1 + types)
    args = [mean, *blocks]
    if separate:
        specs += [pl.BlockSpec((TILE, lead), lambda i: (cap // TILE, 0))] * types
        args += list(first)
    shapes = [
        jax.ShapeDtypeStruct((slots, width), jnp.bfloat16),
        jax.ShapeDtypeStruct((chunks * width, slots), jnp.bfloat16),
        jax.ShapeDtypeStruct((8, 128), jnp.float32),
        jax.ShapeDtypeStruct((slots, chunks * width), jnp.bfloat16),
    ]
    aliases = {}
    for value, output in ((left, 1), (own, 3)):
        if value is not None:
            aliases[len(args)] = output
            specs.append(anywhere)
            args.append(value)
    return pl.pallas_call(
        functools.partial(standardize_kernel, types, cap, lead, separate, chunk),
        grid=(1,),
        out_shape=shapes,
        in_specs=specs,
        out_specs=[whole, anywhere, whole, anywhere],
        scratch_shapes=[
            pltpu.VMEM((slots, width), jnp.float32),
            pltpu.VMEM((width, slots), jnp.bfloat16),
            pltpu.SemaphoreType.DMA((2,)),
        ],
        input_output_aliases=aliases,
        compiler_params=pltpu.CompilerParams(vmem_limit_bytes=VMEM),
        cost_estimate=lengthy,
        name="standardize",
    )(*args)


def gram_kernel(blocks, cores, strip, groups, arrays, count_ref, left_ref, *refs):
    sources = refs[:arrays]
    out_ref, joined, tile, join_sems, sems = refs[-5:]
    rows, slots = left_ref.shape
    inverse = 1.0 / count_ref[0:1, 0:1]
    me = lax.axis_index("blk")

    joins, column = [], 0
    for panels, _ in groups:
        joins.append([])
        if len(panels) > 1:
            for index in panels:
                width = sources[index].shape[1]
                spot = joined.at[:, pl.ds(column, width)]
                joins[-1].append((column, sources[index], spot))
                column += width
    sent = 0
    for parts in joins:
        for _, source, spot in parts:
            pltpu.make_async_copy(source, spot, join_sems.at[sent]).start()
            sent += 1
    stores, sent = [], 0
    for (panels, (chip, flip, first)), parts in zip(groups, joins):
        for _, source, spot in parts:
            pltpu.make_async_copy(source, spot, join_sems.at[sent]).wait()
            sent += 1
        width = sum(sources[index].shape[1] for index in panels)
        owner = lax.rem(me + (blocks - chip * cores), blocks)
        owner = jnp.bitwise_xor(owner, flip)
        column = pl.multiple_of(owner * rows + first, 128)
        for row in range(0, rows, strip):
            slot = len(stores) % 2
            if len(stores) >= 2:
                stores[-2].wait()
            if parts:
                right = joined[:, parts[0][0] : parts[0][0] + width]
            else:
                right = sources[panels[0]][...]
            product = jnp.dot(
                left_ref[row : row + strip, :], right, preferred_element_type=jnp.float32
            )
            tile[slot, :, 0:width] = (product * inverse).astype(jnp.bfloat16)
            stores.append(
                pltpu.make_async_copy(
                    tile.at[slot, :, pl.ds(0, width)],
                    out_ref.at[0, pl.ds(row, strip), pl.ds(column, width)],
                    sems.at[slot],
                )
            )
            stores[-1].start()
    for store in stores[-2:]:
        store.wait()


def gram(blocks, cores, count, left, groups, before, cost):
    rows, slots = left.shape
    arrays, layout = [], []
    for panels, place in groups:
        layout.append((list(range(len(arrays), len(arrays) + len(panels))), place))
        arrays += panels
    joined = [array for panels, _ in groups if len(panels) > 1 for array in panels]
    widest = max(sum(array.shape[1] for array in panels) for panels, _ in groups)
    strip = min(rows, 512 if widest > 512 else 1024)
    args = [count, left, *arrays]
    specs = [whole] * len(args)
    if before is not None:
        args.append(before)
        specs.append(anywhere)
    return pl.pallas_call(
        functools.partial(gram_kernel, blocks, cores, strip, layout, len(arrays)),
        in_specs=specs,
        out_specs=anywhere,
        out_shape=jax.ShapeDtypeStruct((1, rows, rows * blocks), jnp.bfloat16),
        scratch_shapes=[
            pltpu.VMEM((slots, max(sum(array.shape[1] for array in joined), 128)), jnp.bfloat16),
            pltpu.VMEM((2, strip, widest), jnp.bfloat16),
            pltpu.SemaphoreType.DMA((max(len(joined), 1),)),
            pltpu.SemaphoreType.DMA((2,)),
        ],
        input_output_aliases={} if before is None else {len(args) - 1: 0},
        compiler_params=pltpu.CompilerParams(vmem_limit_bytes=VMEM),
        cost_estimate=cost,
        name="gram",
    )(*args)


def after(value, *others):
    return lax.optimization_barrier((value, *others))[0]


def shards(expression, cell_type, size_factor, gene_mean):
    types = lax.axis_size("cells")
    blocks = lax.axis_size("blk")
    shard_rows, panel = expression.shape
    cap = 2 * shard_rows // types
    assert types & (types - 1) == 0
    width = 256
    widths = [width] * (panel // width)
    chunks = len(widths)
    cores = 2
    chips = blocks // cores
    window = 3

    packed = pack(types, cap, widths, cell_type, size_factor, expression)

    def swap(block, by):
        return lax.ppermute(block, "cells", [(s, s ^ by) for s in range(types)])

    def across(panel_, by):
        return lax.ppermute(panel_, "blk", [(b, (b + by * cores) % blocks) for b in range(blocks)])

    def side(name, panel_, *waits):
        with jax.named_scope(name):
            return lax.ppermute(after(panel_, *waits), "blk", [(b, b ^ 1) for b in range(blocks)])

    mean = gene_mean.reshape(1, panel)
    order = sorted(range(1, types), key=lambda j: (j == 2, j == 1, -j))
    left, own, far, before = None, None, [], None
    for k in range(chunks):
        arrived = [packed[k][0]]
        for j in order:
            block = packed[k][j]
            if k:
                block = after(block, before[len(arrived)])
            with jax.named_scope(f"cells_{j}_chunk_{k}"):
                arrived.append(swap(block, j))
        before = list(arrived)
        if k >= 2:
            arrived[0] = after(arrived[0], *far[k - 2])
        if k == 0:
            first = arrived
        scaled, left, count, own = standardize(
            types, cap, width, width, mean, k, arrived, first, left, own
        )
        with jax.named_scope(f"far_{k}"):
            far.append([across(scaled, d) for d in range(1, chips)])

    multiply = functools.partial(gram, blocks, cores, count, left)
    last = chunks - 1
    late = max(last - 1, 1)
    near = side("near", own)
    far_near = [[side(f"far_near_{k}", p, own) for p in far[k]] for k in range(late)]
    out = multiply([([own], (0, 0, 0))], None, brief)
    groups = [([far[k][d - 1] for k in range(last)], (d, 0, 0)) for d in range(1, chips)]
    out = multiply(groups, out, lengthy)
    groups = [([near], (0, 1, 0))]
    for d in range(1, chips):
        groups.append(([far_near[k][d - 1] for k in range(late)], (d, 1, 0)))
    out = multiply(groups, out, brief)
    far_near = [[side(f"far_near_{k}", p, out) for p in far[k]] for k in range(late, chunks)]
    edge = last * width
    out = multiply([([p], (d, 0, edge)) for d, p in enumerate(far[last], 1)], out, brief)
    edge = late * width
    groups = [([p[d - 1] for p in far_near], (d, 1, edge)) for d in range(1, chips)]
    return multiply(groups, out, brief)


def solution(mesh):
    placed = (
        P(("parts", "cells"), "blk"),
        P(("parts", "cells")),
        P(("parts", "cells")),
        P(("parts", "blk")),
    )
    return jax.shard_map(
        shards,
        mesh=mesh,
        in_specs=placed,
        out_specs=P(("parts", "cells"), "blk", None),
        check_vma=False,
    )
```

```python
import functools

import jax
import jax.numpy as jnp
from jax import lax
from jax.experimental import pallas as pl
from jax.experimental.pallas import tpu as pltpu
from jax.sharding import PartitionSpec as P

dispersion = 100.0
epsilon = 1e-05
TILE = 16
VMEM = 16 * 1024 * 1024

brief = pl.CostEstimate(flops=1024, bytes_accessed=1024, transcendentals=0)
lengthy = pl.CostEstimate(flops=2 * 10**10, bytes_accessed=1024, transcendentals=0)
whole = pl.BlockSpec(memory_space=pltpu.VMEM)
anywhere = pl.BlockSpec(memory_space=pl.ANY)


def pack_kernel(types, cap, widths, type_ref, factor_ref, expr_ref, *outs):
    rows = expr_ref.shape[0]
    home = lax.axis_index("cells")
    kind = type_ref[...].reshape(1, rows)
    rel = jnp.bitwise_xor(kind, home)
    lines = max(types, 8)
    hot = lax.broadcasted_iota(jnp.int32, (lines, rows), 0) == rel
    hot_f = jnp.where(hot, 1.0, 0.0)
    upper = jnp.where(
        lax.broadcasted_iota(jnp.int32, (rows, rows), 0)
        <= lax.broadcasted_iota(jnp.int32, (rows, rows), 1),
        1.0,
        0.0,
    ).astype(jnp.bfloat16)
    running = jnp.dot(hot_f.astype(jnp.bfloat16), upper, preferred_element_type=jnp.float32)
    rank = jnp.sum(hot_f * running, axis=0, keepdims=True) - 1.0
    slot = rel * cap + rank.astype(jnp.int32)
    factor = factor_ref[...].astype(jnp.float32).reshape(1, rows)
    factor = jnp.broadcast_to(factor, (TILE, rows)).astype(jnp.bfloat16)
    values = expr_ref[...]
    for j in range(types):
        place = jnp.where(
            lax.broadcasted_iota(jnp.int32, (cap, rows), 0) + j * cap == slot, 1.0, 0.0
        ).astype(jnp.bfloat16)
        block = jnp.dot(place, values, preferred_element_type=jnp.float32).astype(jnp.bfloat16)
        start = 0
        for k, width in enumerate(widths):
            outs[k * types + j][0:cap, :] = block[:, start : start + width]
            start += width
        line = lax.dot_general(
            factor, place, (((1,), (1,)), ((), ())), preferred_element_type=jnp.float32
        )
        row = lax.broadcasted_iota(jnp.int32, (TILE, 1), 0)
        width = widths[0]
        tail = jnp.zeros((TILE, min(width, cap)), jnp.float32)
        for i in range(pl.cdiv(cap, width)):
            tail = jnp.where(row == i, line[:, i * width : min((i + 1) * width, cap)], tail)
        outs[j][cap : cap + TILE, 0 : min(width, cap)] = tail.astype(jnp.bfloat16)


def pack(types, cap, widths, cell_type, size_factor, expression):
    rows = expression.shape[0]
    shapes = [
        jax.ShapeDtypeStruct((cap + (TILE if k == 0 else 0), width), jnp.bfloat16)
        for k, width in enumerate(widths)
        for _ in range(types)
    ]
    flat = pl.pallas_call(
        functools.partial(pack_kernel, types, cap, widths),
        out_shape=shapes,
        in_specs=[whole] * 3,
        out_specs=[whole] * len(shapes),
        compiler_params=pltpu.CompilerParams(vmem_limit_bytes=VMEM),
        cost_estimate=brief,
        name="pack",
    )(cell_type, size_factor, expression)
    return [flat[k * types : (k + 1) * types] for k in range(len(widths))]


def standardize_kernel(types, cap, lead, separate, chunk, mean_ref, *refs):
    blocks = refs[:types]
    tails = refs[types : 2 * types] if separate else blocks
    base = 0 if separate else cap
    refs = refs[2 * types :] if separate else refs[types:]
    scaled_ref, turned_ref, count_ref, all_ref, work, turned, sems = refs[-7:]
    width = work.shape[1]
    mean = mean_ref[:, chunk * width : (chunk + 1) * width]
    piece = min(lead, cap)
    total = jnp.zeros((1, width), jnp.float32)
    count = jnp.zeros((1, 1), jnp.float32)
    alive = []
    for j in range(types):
        column = jnp.zeros((cap, 1), jnp.float32)
        for i in range(pl.cdiv(cap, lead)):
            line = tails[j][base : base + TILE, 0:piece].astype(jnp.float32)[i : i + 1, :]
            diagonal = (
                lax.broadcasted_iota(jnp.int32, (cap, piece), 0)
                == lax.broadcasted_iota(jnp.int32, (cap, piece), 1) + i * lead
            )
            column += jnp.sum(jnp.where(diagonal, line, 0.0), axis=1, keepdims=True)
        live = column > 0.0
        alive.append(live)
        count += jnp.sum(jnp.where(live, 1.0, 0.0), axis=0, keepdims=True)
        expected = jnp.where(live, column * mean, 1.0)
        values = blocks[j][0:cap, :].astype(jnp.float32)
        residual = jnp.where(
            live,
            (values - expected) * lax.rsqrt(expected + expected * expected * (1.0 / dispersion)),
            0.0,
        )
        work[j * cap : (j + 1) * cap, :] = residual
        total += jnp.sum(residual, axis=0, keepdims=True)
    center = total / count
    square = jnp.zeros((1, width), jnp.float32)
    for j in range(types):
        centered = jnp.where(alive[j], work[j * cap : (j + 1) * cap, :] - center, 0.0)
        work[j * cap : (j + 1) * cap, :] = centered
        square += jnp.sum(centered * centered, axis=0, keepdims=True)
    scale = lax.rsqrt(square / count + epsilon)
    for j in range(types):
        scaled = work[j * cap : (j + 1) * cap, :] * scale
        scaled_ref[j * cap : (j + 1) * cap, :] = scaled.astype(jnp.bfloat16)
        work[j * cap : (j + 1) * cap, :] = scaled
    slots = types * cap
    columns = pl.ds(chunk * width, width)
    copies = [pltpu.make_async_copy(scaled_ref, all_ref.at[:, columns], sems.at[0])]
    copies[0].start()
    turned[...] = jnp.transpose(work[...]).astype(jnp.bfloat16)
    copies.append(pltpu.make_async_copy(turned, turned_ref.at[columns, :], sems.at[1]))
    copies[-1].start()
    for copy in copies:
        copy.wait()
    count_ref[...] = jnp.broadcast_to(count, count_ref.shape)


def standardize(types, cap, lead, width, mean, chunk, blocks, first, left, own):
    chunks = mean.shape[1] // width
    separate = first is not blocks
    slots = types * cap
    specs = [whole] * (1 + types)
    args = [mean, *blocks]
    if separate:
        specs += [pl.BlockSpec((TILE, lead), lambda i: (cap // TILE, 0))] * types
        args += list(first)
    shapes = [
        jax.ShapeDtypeStruct((slots, width), jnp.bfloat16),
        jax.ShapeDtypeStruct((chunks * width, slots), jnp.bfloat16),
        jax.ShapeDtypeStruct((8, 128), jnp.float32),
        jax.ShapeDtypeStruct((slots, chunks * width), jnp.bfloat16),
    ]
    aliases = {}
    for value, output in ((left, 1), (own, 3)):
        if value is not None:
            aliases[len(args)] = output
            specs.append(anywhere)
            args.append(value)
    return pl.pallas_call(
        functools.partial(standardize_kernel, types, cap, lead, separate, chunk),
        grid=(1,),
        out_shape=shapes,
        in_specs=specs,
        out_specs=[whole, anywhere, whole, anywhere],
        scratch_shapes=[
            pltpu.VMEM((slots, width), jnp.float32),
            pltpu.VMEM((width, slots), jnp.bfloat16),
            pltpu.SemaphoreType.DMA((2,)),
        ],
        input_output_aliases=aliases,
        compiler_params=pltpu.CompilerParams(vmem_limit_bytes=VMEM),
        cost_estimate=lengthy,
        name="standardize",
    )(*args)


def gram_kernel(blocks, cores, strip, groups, arrays, count_ref, left_ref, *refs):
    sources = refs[:arrays]
    out_ref, joined, tile, join_sems, sems = refs[-5:]
    rows, slots = left_ref.shape
    inverse = 1.0 / count_ref[0:1, 0:1]
    me = lax.axis_index("blk")

    joins, column = [], 0
    for panels, _ in groups:
        joins.append([])
        if len(panels) > 1:
            for index in panels:
                width = sources[index].shape[1]
                spot = joined.at[:, pl.ds(column, width)]
                joins[-1].append((column, sources[index], spot))
                column += width
    sent = 0
    for parts in joins:
        for _, source, spot in parts:
            pltpu.make_async_copy(source, spot, join_sems.at[sent]).start()
            sent += 1
    stores, sent = [], 0
    for (panels, (chip, flip, first)), parts in zip(groups, joins):
        for _, source, spot in parts:
            pltpu.make_async_copy(source, spot, join_sems.at[sent]).wait()
            sent += 1
        width = sum(sources[index].shape[1] for index in panels)
        owner = lax.rem(me + (blocks - chip * cores), blocks)
        owner = jnp.bitwise_xor(owner, flip)
        column = pl.multiple_of(owner * rows + first, 128)
        for row in range(0, rows, strip):
            slot = len(stores) % 2
            if len(stores) >= 2:
                stores[-2].wait()
            if parts:
                right = joined[:, parts[0][0] : parts[0][0] + width]
            else:
                right = sources[panels[0]][...]
            product = jnp.dot(
                left_ref[row : row + strip, :], right, preferred_element_type=jnp.float32
            )
            tile[slot, :, 0:width] = (product * inverse).astype(jnp.bfloat16)
            stores.append(
                pltpu.make_async_copy(
                    tile.at[slot, :, pl.ds(0, width)],
                    out_ref.at[0, pl.ds(row, strip), pl.ds(column, width)],
                    sems.at[slot],
                )
            )
            stores[-1].start()
    for store in stores[-2:]:
        store.wait()


def gram(blocks, cores, count, left, groups, before, cost):
    rows, slots = left.shape
    arrays, layout = [], []
    for panels, place in groups:
        layout.append((list(range(len(arrays), len(arrays) + len(panels))), place))
        arrays += panels
    joined = [array for panels, _ in groups if len(panels) > 1 for array in panels]
    widest = max(sum(array.shape[1] for array in panels) for panels, _ in groups)
    strip = min(rows, 512 if widest > 512 else 1024)
    args = [count, left, *arrays]
    specs = [whole] * len(args)
    if before is not None:
        args.append(before)
        specs.append(anywhere)
    return pl.pallas_call(
        functools.partial(gram_kernel, blocks, cores, strip, layout, len(arrays)),
        in_specs=specs,
        out_specs=anywhere,
        out_shape=jax.ShapeDtypeStruct((1, rows, rows * blocks), jnp.bfloat16),
        scratch_shapes=[
            pltpu.VMEM((slots, max(sum(array.shape[1] for array in joined), 128)), jnp.bfloat16),
            pltpu.VMEM((2, strip, widest), jnp.bfloat16),
            pltpu.SemaphoreType.DMA((max(len(joined), 1),)),
            pltpu.SemaphoreType.DMA((2,)),
        ],
        input_output_aliases={} if before is None else {len(args) - 1: 0},
        compiler_params=pltpu.CompilerParams(vmem_limit_bytes=VMEM),
        cost_estimate=cost,
        name="gram",
    )(*args)


def after(value, *others):
    return lax.optimization_barrier((value, *others))[0]


def shards(expression, cell_type, size_factor, gene_mean):
    types = lax.axis_size("cells")
    blocks = lax.axis_size("blk")
    shard_rows, panel = expression.shape
    cap = 2 * shard_rows // types
    assert types & (types - 1) == 0
    width = 256
    widths = [width] * (panel // width)
    chunks = len(widths)
    cores = 2
    chips = blocks // cores
    window = 3

    packed = pack(types, cap, widths, cell_type, size_factor, expression)

    def swap(block, by):
        return lax.ppermute(block, "cells", [(s, s ^ by) for s in range(types)])

    def across(panel_, by):
        return lax.ppermute(panel_, "blk", [(b, (b + by * cores) % blocks) for b in range(blocks)])

    def side(name, panel_, *waits):
        with jax.named_scope(name):
            return lax.ppermute(after(panel_, *waits), "blk", [(b, b ^ 1) for b in range(blocks)])

    mean = gene_mean.reshape(1, panel)
    order = sorted(range(1, types), key=lambda j: (j == 2, j == 1, -j))
    left, own, far, before = None, None, [], None
    for k in range(chunks):
        arrived = [packed[k][0]]
        for j in order:
            block = packed[k][j]
            if k:
                block = after(block, before[len(arrived)], *(crossing if k == 1 and j > 1 else []))
            with jax.named_scope(f"cells_{j}_chunk_{k}"):
                arrived.append(swap(block, j))
        before = list(arrived)
        crossing = [got for got, j in zip(arrived[1:], order) if j > 1]
        if k >= 2:
            arrived[0] = after(arrived[0], *far[k - 2])
        if k == 0:
            first = arrived
        scaled, left, count, own = standardize(
            types, cap, width, width, mean, k, arrived, first, left, own
        )
        with jax.named_scope(f"far_{k}"):
            far.append([across(scaled, d) for d in range(1, chips)])

    multiply = functools.partial(gram, blocks, cores, count, left)
    last = chunks - 1
    late = max(last - 1, 1)
    near = side("near", own)
    far_near = [[side(f"far_near_{k}", p, own) for p in far[k]] for k in range(late)]
    out = multiply([([own], (0, 0, 0))], None, brief)
    groups = [([far[k][d - 1] for k in range(last)], (d, 0, 0)) for d in range(1, chips)]
    out = multiply(groups, out, lengthy)
    groups = [([near], (0, 1, 0))]
    for d in range(1, chips):
        groups.append(([far_near[k][d - 1] for k in range(late)], (d, 1, 0)))
    out = multiply(groups, out, brief)
    far_near = [[side(f"far_near_{k}", p, out) for p in far[k]] for k in range(late, chunks)]
    edge = last * width
    out = multiply([([p], (d, 0, edge)) for d, p in enumerate(far[last], 1)], out, brief)
    edge = late * width
    groups = [([p[d - 1] for p in far_near], (d, 1, edge)) for d in range(1, chips)]
    return multiply(groups, out, brief)


def solution(mesh):
    placed = (
        P(("parts", "cells"), "blk"),
        P(("parts", "cells")),
        P(("parts", "cells")),
        P(("parts", "blk")),
    )
    return jax.shard_map(
        shards,
        mesh=mesh,
        in_specs=placed,
        out_specs=P(("parts", "cells"), "blk", None),
        check_vma=False,
    )
```

```python
import functools

import jax
import jax.numpy as jnp
from jax import lax
from jax.experimental import pallas as pl
from jax.experimental.pallas import tpu as pltpu
from jax.sharding import PartitionSpec as P

dispersion = 100.0
epsilon = 1e-05
TILE = 16
VMEM = 16 * 1024 * 1024

brief = pl.CostEstimate(flops=1024, bytes_accessed=1024, transcendentals=0)
lengthy = pl.CostEstimate(flops=2 * 10**10, bytes_accessed=1024, transcendentals=0)
whole = pl.BlockSpec(memory_space=pltpu.VMEM)
anywhere = pl.BlockSpec(memory_space=pl.ANY)


def pack_kernel(types, cap, widths, type_ref, factor_ref, expr_ref, *outs):
    rows = expr_ref.shape[0]
    home = lax.axis_index("cells")
    kind = type_ref[...].reshape(1, rows)
    rel = jnp.bitwise_xor(kind, home)
    lines = max(types, 8)
    hot = lax.broadcasted_iota(jnp.int32, (lines, rows), 0) == rel
    hot_f = jnp.where(hot, 1.0, 0.0)
    upper = jnp.where(
        lax.broadcasted_iota(jnp.int32, (rows, rows), 0)
        <= lax.broadcasted_iota(jnp.int32, (rows, rows), 1),
        1.0,
        0.0,
    ).astype(jnp.bfloat16)
    running = jnp.dot(hot_f.astype(jnp.bfloat16), upper, preferred_element_type=jnp.float32)
    rank = jnp.sum(hot_f * running, axis=0, keepdims=True) - 1.0
    slot = rel * cap + rank.astype(jnp.int32)
    factor = factor_ref[...].astype(jnp.float32).reshape(1, rows)
    factor = jnp.broadcast_to(factor, (TILE, rows)).astype(jnp.bfloat16)
    values = expr_ref[...]
    for j in range(types):
        place = jnp.where(
            lax.broadcasted_iota(jnp.int32, (cap, rows), 0) + j * cap == slot, 1.0, 0.0
        ).astype(jnp.bfloat16)
        block = jnp.dot(place, values, preferred_element_type=jnp.float32).astype(jnp.bfloat16)
        start = 0
        for k, width in enumerate(widths):
            outs[k * types + j][0:cap, :] = block[:, start : start + width]
            start += width
        line = lax.dot_general(
            factor, place, (((1,), (1,)), ((), ())), preferred_element_type=jnp.float32
        )
        row = lax.broadcasted_iota(jnp.int32, (TILE, 1), 0)
        width = widths[0]
        tail = jnp.zeros((TILE, min(width, cap)), jnp.float32)
        for i in range(pl.cdiv(cap, width)):
            tail = jnp.where(row == i, line[:, i * width : min((i + 1) * width, cap)], tail)
        outs[j][cap : cap + TILE, 0 : min(width, cap)] = tail.astype(jnp.bfloat16)


def pack(types, cap, widths, cell_type, size_factor, expression):
    rows = expression.shape[0]
    shapes = [
        jax.ShapeDtypeStruct((cap + (TILE if k == 0 else 0), width), jnp.bfloat16)
        for k, width in enumerate(widths)
        for _ in range(types)
    ]
    flat = pl.pallas_call(
        functools.partial(pack_kernel, types, cap, widths),
        out_shape=shapes,
        in_specs=[whole] * 3,
        out_specs=[whole] * len(shapes),
        compiler_params=pltpu.CompilerParams(vmem_limit_bytes=VMEM),
        cost_estimate=brief,
        name="pack",
    )(cell_type, size_factor, expression)
    return [flat[k * types : (k + 1) * types] for k in range(len(widths))]


def standardize_kernel(types, cap, lead, separate, start, gathered, mean_ref, *refs):
    blocks = refs[:types]
    tails = refs[types : 2 * types] if separate else blocks
    base = 0 if separate else cap
    refs = refs[2 * types :] if separate else refs[types:]
    work, turned, sems = refs[-3:]
    if gathered:
        scaled_ref, turned_ref, count_ref, all_ref, *joined_refs = refs[-7 - gathered[0] : -3]
    else:
        scaled_ref, turned_ref, count_ref, all_ref = refs[-7:-3]
        joined_refs = []
    copies = []
    if gathered:
        sources = refs[: len(gathered[1])]
        for source, (joined, column) in zip(sources, gathered[1]):
            spot = joined_refs[joined].at[:, pl.ds(column, source.shape[1])]
            copies.append(pltpu.make_async_copy(source, spot, sems.at[2 + len(copies)]))
            copies[-1].start()
    width = work.shape[1]
    mean = mean_ref[:, start : start + width]
    piece = min(lead, cap)
    total = jnp.zeros((1, width), jnp.float32)
    count = jnp.zeros((1, 1), jnp.float32)
    alive = []
    for j in range(types):
        column = jnp.zeros((cap, 1), jnp.float32)
        for i in range(pl.cdiv(cap, lead)):
            line = tails[j][base : base + TILE, 0:piece].astype(jnp.float32)[i : i + 1, :]
            diagonal = (
                lax.broadcasted_iota(jnp.int32, (cap, piece), 0)
                == lax.broadcasted_iota(jnp.int32, (cap, piece), 1) + i * lead
            )
            column += jnp.sum(jnp.where(diagonal, line, 0.0), axis=1, keepdims=True)
        live = column > 0.0
        alive.append(live)
        count += jnp.sum(jnp.where(live, 1.0, 0.0), axis=0, keepdims=True)
        expected = jnp.where(live, column * mean, 1.0)
        values = blocks[j][0:cap, :].astype(jnp.float32)
        residual = jnp.where(
            live,
            (values - expected) * lax.rsqrt(expected + expected * expected * (1.0 / dispersion)),
            0.0,
        )
        work[j * cap : (j + 1) * cap, :] = residual
        total += jnp.sum(residual, axis=0, keepdims=True)
    center = total / count
    square = jnp.zeros((1, width), jnp.float32)
    for j in range(types):
        centered = jnp.where(alive[j], work[j * cap : (j + 1) * cap, :] - center, 0.0)
        work[j * cap : (j + 1) * cap, :] = centered
        square += jnp.sum(centered * centered, axis=0, keepdims=True)
    scale = lax.rsqrt(square / count + epsilon)
    for j in range(types):
        scaled = work[j * cap : (j + 1) * cap, :] * scale
        scaled_ref[j * cap : (j + 1) * cap, :] = scaled.astype(jnp.bfloat16)
        work[j * cap : (j + 1) * cap, :] = scaled
    slots = types * cap
    columns = pl.ds(start, width)
    copies.append(pltpu.make_async_copy(scaled_ref, all_ref.at[:, columns], sems.at[0]))
    copies[-1].start()
    turned[...] = jnp.transpose(work[...]).astype(jnp.bfloat16)
    copies.append(pltpu.make_async_copy(turned, turned_ref.at[columns, :], sems.at[1]))
    copies[-1].start()
    for copy in copies:
        copy.wait()
    count_ref[...] = jnp.broadcast_to(count, count_ref.shape)


def standardize(types, cap, mean, start, blocks, first, left, own, gather):
    lead, width = first[0].shape[1], blocks[0].shape[1]
    panel = mean.shape[1]
    separate = first is not blocks
    slots = types * cap
    specs = [whole] * (1 + types)
    args = [mean, *blocks]
    if separate:
        specs += [pl.BlockSpec((TILE, lead), lambda i: (cap // TILE, 0))] * types
        args += list(first)
    gathered, shapes = [], []
    for i, panels in enumerate(gather):
        column = 0
        for array in panels:
            gathered.append((i, column))
            column += array.shape[1]
            specs.append(whole)
            args.append(array)
        shapes.append(jax.ShapeDtypeStruct((slots, column), jnp.bfloat16))
    aliases = {}
    for value, output in ((left, 1), (own, 3)):
        if value is not None:
            aliases[len(args)] = output
            specs.append(anywhere)
            args.append(value)
    return pl.pallas_call(
        functools.partial(
            standardize_kernel,
            types,
            cap,
            lead,
            separate,
            start,
            (len(gather), gathered) if gathered else None,
        ),
        grid=(1,),
        out_shape=[
            jax.ShapeDtypeStruct((slots, width), jnp.bfloat16),
            jax.ShapeDtypeStruct((panel, slots), jnp.bfloat16),
            jax.ShapeDtypeStruct((8, 128), jnp.float32),
            jax.ShapeDtypeStruct((slots, panel), jnp.bfloat16),
            *shapes,
        ],
        in_specs=specs,
        out_specs=[whole, anywhere, whole, anywhere] + [whole] * len(shapes),
        scratch_shapes=[
            pltpu.VMEM((slots, width), jnp.float32),
            pltpu.VMEM((width, slots), jnp.bfloat16),
            pltpu.SemaphoreType.DMA((2 + len(gathered),)),
        ],
        input_output_aliases=aliases,
        compiler_params=pltpu.CompilerParams(vmem_limit_bytes=VMEM),
        cost_estimate=lengthy,
        name="standardize",
    )(*args)


def gram_kernel(blocks, cores, strip, groups, arrays, count_ref, left_ref, *refs):
    sources = refs[:arrays]
    out_ref, joined, tile, join_sems, sems = refs[-5:]
    rows, slots = left_ref.shape
    inverse = 1.0 / count_ref[0:1, 0:1]
    me = lax.axis_index("blk")

    joins, column = [], 0
    for panels, _ in groups:
        joins.append([])
        if len(panels) > 1:
            for index in panels:
                width = sources[index].shape[1]
                spot = joined.at[:, pl.ds(column, width)]
                joins[-1].append((column, sources[index], spot))
                column += width
    sent = 0
    for parts in joins:
        for _, source, spot in parts:
            pltpu.make_async_copy(source, spot, join_sems.at[sent]).start()
            sent += 1
    stores, sent = [], 0
    for (panels, (chip, flip, first)), parts in zip(groups, joins):
        for _, source, spot in parts:
            pltpu.make_async_copy(source, spot, join_sems.at[sent]).wait()
            sent += 1
        width = sum(sources[index].shape[1] for index in panels)
        owner = lax.rem(me + (blocks - chip * cores), blocks)
        owner = jnp.bitwise_xor(owner, flip)
        column = pl.multiple_of(owner * rows + first, 128)
        for row in range(0, rows, strip):
            slot = len(stores) % 2
            if len(stores) >= 2:
                stores[-2].wait()
            if parts:
                right = joined[:, parts[0][0] : parts[0][0] + width]
            else:
                right = sources[panels[0]][...]
            product = jnp.dot(
                left_ref[row : row + strip, :], right, preferred_element_type=jnp.float32
            )
            tile[slot, :, 0:width] = (product * inverse).astype(jnp.bfloat16)
            stores.append(
                pltpu.make_async_copy(
                    tile.at[slot, :, pl.ds(0, width)],
                    out_ref.at[0, pl.ds(row, strip), pl.ds(column, width)],
                    sems.at[slot],
                )
            )
            stores[-1].start()
    for store in stores[-2:]:
        store.wait()


def gram(blocks, cores, count, left, groups, before, cost):
    rows, slots = left.shape
    arrays, layout = [], []
    for panels, place in groups:
        layout.append((list(range(len(arrays), len(arrays) + len(panels))), place))
        arrays += panels
    joined = [array for panels, _ in groups if len(panels) > 1 for array in panels]
    widest = max(sum(array.shape[1] for array in panels) for panels, _ in groups)
    strip = min(rows, 512 if widest > 512 else 1024)
    args = [count, left, *arrays]
    specs = [whole] * len(args)
    if before is not None:
        args.append(before)
        specs.append(anywhere)
    return pl.pallas_call(
        functools.partial(gram_kernel, blocks, cores, strip, layout, len(arrays)),
        in_specs=specs,
        out_specs=anywhere,
        out_shape=jax.ShapeDtypeStruct((1, rows, rows * blocks), jnp.bfloat16),
        scratch_shapes=[
            pltpu.VMEM((slots, max(sum(array.shape[1] for array in joined), 128)), jnp.bfloat16),
            pltpu.VMEM((2, strip, widest), jnp.bfloat16),
            pltpu.SemaphoreType.DMA((max(len(joined), 1),)),
            pltpu.SemaphoreType.DMA((2,)),
        ],
        input_output_aliases={} if before is None else {len(args) - 1: 0},
        compiler_params=pltpu.CompilerParams(vmem_limit_bytes=VMEM),
        cost_estimate=cost,
        name="gram",
    )(*args)


def after(value, *others):
    return lax.optimization_barrier((value, *others))[0]


def shards(expression, cell_type, size_factor, gene_mean):
    types = lax.axis_size("cells")
    blocks = lax.axis_size("blk")
    shard_rows, panel = expression.shape
    cap = 2 * shard_rows // types
    assert types & (types - 1) == 0
    widths = [128] + [256] * (panel // 256 - 1) + [128]
    chunks = len(widths)
    starts = [sum(widths[:k]) for k in range(chunks)]
    cores = 2
    chips = blocks // cores
    window = 3

    packed = pack(types, cap, widths, cell_type, size_factor, expression)

    def swap(block, by):
        return lax.ppermute(block, "cells", [(s, s ^ by) for s in range(types)])

    def across(panel_, by):
        return lax.ppermute(panel_, "blk", [(b, (b + by * cores) % blocks) for b in range(blocks)])

    def side(name, panel_, *waits):
        with jax.named_scope(name):
            return lax.ppermute(after(panel_, *waits), "blk", [(b, b ^ 1) for b in range(blocks)])

    mean = gene_mean.reshape(1, panel)
    order = sorted(range(1, types), key=lambda j: (j == 3, j == 1, j))
    left, own, far, before = None, None, [], None
    for k in range(chunks):
        arrived = [packed[k][0]]
        for j in order:
            block = packed[k][j]
            if k:
                block = after(block, before[len(arrived)])
            with jax.named_scope(f"cells_{j}_chunk_{k}"):
                arrived.append(swap(block, j))
        before = list(arrived)
        if k >= 2:
            arrived[0] = after(arrived[0], *far[k - 2])
        if k == 0:
            first = arrived
        gather = []
        if k == chunks - 1:
            gather = [[got[d] for got in far[: k - 1]] for d in range(chips - 1)]
        scaled, left, count, own, *joined = standardize(
            types, cap, mean, starts[k], arrived, first, left, own, gather
        )
        with jax.named_scope(f"far_{k}"):
            far.append([across(scaled, d) for d in range(1, chips)])

    multiply = functools.partial(gram, blocks, cores, count, left)
    last = chunks - 1
    near = side("near", own)
    joined_near = [side("far_near", p) for p in joined]
    out = multiply([([own], (0, 0, 0))], None, brief)
    second = [side(f"far_near_{last - 1}", p, own) for p in far[last - 1]]
    groups = [([p, far[last - 1][i]], (i + 1, 0, 0)) for i, p in enumerate(joined)]
    out = multiply(groups, out, lengthy)
    groups = [([near], (0, 1, 0))]
    groups += [([p, second[i]], (i + 1, 1, 0)) for i, p in enumerate(joined_near)]
    out = multiply(groups, out, brief)
    final = [side(f"far_near_{last}", p, out) for p in far[last]]
    edge = starts[last]
    out = multiply([([p], (d, 0, edge)) for d, p in enumerate(far[last], 1)], out, brief)
    return multiply([([p], (d, 1, edge)) for d, p in enumerate(final, 1)], out, brief)


def solution(mesh):
    placed = (
        P(("parts", "cells"), "blk"),
        P(("parts", "cells")),
        P(("parts", "cells")),
        P(("parts", "blk")),
    )
    return jax.shard_map(
        shards,
        mesh=mesh,
        in_specs=placed,
        out_specs=P(("parts", "cells"), "blk", None),
        check_vma=False,
    )
```

```python
import functools

import jax
import jax.numpy as jnp
from jax import lax
from jax.experimental import pallas as pl
from jax.experimental.pallas import tpu as pltpu
from jax.sharding import PartitionSpec as P

dispersion = 100.0
epsilon = 1e-05
TILE = 16
VMEM = 16 * 1024 * 1024

brief = pl.CostEstimate(flops=1024, bytes_accessed=1024, transcendentals=0)
lengthy = pl.CostEstimate(flops=2 * 10**10, bytes_accessed=1024, transcendentals=0)
whole = pl.BlockSpec(memory_space=pltpu.VMEM)
anywhere = pl.BlockSpec(memory_space=pl.ANY)


def pack_kernel(types, cap, widths, type_ref, factor_ref, expr_ref, *outs):
    rows = expr_ref.shape[0]
    home = lax.axis_index("cells")
    kind = type_ref[...].reshape(1, rows)
    rel = jnp.bitwise_xor(kind, home)
    lines = max(types, 8)
    hot = lax.broadcasted_iota(jnp.int32, (lines, rows), 0) == rel
    hot_f = jnp.where(hot, 1.0, 0.0)
    upper = jnp.where(
        lax.broadcasted_iota(jnp.int32, (rows, rows), 0)
        <= lax.broadcasted_iota(jnp.int32, (rows, rows), 1),
        1.0,
        0.0,
    ).astype(jnp.bfloat16)
    running = jnp.dot(hot_f.astype(jnp.bfloat16), upper, preferred_element_type=jnp.float32)
    rank = jnp.sum(hot_f * running, axis=0, keepdims=True) - 1.0
    slot = rel * cap + rank.astype(jnp.int32)
    factor = factor_ref[...].astype(jnp.float32).reshape(1, rows)
    factor = jnp.broadcast_to(factor, (TILE, rows)).astype(jnp.bfloat16)
    values = expr_ref[...]
    for j in range(types):
        place = jnp.where(
            lax.broadcasted_iota(jnp.int32, (cap, rows), 0) + j * cap == slot, 1.0, 0.0
        ).astype(jnp.bfloat16)
        block = jnp.dot(place, values, preferred_element_type=jnp.float32).astype(jnp.bfloat16)
        start = 0
        for k, width in enumerate(widths):
            outs[k * types + j][0:cap, :] = block[:, start : start + width]
            start += width
        line = lax.dot_general(
            factor, place, (((1,), (1,)), ((), ())), preferred_element_type=jnp.float32
        )
        row = lax.broadcasted_iota(jnp.int32, (TILE, 1), 0)
        width = widths[0]
        tail = jnp.zeros((TILE, min(width, cap)), jnp.float32)
        for i in range(pl.cdiv(cap, width)):
            tail = jnp.where(row == i, line[:, i * width : min((i + 1) * width, cap)], tail)
        outs[j][cap : cap + TILE, 0 : min(width, cap)] = tail.astype(jnp.bfloat16)


def pack(types, cap, widths, cell_type, size_factor, expression):
    rows = expression.shape[0]
    shapes = [
        jax.ShapeDtypeStruct((cap + (TILE if k == 0 else 0), width), jnp.bfloat16)
        for k, width in enumerate(widths)
        for _ in range(types)
    ]
    flat = pl.pallas_call(
        functools.partial(pack_kernel, types, cap, widths),
        out_shape=shapes,
        in_specs=[whole] * 3,
        out_specs=[whole] * len(shapes),
        compiler_params=pltpu.CompilerParams(vmem_limit_bytes=VMEM),
        cost_estimate=brief,
        name="pack",
    )(cell_type, size_factor, expression)
    return [flat[k * types : (k + 1) * types] for k in range(len(widths))]


def standardize_kernel(types, cap, lead, separate, start, gathered, mean_ref, *refs):
    blocks = refs[:types]
    tails = refs[types : 2 * types] if separate else blocks
    base = 0 if separate else cap
    refs = refs[2 * types :] if separate else refs[types:]
    work, turned, sems = refs[-3:]
    if gathered:
        scaled_ref, turned_ref, count_ref, all_ref, *joined_refs = refs[-7 - gathered[0] : -3]
    else:
        scaled_ref, turned_ref, count_ref, all_ref = refs[-7:-3]
        joined_refs = []
    copies = []
    if gathered:
        sources = refs[: len(gathered[1])]
        for source, (joined, column) in zip(sources, gathered[1]):
            spot = joined_refs[joined].at[:, pl.ds(column, source.shape[1])]
            copies.append(pltpu.make_async_copy(source, spot, sems.at[2 + len(copies)]))
            copies[-1].start()
    width = work.shape[1]
    mean = mean_ref[:, start : start + width]
    piece = min(lead, cap)
    total = jnp.zeros((1, width), jnp.float32)
    count = jnp.zeros((1, 1), jnp.float32)
    alive = []
    for j in range(types):
        column = jnp.zeros((cap, 1), jnp.float32)
        for i in range(pl.cdiv(cap, lead)):
            line = tails[j][base : base + TILE, 0:piece].astype(jnp.float32)[i : i + 1, :]
            diagonal = (
                lax.broadcasted_iota(jnp.int32, (cap, piece), 0)
                == lax.broadcasted_iota(jnp.int32, (cap, piece), 1) + i * lead
            )
            column += jnp.sum(jnp.where(diagonal, line, 0.0), axis=1, keepdims=True)
        live = column > 0.0
        alive.append(live)
        count += jnp.sum(jnp.where(live, 1.0, 0.0), axis=0, keepdims=True)
        expected = jnp.where(live, column * mean, 1.0)
        values = blocks[j][0:cap, :].astype(jnp.float32)
        residual = jnp.where(
            live,
            (values - expected) * lax.rsqrt(expected + expected * expected * (1.0 / dispersion)),
            0.0,
        )
        work[j * cap : (j + 1) * cap, :] = residual
        total += jnp.sum(residual, axis=0, keepdims=True)
    center = total / count
    square = jnp.zeros((1, width), jnp.float32)
    for j in range(types):
        centered = jnp.where(alive[j], work[j * cap : (j + 1) * cap, :] - center, 0.0)
        work[j * cap : (j + 1) * cap, :] = centered
        square += jnp.sum(centered * centered, axis=0, keepdims=True)
    scale = lax.rsqrt(square / count + epsilon)
    for j in range(types):
        scaled = work[j * cap : (j + 1) * cap, :] * scale
        scaled_ref[j * cap : (j + 1) * cap, :] = scaled.astype(jnp.bfloat16)
        work[j * cap : (j + 1) * cap, :] = scaled
    slots = types * cap
    columns = pl.ds(start, width)
    copies.append(pltpu.make_async_copy(scaled_ref, all_ref.at[:, columns], sems.at[0]))
    copies[-1].start()
    turned[...] = jnp.transpose(work[...]).astype(jnp.bfloat16)
    copies.append(pltpu.make_async_copy(turned, turned_ref.at[columns, :], sems.at[1]))
    copies[-1].start()
    for copy in copies:
        copy.wait()
    count_ref[...] = jnp.broadcast_to(count, count_ref.shape)


def standardize(types, cap, mean, start, blocks, first, left, own, gather):
    lead, width = first[0].shape[1], blocks[0].shape[1]
    panel = mean.shape[1]
    separate = first is not blocks
    slots = types * cap
    specs = [whole] * (1 + types)
    args = [mean, *blocks]
    if separate:
        specs += [pl.BlockSpec((TILE, lead), lambda i: (cap // TILE, 0))] * types
        args += list(first)
    gathered, shapes = [], []
    for i, panels in enumerate(gather):
        column = 0
        for array in panels:
            gathered.append((i, column))
            column += array.shape[1]
            specs.append(whole)
            args.append(array)
        shapes.append(jax.ShapeDtypeStruct((slots, column), jnp.bfloat16))
    aliases = {}
    for value, output in ((left, 1), (own, 3)):
        if value is not None:
            aliases[len(args)] = output
            specs.append(anywhere)
            args.append(value)
    return pl.pallas_call(
        functools.partial(
            standardize_kernel,
            types,
            cap,
            lead,
            separate,
            start,
            (len(gather), gathered) if gathered else None,
        ),
        grid=(1,),
        out_shape=[
            jax.ShapeDtypeStruct((slots, width), jnp.bfloat16),
            jax.ShapeDtypeStruct((panel, slots), jnp.bfloat16),
            jax.ShapeDtypeStruct((8, 128), jnp.float32),
            jax.ShapeDtypeStruct((slots, panel), jnp.bfloat16),
            *shapes,
        ],
        in_specs=specs,
        out_specs=[whole, anywhere, whole, anywhere] + [whole] * len(shapes),
        scratch_shapes=[
            pltpu.VMEM((slots, width), jnp.float32),
            pltpu.VMEM((width, slots), jnp.bfloat16),
            pltpu.SemaphoreType.DMA((2 + len(gathered),)),
        ],
        input_output_aliases=aliases,
        compiler_params=pltpu.CompilerParams(vmem_limit_bytes=VMEM),
        cost_estimate=lengthy,
        name="standardize",
    )(*args)


def gram_kernel(blocks, cores, strip, groups, arrays, count_ref, left_ref, *refs):
    sources = refs[:arrays]
    out_ref, joined, tile, join_sems, sems = refs[-5:]
    rows, slots = left_ref.shape
    inverse = 1.0 / count_ref[0:1, 0:1]
    me = lax.axis_index("blk")

    joins, column = [], 0
    for panels, _ in groups:
        joins.append([])
        if len(panels) > 1:
            for index in panels:
                width = sources[index].shape[1]
                spot = joined.at[:, pl.ds(column, width)]
                joins[-1].append((column, sources[index], spot))
                column += width
    sent = 0
    for parts in joins:
        for _, source, spot in parts:
            pltpu.make_async_copy(source, spot, join_sems.at[sent]).start()
            sent += 1
    stores, sent = [], 0
    for (panels, (chip, flip, first)), parts in zip(groups, joins):
        for _, source, spot in parts:
            pltpu.make_async_copy(source, spot, join_sems.at[sent]).wait()
            sent += 1
        width = sum(sources[index].shape[1] for index in panels)
        owner = lax.rem(me + (blocks - chip * cores), blocks)
        owner = jnp.bitwise_xor(owner, flip)
        column = pl.multiple_of(owner * rows + first, 128)
        for row in range(0, rows, strip):
            slot = len(stores) % 2
            if len(stores) >= 2:
                stores[-2].wait()
            if parts:
                right = joined[:, parts[0][0] : parts[0][0] + width]
            else:
                right = sources[panels[0]][...]
            product = jnp.dot(
                left_ref[row : row + strip, :], right, preferred_element_type=jnp.float32
            )
            tile[slot, :, 0:width] = (product * inverse).astype(jnp.bfloat16)
            stores.append(
                pltpu.make_async_copy(
                    tile.at[slot, :, pl.ds(0, width)],
                    out_ref.at[0, pl.ds(row, strip), pl.ds(column, width)],
                    sems.at[slot],
                )
            )
            stores[-1].start()
    for store in stores[-2:]:
        store.wait()


def gram(blocks, cores, count, left, groups, before, cost):
    rows, slots = left.shape
    arrays, layout = [], []
    for panels, place in groups:
        layout.append((list(range(len(arrays), len(arrays) + len(panels))), place))
        arrays += panels
    joined = [array for panels, _ in groups if len(panels) > 1 for array in panels]
    widest = max(sum(array.shape[1] for array in panels) for panels, _ in groups)
    strip = min(rows, 512 if widest > 512 else 1024)
    args = [count, left, *arrays]
    specs = [whole] * len(args)
    if before is not None:
        args.append(before)
        specs.append(anywhere)
    return pl.pallas_call(
        functools.partial(gram_kernel, blocks, cores, strip, layout, len(arrays)),
        in_specs=specs,
        out_specs=anywhere,
        out_shape=jax.ShapeDtypeStruct((1, rows, rows * blocks), jnp.bfloat16),
        scratch_shapes=[
            pltpu.VMEM((slots, max(sum(array.shape[1] for array in joined), 128)), jnp.bfloat16),
            pltpu.VMEM((2, strip, widest), jnp.bfloat16),
            pltpu.SemaphoreType.DMA((max(len(joined), 1),)),
            pltpu.SemaphoreType.DMA((2,)),
        ],
        input_output_aliases={} if before is None else {len(args) - 1: 0},
        compiler_params=pltpu.CompilerParams(vmem_limit_bytes=VMEM),
        cost_estimate=cost,
        name="gram",
    )(*args)


def after(value, *others):
    return lax.optimization_barrier((value, *others))[0]


def shards(expression, cell_type, size_factor, gene_mean):
    types = lax.axis_size("cells")
    blocks = lax.axis_size("blk")
    shard_rows, panel = expression.shape
    cap = 2 * shard_rows // types
    assert types & (types - 1) == 0
    widths = [256] * (panel // 256)
    chunks = len(widths)
    starts = [sum(widths[:k]) for k in range(chunks)]
    cores = 2
    chips = blocks // cores
    window = 3

    packed = pack(types, cap, widths, cell_type, size_factor, expression)

    def swap(block, by):
        return lax.ppermute(block, "cells", [(s, s ^ by) for s in range(types)])

    def across(panel_, by):
        return lax.ppermute(panel_, "blk", [(b, (b + by * cores) % blocks) for b in range(blocks)])

    def side(name, panel_, *waits):
        with jax.named_scope(name):
            return lax.ppermute(after(panel_, *waits), "blk", [(b, b ^ 1) for b in range(blocks)])

    mean = gene_mean.reshape(1, panel)
    order = sorted(range(1, types), key=lambda j: (j == 3, j == 1, j))
    left, own, far, before = None, None, [], None
    for k in range(chunks):
        arrived = [packed[k][0]]
        for j in order:
            block = packed[k][j]
            if k:
                block = after(block, before[len(arrived)])
            with jax.named_scope(f"cells_{j}_chunk_{k}"):
                arrived.append(swap(block, j))
        before = list(arrived)
        if k >= 2:
            arrived[0] = after(arrived[0], *far[k - 2])
        if k == 0:
            first = arrived
        gather = []
        if k == chunks - 1 and k > 1:
            gather = [[got[d] for got in far[: k - 1]] for d in range(chips - 1)]
        scaled, left, count, own, *joined = standardize(
            types, cap, mean, starts[k], arrived, first, left, own, gather
        )
        with jax.named_scope(f"far_{k}"):
            far.append([across(scaled, d) for d in range(1, chips)])

    multiply = functools.partial(gram, blocks, cores, count, left)
    last = chunks - 1
    near = side("near", own)
    joined_near = [[side("far_near", p)] for p in joined] or [[]] * (chips - 1)
    joined = [[p] for p in joined] or [[]] * (chips - 1)
    out = multiply([([own], (0, 0, 0))], None, brief)
    second = [side(f"far_near_{last - 1}", p, own) for p in far[last - 1]]
    groups = [([*p, far[last - 1][i]], (i + 1, 0, 0)) for i, p in enumerate(joined)]
    out = multiply(groups, out, lengthy)
    groups = [([near], (0, 1, 0))]
    groups += [([*p, second[i]], (i + 1, 1, 0)) for i, p in enumerate(joined_near)]
    out = multiply(groups, out, brief)
    final = [side(f"far_near_{last}", p, out) for p in far[last]]
    edge = starts[last]
    out = multiply([([p], (d, 0, edge)) for d, p in enumerate(far[last], 1)], out, brief)
    return multiply([([p], (d, 1, edge)) for d, p in enumerate(final, 1)], out, brief)


def solution(mesh):
    placed = (
        P(("parts", "cells"), "blk"),
        P(("parts", "cells")),
        P(("parts", "cells")),
        P(("parts", "blk")),
    )
    return jax.shard_map(
        shards,
        mesh=mesh,
        in_specs=placed,
        out_specs=P(("parts", "cells"), "blk", None),
        check_vma=False,
    )
```

```python
import functools

import jax
import jax.numpy as jnp
from jax import lax
from jax.experimental import pallas as pl
from jax.experimental.pallas import tpu as pltpu
from jax.sharding import PartitionSpec as P

dispersion = 100.0
epsilon = 1e-05
TILE = 16
VMEM = 16 * 1024 * 1024

brief = pl.CostEstimate(flops=1024, bytes_accessed=1024, transcendentals=0)
lengthy = pl.CostEstimate(flops=2 * 10**10, bytes_accessed=1024, transcendentals=0)
whole = pl.BlockSpec(memory_space=pltpu.VMEM)
anywhere = pl.BlockSpec(memory_space=pl.ANY)


def pack_kernel(types, cap, widths, type_ref, factor_ref, expr_ref, *outs):
    rows = expr_ref.shape[0]
    home = lax.axis_index("cells")
    kind = type_ref[...].reshape(1, rows)
    rel = jnp.bitwise_xor(kind, home)
    lines = max(types, 8)
    hot = lax.broadcasted_iota(jnp.int32, (lines, rows), 0) == rel
    hot_f = jnp.where(hot, 1.0, 0.0)
    upper = jnp.where(
        lax.broadcasted_iota(jnp.int32, (rows, rows), 0)
        <= lax.broadcasted_iota(jnp.int32, (rows, rows), 1),
        1.0,
        0.0,
    ).astype(jnp.bfloat16)
    running = jnp.dot(hot_f.astype(jnp.bfloat16), upper, preferred_element_type=jnp.float32)
    rank = jnp.sum(hot_f * running, axis=0, keepdims=True) - 1.0
    slot = rel * cap + rank.astype(jnp.int32)
    factor = factor_ref[...].astype(jnp.float32).reshape(1, rows)
    factor = jnp.broadcast_to(factor, (TILE, rows)).astype(jnp.bfloat16)
    values = expr_ref[...]
    for j in range(types):
        place = jnp.where(
            lax.broadcasted_iota(jnp.int32, (cap, rows), 0) + j * cap == slot, 1.0, 0.0
        ).astype(jnp.bfloat16)
        block = jnp.dot(place, values, preferred_element_type=jnp.float32).astype(jnp.bfloat16)
        start = 0
        for k, width in enumerate(widths):
            outs[k * types + j][0:cap, :] = block[:, start : start + width]
            start += width
        line = lax.dot_general(
            factor, place, (((1,), (1,)), ((), ())), preferred_element_type=jnp.float32
        )
        row = lax.broadcasted_iota(jnp.int32, (TILE, 1), 0)
        width = widths[0]
        tail = jnp.zeros((TILE, min(width, cap)), jnp.float32)
        for i in range(pl.cdiv(cap, width)):
            tail = jnp.where(row == i, line[:, i * width : min((i + 1) * width, cap)], tail)
        outs[j][cap : cap + TILE, 0 : min(width, cap)] = tail.astype(jnp.bfloat16)


def pack(types, cap, widths, cell_type, size_factor, expression):
    rows = expression.shape[0]
    shapes = [
        jax.ShapeDtypeStruct((cap + (TILE if k == 0 else 0), width), jnp.bfloat16)
        for k, width in enumerate(widths)
        for _ in range(types)
    ]
    flat = pl.pallas_call(
        functools.partial(pack_kernel, types, cap, widths),
        out_shape=shapes,
        in_specs=[whole] * 3,
        out_specs=[whole] * len(shapes),
        compiler_params=pltpu.CompilerParams(vmem_limit_bytes=VMEM),
        cost_estimate=brief,
        name="pack",
    )(cell_type, size_factor, expression)
    return [flat[k * types : (k + 1) * types] for k in range(len(widths))]


def standardize_kernel(types, cap, lead, separate, start, gathered, mean_ref, *refs):
    blocks = refs[:types]
    tails = refs[types : 2 * types] if separate else blocks
    base = 0 if separate else cap
    refs = refs[2 * types :] if separate else refs[types:]
    work, turned, sems = refs[-3:]
    if gathered:
        scaled_ref, turned_ref, count_ref, all_ref, *joined_refs = refs[-7 - gathered[0] : -3]
    else:
        scaled_ref, turned_ref, count_ref, all_ref = refs[-7:-3]
        joined_refs = []
    copies = []
    if gathered:
        sources = refs[: len(gathered[1])]
        for source, (joined, column) in zip(sources, gathered[1]):
            spot = joined_refs[joined].at[:, pl.ds(column, source.shape[1])]
            copies.append(pltpu.make_async_copy(source, spot, sems.at[2 + len(copies)]))
            copies[-1].start()
    width = work.shape[1]
    mean = mean_ref[:, start : start + width]
    piece = min(lead, cap)
    total = jnp.zeros((1, width), jnp.float32)
    count = jnp.zeros((1, 1), jnp.float32)
    alive = []
    for j in range(types):
        column = jnp.zeros((cap, 1), jnp.float32)
        for i in range(pl.cdiv(cap, lead)):
            line = tails[j][base : base + TILE, 0:piece].astype(jnp.float32)[i : i + 1, :]
            diagonal = (
                lax.broadcasted_iota(jnp.int32, (cap, piece), 0)
                == lax.broadcasted_iota(jnp.int32, (cap, piece), 1) + i * lead
            )
            column += jnp.sum(jnp.where(diagonal, line, 0.0), axis=1, keepdims=True)
        live = column > 0.0
        alive.append(live)
        count += jnp.sum(jnp.where(live, 1.0, 0.0), axis=0, keepdims=True)
        expected = jnp.where(live, column * mean, 1.0)
        values = blocks[j][0:cap, :].astype(jnp.float32)
        residual = jnp.where(
            live,
            (values - expected) * lax.rsqrt(expected + expected * expected * (1.0 / dispersion)),
            0.0,
        )
        work[j * cap : (j + 1) * cap, :] = residual
        total += jnp.sum(residual, axis=0, keepdims=True)
    center = total / count
    square = jnp.zeros((1, width), jnp.float32)
    for j in range(types):
        centered = jnp.where(alive[j], work[j * cap : (j + 1) * cap, :] - center, 0.0)
        work[j * cap : (j + 1) * cap, :] = centered
        square += jnp.sum(centered * centered, axis=0, keepdims=True)
    scale = lax.rsqrt(square / count + epsilon)
    for j in range(types):
        scaled = work[j * cap : (j + 1) * cap, :] * scale
        scaled_ref[j * cap : (j + 1) * cap, :] = scaled.astype(jnp.bfloat16)
        work[j * cap : (j + 1) * cap, :] = scaled
    slots = types * cap
    columns = pl.ds(start, width)
    copies.append(pltpu.make_async_copy(scaled_ref, all_ref.at[:, columns], sems.at[0]))
    copies[-1].start()
    turned[...] = jnp.transpose(work[...]).astype(jnp.bfloat16)
    copies.append(pltpu.make_async_copy(turned, turned_ref.at[columns, :], sems.at[1]))
    copies[-1].start()
    for copy in copies:
        copy.wait()
    count_ref[...] = jnp.broadcast_to(count, count_ref.shape)


def standardize(types, cap, mean, start, blocks, first, left, own, gather):
    lead, width = first[0].shape[1], blocks[0].shape[1]
    panel = mean.shape[1]
    separate = first is not blocks
    slots = types * cap
    specs = [whole] * (1 + types)
    args = [mean, *blocks]
    if separate:
        specs += [pl.BlockSpec((TILE, lead), lambda i: (cap // TILE, 0))] * types
        args += list(first)
    gathered, shapes = [], []
    for i, panels in enumerate(gather):
        column = 0
        for array in panels:
            gathered.append((i, column))
            column += array.shape[1]
            specs.append(whole)
            args.append(array)
        shapes.append(jax.ShapeDtypeStruct((slots, column), jnp.bfloat16))
    aliases = {}
    for value, output in ((left, 1), (own, 3)):
        if value is not None:
            aliases[len(args)] = output
            specs.append(anywhere)
            args.append(value)
    return pl.pallas_call(
        functools.partial(
            standardize_kernel,
            types,
            cap,
            lead,
            separate,
            start,
            (len(gather), gathered) if gathered else None,
        ),
        grid=(1,),
        out_shape=[
            jax.ShapeDtypeStruct((slots, width), jnp.bfloat16),
            jax.ShapeDtypeStruct((panel, slots), jnp.bfloat16),
            jax.ShapeDtypeStruct((8, 128), jnp.float32),
            jax.ShapeDtypeStruct((slots, panel), jnp.bfloat16),
            *shapes,
        ],
        in_specs=specs,
        out_specs=[whole, anywhere, whole, anywhere] + [whole] * len(shapes),
        scratch_shapes=[
            pltpu.VMEM((slots, width), jnp.float32),
            pltpu.VMEM((width, slots), jnp.bfloat16),
            pltpu.SemaphoreType.DMA((2 + len(gathered),)),
        ],
        input_output_aliases=aliases,
        compiler_params=pltpu.CompilerParams(vmem_limit_bytes=VMEM),
        cost_estimate=lengthy,
        name="standardize",
    )(*args)


def gram_kernel(blocks, cores, strip, groups, arrays, count_ref, left_ref, *refs):
    sources = refs[:arrays]
    out_ref, joined, tile, join_sems, sems = refs[-5:]
    rows, slots = left_ref.shape
    inverse = 1.0 / count_ref[0:1, 0:1]
    me = lax.axis_index("blk")

    joins, column = [], 0
    for panels, _ in groups:
        joins.append([])
        if len(panels) > 1:
            for index in panels:
                width = sources[index].shape[1]
                spot = joined.at[:, pl.ds(column, width)]
                joins[-1].append((column, sources[index], spot))
                column += width
    sent = 0
    for parts in joins:
        for _, source, spot in parts:
            pltpu.make_async_copy(source, spot, join_sems.at[sent]).start()
            sent += 1
    stores, sent = [], 0
    for (panels, (chip, flip, first)), parts in zip(groups, joins):
        for _, source, spot in parts:
            pltpu.make_async_copy(source, spot, join_sems.at[sent]).wait()
            sent += 1
        width = sum(sources[index].shape[1] for index in panels)
        owner = lax.rem(me + (blocks - chip * cores), blocks)
        owner = jnp.bitwise_xor(owner, flip)
        column = pl.multiple_of(owner * rows + first, 128)
        for row in range(0, rows, strip):
            slot = len(stores) % 2
            if len(stores) >= 2:
                stores[-2].wait()
            if parts:
                right = joined[:, parts[0][0] : parts[0][0] + width]
            else:
                right = sources[panels[0]][...]
            product = jnp.dot(
                left_ref[row : row + strip, :], right, preferred_element_type=jnp.float32
            )
            tile[slot, :, 0:width] = (product * inverse).astype(jnp.bfloat16)
            stores.append(
                pltpu.make_async_copy(
                    tile.at[slot, :, pl.ds(0, width)],
                    out_ref.at[0, pl.ds(row, strip), pl.ds(column, width)],
                    sems.at[slot],
                )
            )
            stores[-1].start()
    for store in stores[-2:]:
        store.wait()


def gram(blocks, cores, count, left, groups, before, cost):
    rows, slots = left.shape
    arrays, layout = [], []
    for panels, place in groups:
        layout.append((list(range(len(arrays), len(arrays) + len(panels))), place))
        arrays += panels
    joined = [array for panels, _ in groups if len(panels) > 1 for array in panels]
    widest = max(sum(array.shape[1] for array in panels) for panels, _ in groups)
    strip = min(rows, 512 if widest > 512 else 1024)
    args = [count, left, *arrays]
    specs = [whole] * len(args)
    if before is not None:
        args.append(before)
        specs.append(anywhere)
    return pl.pallas_call(
        functools.partial(gram_kernel, blocks, cores, strip, layout, len(arrays)),
        in_specs=specs,
        out_specs=anywhere,
        out_shape=jax.ShapeDtypeStruct((1, rows, rows * blocks), jnp.bfloat16),
        scratch_shapes=[
            pltpu.VMEM((slots, max(sum(array.shape[1] for array in joined), 128)), jnp.bfloat16),
            pltpu.VMEM((2, strip, widest), jnp.bfloat16),
            pltpu.SemaphoreType.DMA((max(len(joined), 1),)),
            pltpu.SemaphoreType.DMA((2,)),
        ],
        input_output_aliases={} if before is None else {len(args) - 1: 0},
        compiler_params=pltpu.CompilerParams(vmem_limit_bytes=VMEM),
        cost_estimate=cost,
        name="gram",
    )(*args)


def after(value, *others):
    return lax.optimization_barrier((value, *others))[0]


def shards(expression, cell_type, size_factor, gene_mean):
    types = lax.axis_size("cells")
    blocks = lax.axis_size("blk")
    shard_rows, panel = expression.shape
    cap = 2 * shard_rows // types
    assert types & (types - 1) == 0
    widths = [256] * (panel // 256)
    chunks = len(widths)
    starts = [sum(widths[:k]) for k in range(chunks)]
    cores = 2
    chips = blocks // cores
    window = 3

    packed = pack(types, cap, widths, cell_type, size_factor, expression)

    def swap(block, by):
        return lax.ppermute(block, "cells", [(s, s ^ by) for s in range(types)])

    def across(panel_, by):
        return lax.ppermute(panel_, "blk", [(b, (b + by * cores) % blocks) for b in range(blocks)])

    def side(name, panel_, *waits):
        with jax.named_scope(name):
            return lax.ppermute(after(panel_, *waits), "blk", [(b, b ^ 1) for b in range(blocks)])

    mean = gene_mean.reshape(1, panel)
    order = sorted(range(1, types), key=lambda j: (j == 3, j == 1, j))
    left, own, far, before = None, None, [], None
    for k in range(chunks):
        arrived = [packed[k][0]]
        for j in order:
            block = packed[k][j]
            if k:
                block = after(block, before[len(arrived)])
            with jax.named_scope(f"cells_{j}_chunk_{k}"):
                arrived.append(swap(block, j))
        before = list(arrived)
        if k >= 2:
            arrived[0] = after(arrived[0], *far[k - 2])
        if k == 0:
            first = arrived
        gather = []
        if k == chunks - 1 and k > 1:
            gather = [[got[d] for got in far[: k - 1]] for d in range(chips - 1)]
        scaled, left, count, own, *joined = standardize(
            types, cap, mean, starts[k], arrived, first, left, own, gather
        )
        if k < chunks - 1:
            with jax.named_scope(f"far_{k}"):
                far.append([across(scaled, d) for d in range(1, chips)])

    multiply = functools.partial(gram, blocks, cores, count, left)
    last = chunks - 1
    near = side("near", own)
    joined_near = [[side("far_near", p)] for p in joined] or [[]] * (chips - 1)
    joined = [[p] for p in joined] or [[]] * (chips - 1)
    groups = [([own], (0, 0, 0))] + [(p, (d, 0, 0)) for d, p in enumerate(joined, 1) if p]
    out = multiply(groups, None, brief)
    final = [across(after(scaled, out), d) for d in range(1, chips)]
    second = [side(f"far_near_{last - 1}", p, own) for p in far[last - 1]]
    edge = starts[last - 1]
    groups = [([p], (d, 0, edge)) for d, p in enumerate(far[last - 1], 1)]
    out = multiply(groups, out, lengthy)
    groups = [([near], (0, 1, 0))]
    groups += [([*p, second[i]], (i + 1, 1, 0)) for i, p in enumerate(joined_near)]
    out = multiply(groups, out, brief)
    final_near = [side(f"far_near_{last}", p, out) for p in final]
    edge = starts[last]
    out = multiply([([p], (d, 0, edge)) for d, p in enumerate(final, 1)], out, brief)
    return multiply([([p], (d, 1, edge)) for d, p in enumerate(final_near, 1)], out, brief)


def solution(mesh):
    placed = (
        P(("parts", "cells"), "blk"),
        P(("parts", "cells")),
        P(("parts", "cells")),
        P(("parts", "blk")),
    )
    return jax.shard_map(
        shards,
        mesh=mesh,
        in_specs=placed,
        out_specs=P(("parts", "cells"), "blk", None),
        check_vma=False,
    )
```

```python
import functools

import jax
import jax.numpy as jnp
from jax import lax
from jax.experimental import pallas as pl
from jax.experimental.pallas import tpu as pltpu
from jax.sharding import PartitionSpec as P

dispersion = 100.0
epsilon = 1e-05
TILE = 16
VMEM = 16 * 1024 * 1024

brief = pl.CostEstimate(flops=1024, bytes_accessed=1024, transcendentals=0)
lengthy = pl.CostEstimate(flops=2 * 10**10, bytes_accessed=1024, transcendentals=0)
whole = pl.BlockSpec(memory_space=pltpu.VMEM)
anywhere = pl.BlockSpec(memory_space=pl.ANY)


def pack_kernel(types, cap, widths, small_ref, expr_ref, *outs):
    rows = expr_ref.shape[0]
    home = lax.axis_index("cells")
    kind = small_ref[0:1, 0:rows].astype(jnp.int32)
    rel = jnp.bitwise_xor(kind, home)
    lines = max(types, 8)
    hot = lax.broadcasted_iota(jnp.int32, (lines, rows), 0) == rel
    hot_f = jnp.where(hot, 1.0, 0.0)
    upper = jnp.where(
        lax.broadcasted_iota(jnp.int32, (rows, rows), 0)
        <= lax.broadcasted_iota(jnp.int32, (rows, rows), 1),
        1.0,
        0.0,
    ).astype(jnp.bfloat16)
    running = jnp.dot(hot_f.astype(jnp.bfloat16), upper, preferred_element_type=jnp.float32)
    rank = jnp.sum(hot_f * running, axis=0, keepdims=True) - 1.0
    slot = rel * cap + rank.astype(jnp.int32)
    factor = jnp.broadcast_to(small_ref[1:2, 0:rows], (TILE, rows)).astype(jnp.bfloat16)
    values = expr_ref[...]
    for j in range(types):
        place = jnp.where(
            lax.broadcasted_iota(jnp.int32, (cap, rows), 0) + j * cap == slot, 1.0, 0.0
        ).astype(jnp.bfloat16)
        block = jnp.dot(place, values, preferred_element_type=jnp.float32).astype(jnp.bfloat16)
        start = 0
        for k, width in enumerate(widths):
            outs[k * types + j][0:cap, :] = block[:, start : start + width]
            start += width
        line = lax.dot_general(
            factor, place, (((1,), (1,)), ((), ())), preferred_element_type=jnp.float32
        )
        row = lax.broadcasted_iota(jnp.int32, (TILE, 1), 0)
        width = widths[0]
        tail = jnp.zeros((TILE, min(width, cap)), jnp.float32)
        for i in range(pl.cdiv(cap, width)):
            tail = jnp.where(row == i, line[:, i * width : min((i + 1) * width, cap)], tail)
        outs[j][cap : cap + TILE, 0 : min(width, cap)] = tail.astype(jnp.bfloat16)


def pack(types, cap, widths, small, expression):
    rows = expression.shape[0]
    shapes = [
        jax.ShapeDtypeStruct((cap + (TILE if k == 0 else 0), width), jnp.bfloat16)
        for k, width in enumerate(widths)
        for _ in range(types)
    ]
    flat = pl.pallas_call(
        functools.partial(pack_kernel, types, cap, widths),
        out_shape=shapes,
        in_specs=[whole] * 2,
        out_specs=[whole] * len(shapes),
        compiler_params=pltpu.CompilerParams(vmem_limit_bytes=VMEM),
        cost_estimate=brief,
        name="pack",
    )(small, expression)
    return [flat[k * types : (k + 1) * types] for k in range(len(widths))]


def standardize_kernel(types, cap, lead, separate, start, gathered, small_ref, *refs):
    blocks = refs[:types]
    tails = refs[types : 2 * types] if separate else blocks
    base = 0 if separate else cap
    refs = refs[2 * types :] if separate else refs[types:]
    work, turned, sems = refs[-3:]
    if gathered:
        scaled_ref, turned_ref, count_ref, all_ref, *joined_refs = refs[-7 - gathered[0] : -3]
    else:
        scaled_ref, turned_ref, count_ref, all_ref = refs[-7:-3]
        joined_refs = []
    copies = []
    if gathered:
        sources = refs[: len(gathered[1])]
        for source, (joined, column) in zip(sources, gathered[1]):
            spot = joined_refs[joined].at[:, pl.ds(column, source.shape[1])]
            copies.append(pltpu.make_async_copy(source, spot, sems.at[2 + len(copies)]))
            copies[-1].start()
    width = work.shape[1]
    mean = small_ref[2:3, start : start + width]
    piece = min(lead, cap)
    total = jnp.zeros((1, width), jnp.float32)
    count = jnp.zeros((1, 1), jnp.float32)
    alive = []
    for j in range(types):
        column = jnp.zeros((cap, 1), jnp.float32)
        for i in range(pl.cdiv(cap, lead)):
            line = tails[j][base : base + TILE, 0:piece].astype(jnp.float32)[i : i + 1, :]
            diagonal = (
                lax.broadcasted_iota(jnp.int32, (cap, piece), 0)
                == lax.broadcasted_iota(jnp.int32, (cap, piece), 1) + i * lead
            )
            column += jnp.sum(jnp.where(diagonal, line, 0.0), axis=1, keepdims=True)
        live = column > 0.0
        alive.append(live)
        count += jnp.sum(jnp.where(live, 1.0, 0.0), axis=0, keepdims=True)
        expected = jnp.where(live, column * mean, 1.0)
        values = blocks[j][0:cap, :].astype(jnp.float32)
        residual = jnp.where(
            live,
            (values - expected) * lax.rsqrt(expected + expected * expected * (1.0 / dispersion)),
            0.0,
        )
        work[j * cap : (j + 1) * cap, :] = residual
        total += jnp.sum(residual, axis=0, keepdims=True)
    center = total / count
    square = jnp.zeros((1, width), jnp.float32)
    for j in range(types):
        centered = jnp.where(alive[j], work[j * cap : (j + 1) * cap, :] - center, 0.0)
        work[j * cap : (j + 1) * cap, :] = centered
        square += jnp.sum(centered * centered, axis=0, keepdims=True)
    scale = lax.rsqrt(square / count + epsilon)
    for j in range(types):
        scaled = work[j * cap : (j + 1) * cap, :] * scale
        scaled_ref[j * cap : (j + 1) * cap, :] = scaled.astype(jnp.bfloat16)
        work[j * cap : (j + 1) * cap, :] = scaled
    slots = types * cap
    columns = pl.ds(start, width)
    copies.append(pltpu.make_async_copy(scaled_ref, all_ref.at[:, columns], sems.at[0]))
    copies[-1].start()
    turned[...] = jnp.transpose(work[...]).astype(jnp.bfloat16)
    copies.append(pltpu.make_async_copy(turned, turned_ref.at[columns, :], sems.at[1]))
    copies[-1].start()
    for copy in copies:
        copy.wait()
    count_ref[...] = jnp.broadcast_to(count, count_ref.shape)


def standardize(types, cap, panel, small, start, blocks, first, left, own, gather):
    lead, width = first[0].shape[1], blocks[0].shape[1]
    separate = first is not blocks
    slots = types * cap
    specs = [whole] * (1 + types)
    args = [small, *blocks]
    if separate:
        specs += [pl.BlockSpec((TILE, lead), lambda i: (cap // TILE, 0))] * types
        args += list(first)
    gathered, shapes = [], []
    for i, panels in enumerate(gather):
        column = 0
        for array in panels:
            gathered.append((i, column))
            column += array.shape[1]
            specs.append(whole)
            args.append(array)
        shapes.append(jax.ShapeDtypeStruct((slots, column), jnp.bfloat16))
    aliases = {}
    for value, output in ((left, 1), (own, 3)):
        if value is not None:
            aliases[len(args)] = output
            specs.append(anywhere)
            args.append(value)
    return pl.pallas_call(
        functools.partial(
            standardize_kernel,
            types,
            cap,
            lead,
            separate,
            start,
            (len(gather), gathered) if gathered else None,
        ),
        grid=(1,),
        out_shape=[
            jax.ShapeDtypeStruct((slots, width), jnp.bfloat16),
            jax.ShapeDtypeStruct((panel, slots), jnp.bfloat16),
            jax.ShapeDtypeStruct((8, 128), jnp.float32),
            jax.ShapeDtypeStruct((slots, panel), jnp.bfloat16),
            *shapes,
        ],
        in_specs=specs,
        out_specs=[whole, anywhere, whole, anywhere] + [whole] * len(shapes),
        scratch_shapes=[
            pltpu.VMEM((slots, width), jnp.float32),
            pltpu.VMEM((width, slots), jnp.bfloat16),
            pltpu.SemaphoreType.DMA((2 + len(gathered),)),
        ],
        input_output_aliases=aliases,
        compiler_params=pltpu.CompilerParams(vmem_limit_bytes=VMEM),
        cost_estimate=lengthy,
        name="standardize",
    )(*args)


def gram_kernel(blocks, cores, strip, groups, arrays, count_ref, left_ref, *refs):
    sources = refs[:arrays]
    out_ref, joined, tile, join_sems, sems = refs[-5:]
    rows, slots = left_ref.shape
    inverse = 1.0 / count_ref[0:1, 0:1]
    me = lax.axis_index("blk")

    joins, column = [], 0
    for panels, _ in groups:
        joins.append([])
        if len(panels) > 1:
            for index in panels:
                width = sources[index].shape[1]
                spot = joined.at[:, pl.ds(column, width)]
                joins[-1].append((column, sources[index], spot))
                column += width
    sent = 0
    for parts in joins:
        for _, source, spot in parts:
            pltpu.make_async_copy(source, spot, join_sems.at[sent]).start()
            sent += 1
    stores, sent = [], 0
    for (panels, (chip, flip, first)), parts in zip(groups, joins):
        for _, source, spot in parts:
            pltpu.make_async_copy(source, spot, join_sems.at[sent]).wait()
            sent += 1
        width = sum(sources[index].shape[1] for index in panels)
        owner = lax.rem(me + (blocks - chip * cores), blocks)
        owner = jnp.bitwise_xor(owner, flip)
        column = pl.multiple_of(owner * rows + first, 128)
        for row in range(0, rows, strip):
            slot = len(stores) % 2
            if len(stores) >= 2:
                stores[-2].wait()
            if parts:
                right = joined[:, parts[0][0] : parts[0][0] + width]
            else:
                right = sources[panels[0]][...]
            product = jnp.dot(
                left_ref[row : row + strip, :], right, preferred_element_type=jnp.float32
            )
            tile[slot, :, 0:width] = (product * inverse).astype(jnp.bfloat16)
            stores.append(
                pltpu.make_async_copy(
                    tile.at[slot, :, pl.ds(0, width)],
                    out_ref.at[0, pl.ds(row, strip), pl.ds(column, width)],
                    sems.at[slot],
                )
            )
            stores[-1].start()
    for store in stores[-2:]:
        store.wait()


def gram(blocks, cores, count, left, groups, before, cost):
    rows, slots = left.shape
    arrays, layout = [], []
    for panels, place in groups:
        layout.append((list(range(len(arrays), len(arrays) + len(panels))), place))
        arrays += panels
    joined = [array for panels, _ in groups if len(panels) > 1 for array in panels]
    widest = max(sum(array.shape[1] for array in panels) for panels, _ in groups)
    strip = min(rows, 512 if widest > 512 else 1024)
    args = [count, left, *arrays]
    specs = [whole] * len(args)
    if before is not None:
        args.append(before)
        specs.append(anywhere)
    return pl.pallas_call(
        functools.partial(gram_kernel, blocks, cores, strip, layout, len(arrays)),
        in_specs=specs,
        out_specs=anywhere,
        out_shape=jax.ShapeDtypeStruct((1, rows, rows * blocks), jnp.bfloat16),
        scratch_shapes=[
            pltpu.VMEM((slots, max(sum(array.shape[1] for array in joined), 128)), jnp.bfloat16),
            pltpu.VMEM((2, strip, widest), jnp.bfloat16),
            pltpu.SemaphoreType.DMA((max(len(joined), 1),)),
            pltpu.SemaphoreType.DMA((2,)),
        ],
        input_output_aliases={} if before is None else {len(args) - 1: 0},
        compiler_params=pltpu.CompilerParams(vmem_limit_bytes=VMEM),
        cost_estimate=cost,
        name="gram",
    )(*args)


def after(value, *others):
    return lax.optimization_barrier((value, *others))[0]


def shards(expression, cell_type, size_factor, gene_mean):
    types = lax.axis_size("cells")
    blocks = lax.axis_size("blk")
    shard_rows, panel = expression.shape
    cap = 2 * shard_rows // types
    assert types & (types - 1) == 0
    widths = [256] * (panel // 256)
    chunks = len(widths)
    starts = [sum(widths[:k]) for k in range(chunks)]
    cores = 2
    chips = blocks // cores
    window = 3

    small = [row.astype(jnp.float32) for row in (cell_type, size_factor, gene_mean)]
    size = max(shard_rows, panel)
    small = jnp.stack([jnp.pad(row, (0, size - row.shape[0])) for row in small])
    packed = pack(types, cap, widths, small, expression)

    def swap(block, by):
        return lax.ppermute(block, "cells", [(s, s ^ by) for s in range(types)])

    def across(panel_, by):
        return lax.ppermute(panel_, "blk", [(b, (b + by * cores) % blocks) for b in range(blocks)])

    def side(name, panel_, *waits):
        with jax.named_scope(name):
            return lax.ppermute(after(panel_, *waits), "blk", [(b, b ^ 1) for b in range(blocks)])

    order = sorted(range(1, types), key=lambda j: (j == 3, j == 1, j))
    left, own, far, before = None, None, [], None
    for k in range(chunks):
        arrived = [packed[k][0]]
        for j in order:
            block = packed[k][j]
            if k:
                block = after(block, before[len(arrived)])
            with jax.named_scope(f"cells_{j}_chunk_{k}"):
                arrived.append(swap(block, j))
        before = list(arrived)
        if k >= 2:
            arrived[0] = after(arrived[0], *far[k - 2])
        if k == 0:
            first = arrived
        gather = []
        if k == chunks - 1 and k > 1:
            gather = [[got[d] for got in far[: k - 1]] for d in range(chips - 1)]
        scaled, left, count, own, *joined = standardize(
            types, cap, panel, small, starts[k], arrived, first, left, own, gather
        )
        with jax.named_scope(f"far_{k}"):
            far.append([across(scaled, d) for d in range(1, chips)])

    multiply = functools.partial(gram, blocks, cores, count, left)
    last = chunks - 1
    near = side("near", own)
    joined_near = [[side("far_near", p)] for p in joined] or [[]] * (chips - 1)
    joined = [[p] for p in joined] or [[]] * (chips - 1)
    groups = [([own], (0, 0, 0))] + [(p, (d, 0, 0)) for d, p in enumerate(joined, 1) if p]
    out = multiply(groups, None, brief)
    final = far[last]
    second = [side(f"far_near_{last - 1}", p, own) for p in far[last - 1]]
    edge = starts[last - 1]
    groups = [([p], (d, 0, edge)) for d, p in enumerate(far[last - 1], 1)]
    out = multiply(groups, out, lengthy)
    groups = [([near], (0, 1, 0))]
    groups += [([*p, second[i]], (i + 1, 1, 0)) for i, p in enumerate(joined_near)]
    out = multiply(groups, out, brief)
    final_near = [side(f"far_near_{last}", p, out) for p in final]
    edge = starts[last]
    out = multiply([([p], (d, 0, edge)) for d, p in enumerate(final, 1)], out, brief)
    return multiply([([p], (d, 1, edge)) for d, p in enumerate(final_near, 1)], out, brief)


def solution(mesh):
    placed = (
        P(("parts", "cells"), "blk"),
        P(("parts", "cells")),
        P(("parts", "cells")),
        P(("parts", "blk")),
    )
    return jax.shard_map(
        shards,
        mesh=mesh,
        in_specs=placed,
        out_specs=P(("parts", "cells"), "blk", None),
        check_vma=False,
    )
```

```python
import functools

import jax
import jax.numpy as jnp
from jax import lax
from jax.experimental import pallas as pl
from jax.experimental.pallas import tpu as pltpu
from jax.sharding import PartitionSpec as P

dispersion = 100.0
epsilon = 1e-05
TILE = 16
VMEM = 16 * 1024 * 1024

brief = pl.CostEstimate(flops=1024, bytes_accessed=1024, transcendentals=0)
lengthy = pl.CostEstimate(flops=2 * 10**10, bytes_accessed=1024, transcendentals=0)
whole = pl.BlockSpec(memory_space=pltpu.VMEM)
anywhere = pl.BlockSpec(memory_space=pl.ANY)


def pack_kernel(types, cap, widths, type_ref, factor_ref, expr_ref, *outs):
    rows = expr_ref.shape[0]
    home = lax.axis_index("cells")
    kind = type_ref[...].reshape(1, rows)
    rel = jnp.bitwise_xor(kind, home)
    lines = max(types, 8)
    hot = lax.broadcasted_iota(jnp.int32, (lines, rows), 0) == rel
    hot_f = jnp.where(hot, 1.0, 0.0)
    upper = jnp.where(
        lax.broadcasted_iota(jnp.int32, (rows, rows), 0)
        <= lax.broadcasted_iota(jnp.int32, (rows, rows), 1),
        1.0,
        0.0,
    ).astype(jnp.bfloat16)
    running = jnp.dot(hot_f.astype(jnp.bfloat16), upper, preferred_element_type=jnp.float32)
    rank = jnp.sum(hot_f * running, axis=0, keepdims=True) - 1.0
    slot = rel * cap + rank.astype(jnp.int32)
    factor = factor_ref[...].astype(jnp.float32).reshape(1, rows)
    factor = jnp.broadcast_to(factor, (TILE, rows)).astype(jnp.bfloat16)
    values = expr_ref[...]
    for j in range(types):
        place = jnp.where(
            lax.broadcasted_iota(jnp.int32, (cap, rows), 0) + j * cap == slot, 1.0, 0.0
        ).astype(jnp.bfloat16)
        block = jnp.dot(place, values, preferred_element_type=jnp.float32).astype(jnp.bfloat16)
        start = 0
        for k, width in enumerate(widths):
            outs[k * types + j][0:cap, :] = block[:, start : start + width]
            start += width
        line = lax.dot_general(
            factor, place, (((1,), (1,)), ((), ())), preferred_element_type=jnp.float32
        )
        row = lax.broadcasted_iota(jnp.int32, (TILE, 1), 0)
        width = widths[0]
        tail = jnp.zeros((TILE, min(width, cap)), jnp.float32)
        for i in range(pl.cdiv(cap, width)):
            tail = jnp.where(row == i, line[:, i * width : min((i + 1) * width, cap)], tail)
        outs[j][cap : cap + TILE, 0 : min(width, cap)] = tail.astype(jnp.bfloat16)


def pack(types, cap, widths, cell_type, size_factor, expression):
    rows = expression.shape[0]
    shapes = [
        jax.ShapeDtypeStruct((cap + (TILE if k == 0 else 0), width), jnp.bfloat16)
        for k, width in enumerate(widths)
        for _ in range(types)
    ]
    flat = pl.pallas_call(
        functools.partial(pack_kernel, types, cap, widths),
        out_shape=shapes,
        in_specs=[whole] * 3,
        out_specs=[whole] * len(shapes),
        compiler_params=pltpu.CompilerParams(vmem_limit_bytes=VMEM),
        cost_estimate=brief,
        name="pack",
    )(cell_type, size_factor, expression)
    return [flat[k * types : (k + 1) * types] for k in range(len(widths))]


def standardize_kernel(types, cap, lead, separate, start, gathered, mean_ref, *refs):
    blocks = refs[:types]
    tails = refs[types : 2 * types] if separate else blocks
    base = 0 if separate else cap
    refs = refs[2 * types :] if separate else refs[types:]
    work, turned, sems = refs[-3:]
    if gathered:
        scaled_ref, turned_ref, count_ref, all_ref, *joined_refs = refs[-7 - gathered[0] : -3]
    else:
        scaled_ref, turned_ref, count_ref, all_ref = refs[-7:-3]
        joined_refs = []
    copies = []
    if gathered:
        sources = refs[: len(gathered[1])]
        for source, (joined, column) in zip(sources, gathered[1]):
            spot = joined_refs[joined].at[:, pl.ds(column, source.shape[1])]
            copies.append(pltpu.make_async_copy(source, spot, sems.at[2 + len(copies)]))
            copies[-1].start()
    width = work.shape[1]
    mean = mean_ref[0:1, start : start + width]
    piece = min(lead, cap)
    total = jnp.zeros((1, width), jnp.float32)
    count = jnp.zeros((1, 1), jnp.float32)
    alive = []
    for j in range(types):
        column = jnp.zeros((cap, 1), jnp.float32)
        for i in range(pl.cdiv(cap, lead)):
            line = tails[j][base : base + TILE, 0:piece].astype(jnp.float32)[i : i + 1, :]
            diagonal = (
                lax.broadcasted_iota(jnp.int32, (cap, piece), 0)
                == lax.broadcasted_iota(jnp.int32, (cap, piece), 1) + i * lead
            )
            column += jnp.sum(jnp.where(diagonal, line, 0.0), axis=1, keepdims=True)
        live = column > 0.0
        alive.append(live)
        count += jnp.sum(jnp.where(live, 1.0, 0.0), axis=0, keepdims=True)
        expected = jnp.where(live, column * mean, 1.0)
        values = blocks[j][0:cap, :].astype(jnp.float32)
        residual = jnp.where(
            live,
            (values - expected) * lax.rsqrt(expected + expected * expected * (1.0 / dispersion)),
            0.0,
        )
        work[j * cap : (j + 1) * cap, :] = residual
        total += jnp.sum(residual, axis=0, keepdims=True)
    center = total / count
    square = jnp.zeros((1, width), jnp.float32)
    for j in range(types):
        centered = jnp.where(alive[j], work[j * cap : (j + 1) * cap, :] - center, 0.0)
        work[j * cap : (j + 1) * cap, :] = centered
        square += jnp.sum(centered * centered, axis=0, keepdims=True)
    scale = lax.rsqrt(square / count + epsilon)
    for j in range(types):
        scaled = work[j * cap : (j + 1) * cap, :] * scale
        scaled_ref[j * cap : (j + 1) * cap, :] = scaled.astype(jnp.bfloat16)
        work[j * cap : (j + 1) * cap, :] = scaled
    slots = types * cap
    columns = pl.ds(start, width)
    copies.append(pltpu.make_async_copy(scaled_ref, all_ref.at[:, columns], sems.at[0]))
    copies[-1].start()
    turned[...] = jnp.transpose(work[...]).astype(jnp.bfloat16)
    copies.append(pltpu.make_async_copy(turned, turned_ref.at[columns, :], sems.at[1]))
    copies[-1].start()
    for copy in copies:
        copy.wait()
    count_ref[...] = jnp.broadcast_to(count, count_ref.shape)


def standardize(types, cap, mean, start, blocks, first, left, own, gather):
    lead, width = first[0].shape[1], blocks[0].shape[1]
    panel = mean.shape[1]
    separate = first is not blocks
    slots = types * cap
    specs = [whole] * (1 + types)
    args = [mean, *blocks]
    if separate:
        specs += [pl.BlockSpec((TILE, lead), lambda i: (cap // TILE, 0))] * types
        args += list(first)
    gathered, shapes = [], []
    for i, panels in enumerate(gather):
        column = 0
        for array in panels:
            gathered.append((i, column))
            column += array.shape[1]
            specs.append(whole)
            args.append(array)
        shapes.append(jax.ShapeDtypeStruct((slots, column), jnp.bfloat16))
    aliases = {}
    for value, output in ((left, 1), (own, 3)):
        if value is not None:
            aliases[len(args)] = output
            specs.append(anywhere)
            args.append(value)
    return pl.pallas_call(
        functools.partial(
            standardize_kernel,
            types,
            cap,
            lead,
            separate,
            start,
            (len(gather), gathered) if gathered else None,
        ),
        grid=(1,),
        out_shape=[
            jax.ShapeDtypeStruct((slots, width), jnp.bfloat16),
            jax.ShapeDtypeStruct((panel, slots), jnp.bfloat16),
            jax.ShapeDtypeStruct((8, 128), jnp.float32),
            jax.ShapeDtypeStruct((slots, panel), jnp.bfloat16),
            *shapes,
        ],
        in_specs=specs,
        out_specs=[whole, anywhere, whole, anywhere] + [whole] * len(shapes),
        scratch_shapes=[
            pltpu.VMEM((slots, width), jnp.float32),
            pltpu.VMEM((width, slots), jnp.bfloat16),
            pltpu.SemaphoreType.DMA((2 + len(gathered),)),
        ],
        input_output_aliases=aliases,
        compiler_params=pltpu.CompilerParams(vmem_limit_bytes=VMEM),
        cost_estimate=lengthy,
        name="standardize",
    )(*args)


def gram_kernel(blocks, cores, strip, groups, arrays, count_ref, left_ref, *refs):
    sources = refs[:arrays]
    out_ref, joined, tile, join_sems, sems = refs[-5:]
    rows, slots = left_ref.shape
    inverse = 1.0 / count_ref[0:1, 0:1]
    me = lax.axis_index("blk")

    joins, column = [], 0
    for panels, _ in groups:
        joins.append([])
        if len(panels) > 1:
            for index in panels:
                width = sources[index].shape[1]
                spot = joined.at[:, pl.ds(column, width)]
                joins[-1].append((column, sources[index], spot))
                column += width
    sent = 0
    for parts in joins:
        for _, source, spot in parts:
            pltpu.make_async_copy(source, spot, join_sems.at[sent]).start()
            sent += 1
    stores, sent = [], 0
    for (panels, (chip, flip, first)), parts in zip(groups, joins):
        for _, source, spot in parts:
            pltpu.make_async_copy(source, spot, join_sems.at[sent]).wait()
            sent += 1
        width = sum(sources[index].shape[1] for index in panels)
        owner = lax.rem(me + (blocks - chip * cores), blocks)
        owner = jnp.bitwise_xor(owner, flip)
        column = pl.multiple_of(owner * rows + first, 128)
        for row in range(0, rows, strip):
            slot = len(stores) % 2
            if len(stores) >= 2:
                stores[-2].wait()
            if parts:
                right = joined[:, parts[0][0] : parts[0][0] + width]
            else:
                right = sources[panels[0]][...]
            product = jnp.dot(
                left_ref[row : row + strip, :], right, preferred_element_type=jnp.float32
            )
            tile[slot, :, 0:width] = (product * inverse).astype(jnp.bfloat16)
            stores.append(
                pltpu.make_async_copy(
                    tile.at[slot, :, pl.ds(0, width)],
                    out_ref.at[0, pl.ds(row, strip), pl.ds(column, width)],
                    sems.at[slot],
                )
            )
            stores[-1].start()
    for store in stores[-2:]:
        store.wait()


def gram(blocks, cores, count, left, groups, before, cost):
    rows, slots = left.shape
    arrays, layout = [], []
    for panels, place in groups:
        layout.append((list(range(len(arrays), len(arrays) + len(panels))), place))
        arrays += panels
    joined = [array for panels, _ in groups if len(panels) > 1 for array in panels]
    widest = max(sum(array.shape[1] for array in panels) for panels, _ in groups)
    strip = min(rows, 512 if widest > 512 else 1024)
    args = [count, left, *arrays]
    specs = [whole] * len(args)
    if before is not None:
        args.append(before)
        specs.append(anywhere)
    return pl.pallas_call(
        functools.partial(gram_kernel, blocks, cores, strip, layout, len(arrays)),
        in_specs=specs,
        out_specs=anywhere,
        out_shape=jax.ShapeDtypeStruct((1, rows, rows * blocks), jnp.bfloat16),
        scratch_shapes=[
            pltpu.VMEM((slots, max(sum(array.shape[1] for array in joined), 128)), jnp.bfloat16),
            pltpu.VMEM((2, strip, widest), jnp.bfloat16),
            pltpu.SemaphoreType.DMA((max(len(joined), 1),)),
            pltpu.SemaphoreType.DMA((2,)),
        ],
        input_output_aliases={} if before is None else {len(args) - 1: 0},
        compiler_params=pltpu.CompilerParams(vmem_limit_bytes=VMEM),
        cost_estimate=cost,
        name="gram",
    )(*args)


def after(value, *others):
    return lax.optimization_barrier((value, *others))[0]


def shards(expression, cell_type, size_factor, gene_mean):
    types = lax.axis_size("cells")
    blocks = lax.axis_size("blk")
    shard_rows, panel = expression.shape
    cap = 2 * shard_rows // types
    assert types & (types - 1) == 0
    widths = [256] * (panel // 256)
    chunks = len(widths)
    starts = [sum(widths[:k]) for k in range(chunks)]
    cores = 2
    chips = blocks // cores
    window = 3

    packed = pack(types, cap, widths, cell_type, size_factor, expression)

    def swap(block, by):
        return lax.ppermute(block, "cells", [(s, s ^ by) for s in range(types)])

    def across(panel_, by):
        return lax.ppermute(panel_, "blk", [(b, (b + by * cores) % blocks) for b in range(blocks)])

    def side(name, panel_, *waits):
        with jax.named_scope(name):
            return lax.ppermute(after(panel_, *waits), "blk", [(b, b ^ 1) for b in range(blocks)])

    mean = jnp.broadcast_to(after(gene_mean, packed[0][0]), (8, panel))

    order = sorted(range(1, types), key=lambda j: (j == 3, j == 1, j))
    left, own, far, before = None, None, [], None
    for k in range(chunks):
        arrived = [packed[k][0]]
        for j in order:
            block = packed[k][j]
            if k:
                block = after(block, before[len(arrived)])
            with jax.named_scope(f"cells_{j}_chunk_{k}"):
                arrived.append(swap(block, j))
        before = list(arrived)
        if k >= 2:
            arrived[0] = after(arrived[0], *far[k - 2])
        if k == 0:
            first = arrived
        gather = []
        if k == chunks - 1 and k > 1:
            gather = [[got[d] for got in far[: k - 1]] for d in range(chips - 1)]
        scaled, left, count, own, *joined = standardize(
            types, cap, mean, starts[k], arrived, first, left, own, gather
        )
        if k < chunks - 1:
            with jax.named_scope(f"far_{k}"):
                far.append([across(scaled, d) for d in range(1, chips)])

    multiply = functools.partial(gram, blocks, cores, count, left)
    last = chunks - 1
    near = side("near", own)
    joined_near = [[side("far_near", p)] for p in joined] or [[]] * (chips - 1)
    joined = [[p] for p in joined] or [[]] * (chips - 1)
    out = multiply([([own], (0, 0, 0))], None, brief)
    final = [across(after(scaled, out), d) for d in range(1, chips)]
    second = [side(f"far_near_{last - 1}", p, own) for p in far[last - 1]]
    groups = [([*p, far[last - 1][i]], (i + 1, 0, 0)) for i, p in enumerate(joined)]
    out = multiply(groups, out, lengthy)
    groups = [([near], (0, 1, 0))]
    groups += [([*p, second[i]], (i + 1, 1, 0)) for i, p in enumerate(joined_near)]
    out = multiply(groups, out, brief)
    final_near = [side(f"far_near_{last}", p, out) for p in final]
    edge = starts[last]
    out = multiply([([p], (d, 0, edge)) for d, p in enumerate(final, 1)], out, brief)
    return multiply([([p], (d, 1, edge)) for d, p in enumerate(final_near, 1)], out, brief)


def solution(mesh):
    placed = (
        P(("parts", "cells"), "blk"),
        P(("parts", "cells")),
        P(("parts", "cells")),
        P(("parts", "blk")),
    )
    return jax.shard_map(
        shards,
        mesh=mesh,
        in_specs=placed,
        out_specs=P(("parts", "cells"), "blk", None),
        check_vma=False,
    )
```

```python
import functools

import jax
import jax.numpy as jnp
from jax import lax
from jax.experimental import pallas as pl
from jax.experimental.pallas import tpu as pltpu
from jax.sharding import PartitionSpec as P

dispersion = 100.0
epsilon = 1e-05
TILE = 16
VMEM = 16 * 1024 * 1024

brief = pl.CostEstimate(flops=1024, bytes_accessed=1024, transcendentals=0)
lengthy = pl.CostEstimate(flops=2 * 10**10, bytes_accessed=1024, transcendentals=0)
whole = pl.BlockSpec(memory_space=pltpu.VMEM)
anywhere = pl.BlockSpec(memory_space=pl.ANY)


def pack_kernel(types, cap, widths, type_ref, factor_ref, expr_ref, *outs):
    rows = expr_ref.shape[0]
    home = lax.axis_index("cells")
    kind = type_ref[...].reshape(1, rows)
    rel = jnp.bitwise_xor(kind, home)
    lines = max(types, 8)
    hot = lax.broadcasted_iota(jnp.int32, (lines, rows), 0) == rel
    hot_f = jnp.where(hot, 1.0, 0.0)
    upper = jnp.where(
        lax.broadcasted_iota(jnp.int32, (rows, rows), 0)
        <= lax.broadcasted_iota(jnp.int32, (rows, rows), 1),
        1.0,
        0.0,
    ).astype(jnp.bfloat16)
    running = jnp.dot(hot_f.astype(jnp.bfloat16), upper, preferred_element_type=jnp.float32)
    rank = jnp.sum(hot_f * running, axis=0, keepdims=True) - 1.0
    slot = rel * cap + rank.astype(jnp.int32)
    factor = factor_ref[...].astype(jnp.float32).reshape(1, rows)
    factor = jnp.broadcast_to(factor, (TILE, rows)).astype(jnp.bfloat16)
    values = expr_ref[...]
    for j in range(types):
        place = jnp.where(
            lax.broadcasted_iota(jnp.int32, (cap, rows), 0) + j * cap == slot, 1.0, 0.0
        ).astype(jnp.bfloat16)
        block = jnp.dot(place, values, preferred_element_type=jnp.float32).astype(jnp.bfloat16)
        start = 0
        for k, width in enumerate(widths):
            outs[k * types + j][0:cap, :] = block[:, start : start + width]
            start += width
        line = lax.dot_general(
            factor, place, (((1,), (1,)), ((), ())), preferred_element_type=jnp.float32
        )
        row = lax.broadcasted_iota(jnp.int32, (TILE, 1), 0)
        width = widths[0]
        tail = jnp.zeros((TILE, min(width, cap)), jnp.float32)
        for i in range(pl.cdiv(cap, width)):
            tail = jnp.where(row == i, line[:, i * width : min((i + 1) * width, cap)], tail)
        outs[j][cap : cap + TILE, 0 : min(width, cap)] = tail.astype(jnp.bfloat16)


def pack(types, cap, widths, cell_type, size_factor, expression):
    rows = expression.shape[0]
    shapes = [
        jax.ShapeDtypeStruct((cap + (TILE if k == 0 else 0), width), jnp.bfloat16)
        for k, width in enumerate(widths)
        for _ in range(types)
    ]
    flat = pl.pallas_call(
        functools.partial(pack_kernel, types, cap, widths),
        out_shape=shapes,
        in_specs=[whole] * 3,
        out_specs=[whole] * len(shapes),
        compiler_params=pltpu.CompilerParams(vmem_limit_bytes=VMEM),
        cost_estimate=brief,
        name="pack",
    )(cell_type, size_factor, expression)
    return [flat[k * types : (k + 1) * types] for k in range(len(widths))]


def standardize_kernel(types, cap, lead, separate, start, gathered, mean_ref, *refs):
    blocks = refs[:types]
    tails = refs[types : 2 * types] if separate else blocks
    base = 0 if separate else cap
    refs = refs[2 * types :] if separate else refs[types:]
    work, turned, sems = refs[-3:]
    if gathered:
        scaled_ref, turned_ref, count_ref, all_ref, *joined_refs = refs[-7 - gathered[0] : -3]
    else:
        scaled_ref, turned_ref, count_ref, all_ref = refs[-7:-3]
        joined_refs = []
    copies = []
    if gathered:
        sources = refs[: len(gathered[1])]
        for source, (joined, column) in zip(sources, gathered[1]):
            spot = joined_refs[joined].at[:, pl.ds(column, source.shape[1])]
            copies.append(pltpu.make_async_copy(source, spot, sems.at[2 + len(copies)]))
            copies[-1].start()
    width = work.shape[1]
    mean = mean_ref[0:1, start : start + width]
    piece = min(lead, cap)
    total = jnp.zeros((1, width), jnp.float32)
    count = jnp.zeros((1, 1), jnp.float32)
    alive = []
    for j in range(types):
        column = jnp.zeros((cap, 1), jnp.float32)
        for i in range(pl.cdiv(cap, lead)):
            line = tails[j][base : base + TILE, 0:piece].astype(jnp.float32)[i : i + 1, :]
            diagonal = (
                lax.broadcasted_iota(jnp.int32, (cap, piece), 0)
                == lax.broadcasted_iota(jnp.int32, (cap, piece), 1) + i * lead
            )
            column += jnp.sum(jnp.where(diagonal, line, 0.0), axis=1, keepdims=True)
        live = column > 0.0
        alive.append(live)
        count += jnp.sum(jnp.where(live, 1.0, 0.0), axis=0, keepdims=True)
        expected = jnp.where(live, column * mean, 1.0)
        values = blocks[j][0:cap, :].astype(jnp.float32)
        residual = jnp.where(
            live,
            (values - expected) * lax.rsqrt(expected + expected * expected * (1.0 / dispersion)),
            0.0,
        )
        work[j * cap : (j + 1) * cap, :] = residual
        total += jnp.sum(residual, axis=0, keepdims=True)
    center = total / count
    square = jnp.zeros((1, width), jnp.float32)
    for j in range(types):
        centered = jnp.where(alive[j], work[j * cap : (j + 1) * cap, :] - center, 0.0)
        work[j * cap : (j + 1) * cap, :] = centered
        square += jnp.sum(centered * centered, axis=0, keepdims=True)
    scale = lax.rsqrt(square / count + epsilon)
    for j in range(types):
        scaled = work[j * cap : (j + 1) * cap, :] * scale
        scaled_ref[j * cap : (j + 1) * cap, :] = scaled.astype(jnp.bfloat16)
        work[j * cap : (j + 1) * cap, :] = scaled
    slots = types * cap
    columns = pl.ds(start, width)
    copies.append(pltpu.make_async_copy(scaled_ref, all_ref.at[:, columns], sems.at[0]))
    copies[-1].start()
    turned[...] = jnp.transpose(work[...]).astype(jnp.bfloat16)
    copies.append(pltpu.make_async_copy(turned, turned_ref.at[columns, :], sems.at[1]))
    copies[-1].start()
    for copy in copies:
        copy.wait()
    count_ref[...] = jnp.broadcast_to(count, count_ref.shape)


def standardize(types, cap, mean, start, blocks, first, left, own, gather):
    lead, width = first[0].shape[1], blocks[0].shape[1]
    panel = mean.shape[1]
    separate = first is not blocks
    slots = types * cap
    specs = [whole] * (1 + types)
    args = [mean, *blocks]
    if separate:
        specs += [pl.BlockSpec((TILE, lead), lambda i: (cap // TILE, 0))] * types
        args += list(first)
    gathered, shapes = [], []
    for i, panels in enumerate(gather):
        column = 0
        for array in panels:
            gathered.append((i, column))
            column += array.shape[1]
            specs.append(whole)
            args.append(array)
        shapes.append(jax.ShapeDtypeStruct((slots, column), jnp.bfloat16))
    aliases = {}
    for value, output in ((left, 1), (own, 3)):
        if value is not None:
            aliases[len(args)] = output
            specs.append(anywhere)
            args.append(value)
    return pl.pallas_call(
        functools.partial(
            standardize_kernel,
            types,
            cap,
            lead,
            separate,
            start,
            (len(gather), gathered) if gathered else None,
        ),
        grid=(1,),
        out_shape=[
            jax.ShapeDtypeStruct((slots, width), jnp.bfloat16),
            jax.ShapeDtypeStruct((panel, slots), jnp.bfloat16),
            jax.ShapeDtypeStruct((8, 128), jnp.float32),
            jax.ShapeDtypeStruct((slots, panel), jnp.bfloat16),
            *shapes,
        ],
        in_specs=specs,
        out_specs=[whole, anywhere, whole, anywhere] + [whole] * len(shapes),
        scratch_shapes=[
            pltpu.VMEM((slots, width), jnp.float32),
            pltpu.VMEM((width, slots), jnp.bfloat16),
            pltpu.SemaphoreType.DMA((2 + len(gathered),)),
        ],
        input_output_aliases=aliases,
        compiler_params=pltpu.CompilerParams(vmem_limit_bytes=VMEM),
        cost_estimate=lengthy,
        name="standardize",
    )(*args)


def gram_kernel(blocks, cores, strip, groups, arrays, count_ref, left_ref, *refs):
    sources = refs[:arrays]
    out_ref, joined, tile, join_sems, sems = refs[-5:]
    rows, slots = left_ref.shape
    inverse = 1.0 / count_ref[0:1, 0:1]
    me = lax.axis_index("blk")

    joins, column = [], 0
    for panels, _ in groups:
        joins.append([])
        if len(panels) > 1:
            for index in panels:
                width = sources[index].shape[1]
                spot = joined.at[:, pl.ds(column, width)]
                joins[-1].append((column, sources[index], spot))
                column += width
    sent = 0
    for parts in joins:
        for _, source, spot in parts:
            pltpu.make_async_copy(source, spot, join_sems.at[sent]).start()
            sent += 1
    stores, sent = [], 0
    for (panels, (chip, flip, first, *part)), parts in zip(groups, joins):
        for _, source, spot in parts:
            pltpu.make_async_copy(source, spot, join_sems.at[sent]).wait()
            sent += 1
        width = part[0] if part else sum(sources[index].shape[1] for index in panels)
        owner = lax.rem(me + (blocks - chip * cores), blocks)
        owner = jnp.bitwise_xor(owner, flip)
        column = pl.multiple_of(owner * rows + first, 128)
        for row in range(0, rows, strip):
            slot = len(stores) % 2
            if len(stores) >= 2:
                stores[-2].wait()
            if parts:
                right = joined[:, parts[0][0] : parts[0][0] + width]
            else:
                skip = first if part else 0
                right = sources[panels[0]][:, skip : skip + width]
            product = jnp.dot(
                left_ref[row : row + strip, :], right, preferred_element_type=jnp.float32
            )
            tile[slot, :, 0:width] = (product * inverse).astype(jnp.bfloat16)
            stores.append(
                pltpu.make_async_copy(
                    tile.at[slot, :, pl.ds(0, width)],
                    out_ref.at[0, pl.ds(row, strip), pl.ds(column, width)],
                    sems.at[slot],
                )
            )
            stores[-1].start()
    for store in stores[-2:]:
        store.wait()


def gram(blocks, cores, count, left, groups, before, cost):
    rows, slots = left.shape
    arrays, layout = [], []
    for panels, place in groups:
        layout.append((list(range(len(arrays), len(arrays) + len(panels))), place))
        arrays += panels
    joined = [array for panels, _ in groups if len(panels) > 1 for array in panels]
    widest = max(sum(array.shape[1] for array in panels) for panels, _ in groups)
    strip = min(rows, 512 if widest > 512 else 1024)
    args = [count, left, *arrays]
    specs = [whole] * len(args)
    if before is not None:
        args.append(before)
        specs.append(anywhere)
    return pl.pallas_call(
        functools.partial(gram_kernel, blocks, cores, strip, layout, len(arrays)),
        in_specs=specs,
        out_specs=anywhere,
        out_shape=jax.ShapeDtypeStruct((1, rows, rows * blocks), jnp.bfloat16),
        scratch_shapes=[
            pltpu.VMEM((slots, max(sum(array.shape[1] for array in joined), 128)), jnp.bfloat16),
            pltpu.VMEM((2, strip, widest), jnp.bfloat16),
            pltpu.SemaphoreType.DMA((max(len(joined), 1),)),
            pltpu.SemaphoreType.DMA((2,)),
        ],
        input_output_aliases={} if before is None else {len(args) - 1: 0},
        compiler_params=pltpu.CompilerParams(vmem_limit_bytes=VMEM),
        cost_estimate=cost,
        name="gram",
    )(*args)


def after(value, *others):
    return lax.optimization_barrier((value, *others))[0]


def shards(expression, cell_type, size_factor, gene_mean):
    types = lax.axis_size("cells")
    blocks = lax.axis_size("blk")
    shard_rows, panel = expression.shape
    cap = 2 * shard_rows // types
    assert types & (types - 1) == 0
    widths = [256] * (panel // 256)
    chunks = len(widths)
    starts = [sum(widths[:k]) for k in range(chunks)]
    cores = 2
    chips = blocks // cores
    window = 3

    packed = pack(types, cap, widths, cell_type, size_factor, expression)

    def swap(block, by):
        return lax.ppermute(block, "cells", [(s, s ^ by) for s in range(types)])

    def across(panel_, by):
        return lax.ppermute(panel_, "blk", [(b, (b + by * cores) % blocks) for b in range(blocks)])

    def side(name, panel_, *waits):
        with jax.named_scope(name):
            return lax.ppermute(after(panel_, *waits), "blk", [(b, b ^ 1) for b in range(blocks)])

    mean = jnp.broadcast_to(after(gene_mean, packed[0][0]), (8, panel))

    order = sorted(range(1, types), key=lambda j: (j == 3, j == 1, j))
    left, own, far, before = None, None, [], None
    for k in range(chunks):
        arrived = [packed[k][0]]
        for j in order:
            block = packed[k][j]
            if k:
                block = after(block, before[len(arrived)], *([mean] if k == 1 else []))
            with jax.named_scope(f"cells_{j}_chunk_{k}"):
                arrived.append(swap(block, j))
        before = list(arrived)
        if k >= 2:
            arrived[0] = after(arrived[0], *far[k - 2])
        if k == 0:
            first = arrived
        gather = []
        if k == chunks - 1 and k > 1:
            gather = [[got[d] for got in far[: k - 1]] for d in range(chips - 1)]
        scaled, left, count, own, *joined = standardize(
            types, cap, mean, starts[k], arrived, first, left, own, gather
        )
        if k < chunks - 1:
            with jax.named_scope(f"far_{k}"):
                far.append([across(scaled, d) for d in range(1, chips)])

    multiply = functools.partial(gram, blocks, cores, count, left)
    last = chunks - 1
    near = side("near", own)
    joined_near = [[side("far_near", p)] for p in joined] or [[]] * (chips - 1)
    joined = [[p] for p in joined] or [[]] * (chips - 1)
    half = panel // 2
    out = multiply([([own], (0, 0, 0, half))], None, brief)
    final = [across(after(scaled, out), d) for d in range(1, chips)]
    second = [side(f"far_near_{last - 1}", p, own) for p in far[last - 1]]
    groups = [([own], (0, 0, half, half))]
    groups += [([*p, far[last - 1][i]], (i + 1, 0, 0)) for i, p in enumerate(joined)]
    out = multiply(groups, out, lengthy)
    groups = [([near], (0, 1, 0))]
    groups += [([*p, second[i]], (i + 1, 1, 0)) for i, p in enumerate(joined_near)]
    out = multiply(groups, out, brief)
    final_near = [side(f"far_near_{last}", p, out) for p in final]
    edge = starts[last]
    out = multiply([([p], (d, 0, edge)) for d, p in enumerate(final, 1)], out, brief)
    return multiply([([p], (d, 1, edge)) for d, p in enumerate(final_near, 1)], out, brief)


def solution(mesh):
    placed = (
        P(("parts", "cells"), "blk"),
        P(("parts", "cells")),
        P(("parts", "cells")),
        P(("parts", "blk")),
    )
    return jax.shard_map(
        shards,
        mesh=mesh,
        in_specs=placed,
        out_specs=P(("parts", "cells"), "blk", None),
        check_vma=False,
    )
```

```python
import functools

import jax
import jax.numpy as jnp
from jax import lax
from jax.experimental import pallas as pl
from jax.experimental.pallas import tpu as pltpu
from jax.sharding import PartitionSpec as P

dispersion = 100.0
epsilon = 1e-05
TILE = 16
VMEM = 16 * 1024 * 1024

brief = pl.CostEstimate(flops=1024, bytes_accessed=1024, transcendentals=0)
lengthy = pl.CostEstimate(flops=2 * 10**10, bytes_accessed=1024, transcendentals=0)
whole = pl.BlockSpec(memory_space=pltpu.VMEM)
anywhere = pl.BlockSpec(memory_space=pl.ANY)


def pack_kernel(types, cap, widths, type_ref, factor_ref, expr_ref, *outs):
    rows = expr_ref.shape[0]
    home = lax.axis_index("cells")
    kind = type_ref[...].reshape(1, rows)
    rel = jnp.bitwise_xor(kind, home)
    lines = max(types, 8)
    hot = lax.broadcasted_iota(jnp.int32, (lines, rows), 0) == rel
    hot_f = jnp.where(hot, 1.0, 0.0)
    upper = jnp.where(
        lax.broadcasted_iota(jnp.int32, (rows, rows), 0)
        <= lax.broadcasted_iota(jnp.int32, (rows, rows), 1),
        1.0,
        0.0,
    ).astype(jnp.bfloat16)
    running = jnp.dot(hot_f.astype(jnp.bfloat16), upper, preferred_element_type=jnp.float32)
    rank = jnp.sum(hot_f * running, axis=0, keepdims=True) - 1.0
    slot = rel * cap + rank.astype(jnp.int32)
    factor = factor_ref[...].astype(jnp.float32).reshape(1, rows)
    factor = jnp.broadcast_to(factor, (TILE, rows)).astype(jnp.bfloat16)
    values = expr_ref[...]
    for j in range(types):
        place = jnp.where(
            lax.broadcasted_iota(jnp.int32, (cap, rows), 0) + j * cap == slot, 1.0, 0.0
        ).astype(jnp.bfloat16)
        block = jnp.dot(place, values, preferred_element_type=jnp.float32).astype(jnp.bfloat16)
        start = 0
        for k, width in enumerate(widths):
            outs[k * types + j][0:cap, :] = block[:, start : start + width]
            start += width
        line = lax.dot_general(
            factor, place, (((1,), (1,)), ((), ())), preferred_element_type=jnp.float32
        )
        row = lax.broadcasted_iota(jnp.int32, (TILE, 1), 0)
        width = widths[0]
        tail = jnp.zeros((TILE, min(width, cap)), jnp.float32)
        for i in range(pl.cdiv(cap, width)):
            tail = jnp.where(row == i, line[:, i * width : min((i + 1) * width, cap)], tail)
        outs[j][cap : cap + TILE, 0 : min(width, cap)] = tail.astype(jnp.bfloat16)


def pack(types, cap, widths, cell_type, size_factor, expression):
    rows = expression.shape[0]
    shapes = [
        jax.ShapeDtypeStruct((cap + (TILE if k == 0 else 0), width), jnp.bfloat16)
        for k, width in enumerate(widths)
        for _ in range(types)
    ]
    flat = pl.pallas_call(
        functools.partial(pack_kernel, types, cap, widths),
        out_shape=shapes,
        in_specs=[whole] * 3,
        out_specs=[whole] * len(shapes),
        compiler_params=pltpu.CompilerParams(vmem_limit_bytes=VMEM),
        cost_estimate=brief,
        name="pack",
    )(cell_type, size_factor, expression)
    return [flat[k * types : (k + 1) * types] for k in range(len(widths))]


def standardize_kernel(types, cap, lead, separate, start, gathered, mean_ref, *refs):
    blocks = refs[:types]
    tails = refs[types : 2 * types] if separate else blocks
    base = 0 if separate else cap
    refs = refs[2 * types :] if separate else refs[types:]
    work, turned, sems = refs[-3:]
    if gathered:
        scaled_ref, turned_ref, count_ref, all_ref, *joined_refs = refs[-7 - gathered[0] : -3]
    else:
        scaled_ref, turned_ref, count_ref, all_ref = refs[-7:-3]
        joined_refs = []
    copies = []
    if gathered:
        sources = refs[: len(gathered[1])]
        for source, (joined, column) in zip(sources, gathered[1]):
            spot = joined_refs[joined].at[:, pl.ds(column, source.shape[1])]
            copies.append(pltpu.make_async_copy(source, spot, sems.at[2 + len(copies)]))
            copies[-1].start()
    width = work.shape[1]
    mean = mean_ref[0:1, start : start + width]
    piece = min(lead, cap)
    total = jnp.zeros((1, width), jnp.float32)
    count = jnp.zeros((1, 1), jnp.float32)
    alive = []
    for j in range(types):
        column = jnp.zeros((cap, 1), jnp.float32)
        for i in range(pl.cdiv(cap, lead)):
            line = tails[j][base : base + TILE, 0:piece].astype(jnp.float32)[i : i + 1, :]
            diagonal = (
                lax.broadcasted_iota(jnp.int32, (cap, piece), 0)
                == lax.broadcasted_iota(jnp.int32, (cap, piece), 1) + i * lead
            )
            column += jnp.sum(jnp.where(diagonal, line, 0.0), axis=1, keepdims=True)
        live = column > 0.0
        alive.append(live)
        count += jnp.sum(jnp.where(live, 1.0, 0.0), axis=0, keepdims=True)
        expected = jnp.where(live, column * mean, 1.0)
        values = blocks[j][0:cap, :].astype(jnp.float32)
        residual = jnp.where(
            live,
            (values - expected) * lax.rsqrt(expected + expected * expected * (1.0 / dispersion)),
            0.0,
        )
        work[j * cap : (j + 1) * cap, :] = residual
        total += jnp.sum(residual, axis=0, keepdims=True)
    center = total / count
    square = jnp.zeros((1, width), jnp.float32)
    for j in range(types):
        centered = jnp.where(alive[j], work[j * cap : (j + 1) * cap, :] - center, 0.0)
        work[j * cap : (j + 1) * cap, :] = centered
        square += jnp.sum(centered * centered, axis=0, keepdims=True)
    scale = lax.rsqrt(square / count + epsilon)
    for j in range(types):
        scaled = work[j * cap : (j + 1) * cap, :] * scale
        scaled_ref[j * cap : (j + 1) * cap, :] = scaled.astype(jnp.bfloat16)
        work[j * cap : (j + 1) * cap, :] = scaled
    slots = types * cap
    columns = pl.ds(start, width)
    copies.append(pltpu.make_async_copy(scaled_ref, all_ref.at[:, columns], sems.at[0]))
    copies[-1].start()
    turned[...] = jnp.transpose(work[...]).astype(jnp.bfloat16)
    copies.append(pltpu.make_async_copy(turned, turned_ref.at[columns, :], sems.at[1]))
    copies[-1].start()
    for copy in copies:
        copy.wait()
    count_ref[...] = jnp.broadcast_to(count, count_ref.shape)


def standardize(types, cap, mean, start, blocks, first, left, own, gather):
    lead, width = first[0].shape[1], blocks[0].shape[1]
    panel = mean.shape[1]
    separate = first is not blocks
    slots = types * cap
    specs = [whole] * (1 + types)
    args = [mean, *blocks]
    if separate:
        specs += [pl.BlockSpec((TILE, lead), lambda i: (cap // TILE, 0))] * types
        args += list(first)
    gathered, shapes = [], []
    for i, panels in enumerate(gather):
        column = 0
        for array in panels:
            gathered.append((i, column))
            column += array.shape[1]
            specs.append(whole)
            args.append(array)
        shapes.append(jax.ShapeDtypeStruct((slots, column), jnp.bfloat16))
    aliases = {}
    for value, output in ((left, 1), (own, 3)):
        if value is not None:
            aliases[len(args)] = output
            specs.append(anywhere)
            args.append(value)
    return pl.pallas_call(
        functools.partial(
            standardize_kernel,
            types,
            cap,
            lead,
            separate,
            start,
            (len(gather), gathered) if gathered else None,
        ),
        grid=(1,),
        out_shape=[
            jax.ShapeDtypeStruct((slots, width), jnp.bfloat16),
            jax.ShapeDtypeStruct((panel, slots), jnp.bfloat16),
            jax.ShapeDtypeStruct((8, 128), jnp.float32),
            jax.ShapeDtypeStruct((slots, panel), jnp.bfloat16),
            *shapes,
        ],
        in_specs=specs,
        out_specs=[whole, anywhere, whole, anywhere] + [whole] * len(shapes),
        scratch_shapes=[
            pltpu.VMEM((slots, width), jnp.float32),
            pltpu.VMEM((width, slots), jnp.bfloat16),
            pltpu.SemaphoreType.DMA((2 + len(gathered),)),
        ],
        input_output_aliases=aliases,
        compiler_params=pltpu.CompilerParams(vmem_limit_bytes=VMEM),
        cost_estimate=lengthy,
        name="standardize",
    )(*args)


def gram_kernel(blocks, cores, strip, groups, arrays, count_ref, left_ref, *refs):
    sources = refs[:arrays]
    out_ref, joined, tile, join_sems, sems = refs[-5:]
    rows, slots = left_ref.shape
    inverse = 1.0 / count_ref[0:1, 0:1]
    me = lax.axis_index("blk")

    joins, column = [], 0
    for panels, _ in groups:
        joins.append([])
        if len(panels) > 1:
            for index in panels:
                width = sources[index].shape[1]
                spot = joined.at[:, pl.ds(column, width)]
                joins[-1].append((column, sources[index], spot))
                column += width
    sent = 0
    for parts in joins:
        for _, source, spot in parts:
            pltpu.make_async_copy(source, spot, join_sems.at[sent]).start()
            sent += 1
    stores, sent = [], 0
    for (panels, (chip, flip, first, *part)), parts in zip(groups, joins):
        for _, source, spot in parts:
            pltpu.make_async_copy(source, spot, join_sems.at[sent]).wait()
            sent += 1
        width = part[0] if part else sum(sources[index].shape[1] for index in panels)
        low, high = part[1:] if part[1:] else (0, rows)
        owner = lax.rem(me + (blocks - chip * cores), blocks)
        owner = jnp.bitwise_xor(owner, flip)
        column = pl.multiple_of(owner * rows + first, 128)
        for row in range(low, high, strip):
            size = min(strip, high - row)
            slot = len(stores) % 2
            if len(stores) >= 2:
                stores[-2].wait()
            if parts:
                right = joined[:, parts[0][0] : parts[0][0] + width]
            else:
                skip = first if part else 0
                right = sources[panels[0]][:, skip : skip + width]
            product = jnp.dot(
                left_ref[row : row + size, :], right, preferred_element_type=jnp.float32
            )
            tile[slot, 0:size, 0:width] = (product * inverse).astype(jnp.bfloat16)
            stores.append(
                pltpu.make_async_copy(
                    tile.at[slot, pl.ds(0, size), pl.ds(0, width)],
                    out_ref.at[0, pl.ds(row, size), pl.ds(column, width)],
                    sems.at[slot],
                )
            )
            stores[-1].start()
    for store in stores[-2:]:
        store.wait()


def gram(blocks, cores, count, left, groups, before, cost):
    rows, slots = left.shape
    arrays, layout = [], []
    for panels, place in groups:
        layout.append((list(range(len(arrays), len(arrays) + len(panels))), place))
        arrays += panels
    joined = [array for panels, _ in groups if len(panels) > 1 for array in panels]
    widest = max(sum(array.shape[1] for array in panels) for panels, _ in groups)
    strip = min(rows, 512 if widest > 512 else 1024)
    args = [count, left, *arrays]
    specs = [whole] * len(args)
    if before is not None:
        args.append(before)
        specs.append(anywhere)
    return pl.pallas_call(
        functools.partial(gram_kernel, blocks, cores, strip, layout, len(arrays)),
        in_specs=specs,
        out_specs=anywhere,
        out_shape=jax.ShapeDtypeStruct((1, rows, rows * blocks), jnp.bfloat16),
        scratch_shapes=[
            pltpu.VMEM((slots, max(sum(array.shape[1] for array in joined), 128)), jnp.bfloat16),
            pltpu.VMEM((2, strip, widest), jnp.bfloat16),
            pltpu.SemaphoreType.DMA((max(len(joined), 1),)),
            pltpu.SemaphoreType.DMA((2,)),
        ],
        input_output_aliases={} if before is None else {len(args) - 1: 0},
        compiler_params=pltpu.CompilerParams(vmem_limit_bytes=VMEM),
        cost_estimate=cost,
        name="gram",
    )(*args)


def after(value, *others):
    return lax.optimization_barrier((value, *others))[0]


def shards(expression, cell_type, size_factor, gene_mean):
    types = lax.axis_size("cells")
    blocks = lax.axis_size("blk")
    shard_rows, panel = expression.shape
    cap = 2 * shard_rows // types
    assert types & (types - 1) == 0
    widths = [256] * (panel // 256)
    chunks = len(widths)
    starts = [sum(widths[:k]) for k in range(chunks)]
    cores = 2
    chips = blocks // cores
    window = 3

    packed = pack(types, cap, widths, cell_type, size_factor, expression)

    def swap(block, by):
        return lax.ppermute(block, "cells", [(s, s ^ by) for s in range(types)])

    def across(panel_, by):
        return lax.ppermute(panel_, "blk", [(b, (b + by * cores) % blocks) for b in range(blocks)])

    def side(name, panel_, *waits):
        with jax.named_scope(name):
            return lax.ppermute(after(panel_, *waits), "blk", [(b, b ^ 1) for b in range(blocks)])

    mean = jnp.broadcast_to(after(gene_mean, packed[0][0]), (8, panel))

    order = sorted(range(1, types), key=lambda j: (j == 3, j == 1, j))
    left, own, out, far, before = None, None, None, [], None
    for k in range(chunks):
        arrived = [packed[k][0]]
        for j in order:
            block = packed[k][j]
            if k:
                block = after(block, before[len(arrived)], *([mean] if k == 1 else []))
            with jax.named_scope(f"cells_{j}_chunk_{k}"):
                arrived.append(swap(block, j))
        before = list(arrived)
        if k >= 2:
            arrived[0] = after(arrived[0], *far[k - 2])
        if k == 0:
            first = arrived
        gather = []
        if k == chunks - 1 and k > 1:
            groups = [([own], (0, 0, 0, starts[k], 0, starts[k]))]
            out = gram(blocks, cores, count, left, groups, None, brief)
            arrived[0] = after(arrived[0], out)
            gather = [[got[d] for got in far[: k - 1]] for d in range(chips - 1)]
        scaled, left, count, own, *joined = standardize(
            types, cap, mean, starts[k], arrived, first, left, own, gather
        )
        if k < chunks - 1:
            with jax.named_scope(f"far_{k}"):
                far.append([across(scaled, d) for d in range(1, chips)])

    multiply = functools.partial(gram, blocks, cores, count, left)
    last = chunks - 1
    near = side("near", own)
    joined_near = [[side("far_near", p)] for p in joined] or [[]] * (chips - 1)
    joined = [[p] for p in joined] or [[]] * (chips - 1)
    if out is None:
        out = multiply([([own], (0, 0, 0))], None, brief)
    else:
        edge = starts[last]
        groups = [
            ([own], (0, 0, 0, panel, edge, panel)),
            ([own], (0, 0, edge, panel - edge, 0, edge)),
        ]
        out = multiply(groups, out, brief)
    final = [across(after(scaled, out), d) for d in range(1, chips)]
    second = [side(f"far_near_{last - 1}", p, own) for p in far[last - 1]]
    groups = [([*p, far[last - 1][i]], (i + 1, 0, 0)) for i, p in enumerate(joined)]
    out = multiply(groups, out, lengthy)
    groups = [([near], (0, 1, 0))]
    groups += [([*p, second[i]], (i + 1, 1, 0)) for i, p in enumerate(joined_near)]
    out = multiply(groups, out, brief)
    final_near = [side(f"far_near_{last}", p, out) for p in final]
    edge = starts[last]
    out = multiply([([p], (d, 0, edge)) for d, p in enumerate(final, 1)], out, brief)
    return multiply([([p], (d, 1, edge)) for d, p in enumerate(final_near, 1)], out, brief)


def solution(mesh):
    placed = (
        P(("parts", "cells"), "blk"),
        P(("parts", "cells")),
        P(("parts", "cells")),
        P(("parts", "blk")),
    )
    return jax.shard_map(
        shards,
        mesh=mesh,
        in_specs=placed,
        out_specs=P(("parts", "cells"), "blk", None),
        check_vma=False,
    )
```

```python
import functools

import jax
import jax.numpy as jnp
from jax import lax
from jax.experimental import pallas as pl
from jax.experimental.pallas import tpu as pltpu
from jax.sharding import PartitionSpec as P

dispersion = 100.0
epsilon = 1e-05
TILE = 16
VMEM = 16 * 1024 * 1024

brief = pl.CostEstimate(flops=1024, bytes_accessed=1024, transcendentals=0)
lengthy = pl.CostEstimate(flops=2 * 10**10, bytes_accessed=1024, transcendentals=0)
whole = pl.BlockSpec(memory_space=pltpu.VMEM)
anywhere = pl.BlockSpec(memory_space=pl.ANY)


def pack_kernel(types, cap, widths, type_ref, factor_ref, expr_ref, *outs):
    rows = expr_ref.shape[0]
    home = lax.axis_index("cells")
    kind = type_ref[...].reshape(1, rows)
    rel = jnp.bitwise_xor(kind, home)
    lines = max(types, 8)
    hot = lax.broadcasted_iota(jnp.int32, (lines, rows), 0) == rel
    hot_f = jnp.where(hot, 1.0, 0.0)
    upper = jnp.where(
        lax.broadcasted_iota(jnp.int32, (rows, rows), 0)
        <= lax.broadcasted_iota(jnp.int32, (rows, rows), 1),
        1.0,
        0.0,
    ).astype(jnp.bfloat16)
    running = jnp.dot(hot_f.astype(jnp.bfloat16), upper, preferred_element_type=jnp.float32)
    rank = jnp.sum(hot_f * running, axis=0, keepdims=True) - 1.0
    slot = rel * cap + rank.astype(jnp.int32)
    factor = factor_ref[...].astype(jnp.float32).reshape(1, rows)
    factor = jnp.broadcast_to(factor, (TILE, rows)).astype(jnp.bfloat16)
    values = expr_ref[...]
    for j in range(types):
        place = jnp.where(
            lax.broadcasted_iota(jnp.int32, (cap, rows), 0) + j * cap == slot, 1.0, 0.0
        ).astype(jnp.bfloat16)
        block = jnp.dot(place, values, preferred_element_type=jnp.float32).astype(jnp.bfloat16)
        start = 0
        for k, width in enumerate(widths):
            outs[k * types + j][0:cap, :] = block[:, start : start + width]
            start += width
        line = lax.dot_general(
            factor, place, (((1,), (1,)), ((), ())), preferred_element_type=jnp.float32
        )
        row = lax.broadcasted_iota(jnp.int32, (TILE, 1), 0)
        width = widths[0]
        tail = jnp.zeros((TILE, min(width, cap)), jnp.float32)
        for i in range(pl.cdiv(cap, width)):
            tail = jnp.where(row == i, line[:, i * width : min((i + 1) * width, cap)], tail)
        outs[j][cap : cap + TILE, 0 : min(width, cap)] = tail.astype(jnp.bfloat16)


def pack(types, cap, widths, cell_type, size_factor, expression):
    rows = expression.shape[0]
    shapes = [
        jax.ShapeDtypeStruct((cap + (TILE if k == 0 else 0), width), jnp.bfloat16)
        for k, width in enumerate(widths)
        for _ in range(types)
    ]
    flat = pl.pallas_call(
        functools.partial(pack_kernel, types, cap, widths),
        out_shape=shapes,
        in_specs=[whole] * 3,
        out_specs=[whole] * len(shapes),
        compiler_params=pltpu.CompilerParams(vmem_limit_bytes=VMEM),
        cost_estimate=brief,
        name="pack",
    )(cell_type, size_factor, expression)
    return [flat[k * types : (k + 1) * types] for k in range(len(widths))]


def factor_column(cap, lead, tail_ref, base):
    piece = min(lead, cap)
    column = jnp.zeros((cap, 1), jnp.float32)
    for i in range(pl.cdiv(cap, lead)):
        line = tail_ref[base : base + TILE, 0:piece].astype(jnp.float32)[i : i + 1, :]
        diagonal = (
            lax.broadcasted_iota(jnp.int32, (cap, piece), 0)
            == lax.broadcasted_iota(jnp.int32, (cap, piece), 1) + i * lead
        )
        column += jnp.sum(jnp.where(diagonal, line, 0.0), axis=1, keepdims=True)
    return column


def residuals(column, mean, levels):
    live = column > 0.0
    expected = jnp.where(live, column * mean, 1.0)
    return jnp.where(
        live,
        (levels.astype(jnp.float32) - expected)
        * lax.rsqrt(expected + expected * expected * (1.0 / dispersion)),
        0.0,
    )


def thirds(value):
    parts = []
    for _ in range(3):
        parts.append(value.astype(jnp.bfloat16).astype(jnp.float32))
        value = value - parts[-1]
    return parts


def standardize_kernel(types, cap, lead, separate, start, gathered, late, mean_ref, *refs):
    blocks = refs[:types]
    tails = refs[types : 2 * types] if separate else blocks
    base = 0 if separate else cap
    refs = refs[2 * types :] if separate else refs[types:]
    work, turned, sems = refs[-3:]
    more = (gathered[0] if gathered else 0) + (1 if late else 0)
    scaled_ref, turned_ref, count_ref, all_ref, *joined_refs = refs[-7 - more : -3]
    copies = []
    if gathered:
        sources = refs[: len(gathered[1])]
        for source, (joined, column) in zip(sources, gathered[1]):
            spot = joined_refs[joined].at[:, pl.ds(column, source.shape[1])]
            copies.append(pltpu.make_async_copy(source, spot, sems.at[2 + len(copies)]))
            copies[-1].start()
    width = work.shape[1]
    mean = mean_ref[0:1, start : start + width]
    total = jnp.zeros((1, width), jnp.float32)
    count = jnp.zeros((1, 1), jnp.float32)
    alive = []
    for j in range(types):
        column = factor_column(cap, lead, tails[j], base)
        live = column > 0.0
        alive.append(live)
        count += jnp.sum(jnp.where(live, 1.0, 0.0), axis=0, keepdims=True)
        residual = residuals(column, mean, blocks[j][0:cap, :])
        work[j * cap : (j + 1) * cap, :] = residual
        total += jnp.sum(residual, axis=0, keepdims=True)
    center = total / count
    square = jnp.zeros((1, width), jnp.float32)
    for j in range(types):
        centered = jnp.where(alive[j], work[j * cap : (j + 1) * cap, :] - center, 0.0)
        work[j * cap : (j + 1) * cap, :] = centered
        square += jnp.sum(centered * centered, axis=0, keepdims=True)
    scale = lax.rsqrt(square / count + epsilon)
    for j in range(types):
        scaled = work[j * cap : (j + 1) * cap, :] * scale
        scaled_ref[j * cap : (j + 1) * cap, :] = scaled.astype(jnp.bfloat16)
        work[j * cap : (j + 1) * cap, :] = scaled
    slots = types * cap
    if late:
        sent_ref = joined_refs[-1]
        sent_ref[0 : slots - cap, :] = scaled_ref[cap:slots, :]
        row = lax.broadcasted_iota(jnp.int32, (TILE, 1), 0)
        notes = jnp.zeros((TILE, width), jnp.float32)
        for i, part in enumerate(thirds(center) + thirds(scale) + thirds(mean)):
            notes = jnp.where(row == i, part, notes)
        sent_ref[slots - cap : slots - cap + TILE, :] = notes.astype(jnp.bfloat16)
    columns = pl.ds(start, width)
    copies.append(pltpu.make_async_copy(scaled_ref, all_ref.at[:, columns], sems.at[0]))
    copies[-1].start()
    turned[...] = jnp.transpose(work[...]).astype(jnp.bfloat16)
    copies.append(pltpu.make_async_copy(turned, turned_ref.at[columns, :], sems.at[1]))
    copies[-1].start()
    for copy in copies:
        copy.wait()
    count_ref[...] = jnp.broadcast_to(count, count_ref.shape)


def standardize(types, cap, mean, start, blocks, first, left, own, gather, late):
    lead, width = first[0].shape[1], blocks[0].shape[1]
    panel = mean.shape[1]
    separate = first is not blocks
    slots = types * cap
    specs = [whole] * (1 + types)
    args = [mean, *blocks]
    if separate:
        specs += [pl.BlockSpec((TILE, lead), lambda i: (cap // TILE, 0))] * types
        args += list(first)
    gathered, shapes = [], []
    for i, panels in enumerate(gather):
        column = 0
        for array in panels:
            gathered.append((i, column))
            column += array.shape[1]
            specs.append(whole)
            args.append(array)
        shapes.append(jax.ShapeDtypeStruct((slots, column), jnp.bfloat16))
    if late:
        shapes.append(jax.ShapeDtypeStruct((slots - cap + TILE, width), jnp.bfloat16))
    aliases = {}
    for value, output in ((left, 1), (own, 3)):
        if value is not None:
            aliases[len(args)] = output
            specs.append(anywhere)
            args.append(value)
    return pl.pallas_call(
        functools.partial(
            standardize_kernel,
            types,
            cap,
            lead,
            separate,
            start,
            (len(gather), gathered) if gathered else None,
            late,
        ),
        grid=(1,),
        out_shape=[
            jax.ShapeDtypeStruct((slots, width), jnp.bfloat16),
            jax.ShapeDtypeStruct((panel, slots), jnp.bfloat16),
            jax.ShapeDtypeStruct((8, 128), jnp.float32),
            jax.ShapeDtypeStruct((slots, panel), jnp.bfloat16),
            *shapes,
        ],
        in_specs=specs,
        out_specs=[whole, anywhere, whole, anywhere] + [whole] * len(shapes),
        scratch_shapes=[
            pltpu.VMEM((slots, width), jnp.float32),
            pltpu.VMEM((width, slots), jnp.bfloat16),
            pltpu.SemaphoreType.DMA((2 + len(gathered),)),
        ],
        input_output_aliases=aliases,
        compiler_params=pltpu.CompilerParams(vmem_limit_bytes=VMEM),
        cost_estimate=lengthy,
        name="standardize",
    )(*args)


def finish_kernel(cap, lead, sent_ref, local_ref, tail_ref, out_ref):
    rest = out_ref.shape[0] - cap
    out_ref[cap : cap + rest, :] = sent_ref[0:rest, :]
    notes = sent_ref[rest : rest + TILE, :].astype(jnp.float32)
    center, scale, mean = [
        notes[i : i + 1, :] + notes[i + 1 : i + 2, :] + notes[i + 2 : i + 3, :] for i in (0, 3, 6)
    ]
    column = factor_column(cap, lead, tail_ref, 0)
    residual = residuals(column, mean, local_ref[0:cap, :])
    centered = jnp.where(column > 0.0, residual - center, 0.0)
    out_ref[0:cap, :] = (centered * scale).astype(jnp.bfloat16)


def finish(types, cap, first, local, sent):
    lead, width = first.shape[1], sent.shape[1]
    return pl.pallas_call(
        functools.partial(finish_kernel, cap, lead),
        grid=(1,),
        out_shape=jax.ShapeDtypeStruct((types * cap, width), jnp.bfloat16),
        in_specs=[whole, whole, pl.BlockSpec((TILE, lead), lambda i: (cap // TILE, 0))],
        out_specs=whole,
        compiler_params=pltpu.CompilerParams(vmem_limit_bytes=VMEM),
        cost_estimate=brief,
        name="finish",
    )(sent, local, first)


def gram_kernel(blocks, cores, strip, groups, arrays, count_ref, left_ref, *refs):
    sources = refs[:arrays]
    out_ref, joined, tile, join_sems, sems = refs[-5:]
    rows, slots = left_ref.shape
    inverse = 1.0 / count_ref[0:1, 0:1]
    me = lax.axis_index("blk")

    joins, column = [], 0
    for panels, _ in groups:
        joins.append([])
        if len(panels) > 1:
            for index in panels:
                width = sources[index].shape[1]
                spot = joined.at[:, pl.ds(column, width)]
                joins[-1].append((column, sources[index], spot))
                column += width
    sent = 0
    for parts in joins:
        for _, source, spot in parts:
            pltpu.make_async_copy(source, spot, join_sems.at[sent]).start()
            sent += 1
    stores, sent = [], 0
    for (panels, (chip, flip, first, *part)), parts in zip(groups, joins):
        for _, source, spot in parts:
            pltpu.make_async_copy(source, spot, join_sems.at[sent]).wait()
            sent += 1
        width = part[0] if part else sum(sources[index].shape[1] for index in panels)
        low, high = part[1:] if part[1:] else (0, rows)
        owner = lax.rem(me + (blocks - chip * cores), blocks)
        owner = jnp.bitwise_xor(owner, flip)
        column = pl.multiple_of(owner * rows + first, 128)
        for row in range(low, high, strip):
            size = min(strip, high - row)
            slot = len(stores) % 2
            if len(stores) >= 2:
                stores[-2].wait()
            if parts:
                right = joined[:, parts[0][0] : parts[0][0] + width]
            else:
                skip = first if part else 0
                right = sources[panels[0]][:, skip : skip + width]
            product = jnp.dot(
                left_ref[row : row + size, :], right, preferred_element_type=jnp.float32
            )
            tile[slot, 0:size, 0:width] = (product * inverse).astype(jnp.bfloat16)
            stores.append(
                pltpu.make_async_copy(
                    tile.at[slot, pl.ds(0, size), pl.ds(0, width)],
                    out_ref.at[0, pl.ds(row, size), pl.ds(column, width)],
                    sems.at[slot],
                )
            )
            stores[-1].start()
    for store in stores[-2:]:
        store.wait()


def gram(blocks, cores, count, left, groups, before, cost):
    rows, slots = left.shape
    arrays, layout = [], []
    for panels, place in groups:
        layout.append((list(range(len(arrays), len(arrays) + len(panels))), place))
        arrays += panels
    joined = [array for panels, _ in groups if len(panels) > 1 for array in panels]
    widest = max(sum(array.shape[1] for array in panels) for panels, _ in groups)
    strip = min(rows, 512 if widest > 512 else 1024)
    args = [count, left, *arrays]
    specs = [whole] * len(args)
    if before is not None:
        args.append(before)
        specs.append(anywhere)
    return pl.pallas_call(
        functools.partial(gram_kernel, blocks, cores, strip, layout, len(arrays)),
        in_specs=specs,
        out_specs=anywhere,
        out_shape=jax.ShapeDtypeStruct((1, rows, rows * blocks), jnp.bfloat16),
        scratch_shapes=[
            pltpu.VMEM((slots, max(sum(array.shape[1] for array in joined), 128)), jnp.bfloat16),
            pltpu.VMEM((2, strip, widest), jnp.bfloat16),
            pltpu.SemaphoreType.DMA((max(len(joined), 1),)),
            pltpu.SemaphoreType.DMA((2,)),
        ],
        input_output_aliases={} if before is None else {len(args) - 1: 0},
        compiler_params=pltpu.CompilerParams(vmem_limit_bytes=VMEM),
        cost_estimate=cost,
        name="gram",
    )(*args)


def after(value, *others):
    return lax.optimization_barrier((value, *others))[0]


def shards(expression, cell_type, size_factor, gene_mean):
    types = lax.axis_size("cells")
    blocks = lax.axis_size("blk")
    shard_rows, panel = expression.shape
    cap = 2 * shard_rows // types
    assert types & (types - 1) == 0
    widths = [256] * (panel // 256)
    chunks = len(widths)
    starts = [sum(widths[:k]) for k in range(chunks)]
    cores = 2
    chips = blocks // cores
    window = 3

    packed = pack(types, cap, widths, cell_type, size_factor, expression)

    def swap(block, by):
        return lax.ppermute(block, "cells", [(s, s ^ by) for s in range(types)])

    def across(panel_, by):
        return lax.ppermute(panel_, "blk", [(b, (b + by * cores) % blocks) for b in range(blocks)])

    def side(name, panel_, *waits):
        with jax.named_scope(name):
            return lax.ppermute(after(panel_, *waits), "blk", [(b, b ^ 1) for b in range(blocks)])

    mean = jnp.broadcast_to(after(gene_mean, packed[0][0]), (8, panel))

    order = sorted(range(1, types), key=lambda j: (j == 3, j == 1, j))
    left, own, out, far, before = None, None, None, [], None
    for k in range(chunks):
        arrived = [packed[k][0]]
        for j in order:
            block = packed[k][j]
            if k:
                block = after(block, before[len(arrived)], *([mean] if k == 1 else []))
            with jax.named_scope(f"cells_{j}_chunk_{k}"):
                arrived.append(swap(block, j))
        before = list(arrived)
        if k == 1:
            with jax.named_scope("far_local"):
                local = [across(packed[-1][0], d) for d in range(1, chips)]
            arrived[0] = after(arrived[0], *local)
        if k >= 2:
            arrived[0] = after(arrived[0], *far[k - 2])
        if k == 0:
            first = arrived
        gather = []
        if k == chunks - 1 and k > 1:
            groups = [([own], (0, 0, 0, starts[k], 0, starts[k]))]
            out = gram(blocks, cores, count, left, groups, None, brief)
            arrived[0] = after(arrived[0], out)
            gather = [[got[d] for got in far[: k - 1]] for d in range(chips - 1)]
        scaled, left, count, own, *joined = standardize(
            types, cap, mean, starts[k], arrived, first, left, own, gather, k == chunks - 1
        )
        if k < chunks - 1:
            with jax.named_scope(f"far_{k}"):
                far.append([across(scaled, d) for d in range(1, chips)])

    multiply = functools.partial(gram, blocks, cores, count, left)
    last = chunks - 1
    near = side("near", own)
    sent = joined.pop()
    joined_near = [[side("far_near", p)] for p in joined] or [[]] * (chips - 1)
    joined = [[p] for p in joined] or [[]] * (chips - 1)
    if out is None:
        out = multiply([([own], (0, 0, 0))], None, brief)
    else:
        edge = starts[last]
        groups = [
            ([own], (0, 0, 0, panel, edge, panel)),
            ([own], (0, 0, edge, panel - edge, 0, edge)),
        ]
        out = multiply(groups, out, brief)
    final = [across(after(sent, out), d) for d in range(1, chips)]
    second = [side(f"far_near_{last - 1}", p, own) for p in far[last - 1]]
    groups = [([*p, far[last - 1][i]], (i + 1, 0, 0)) for i, p in enumerate(joined)]
    out = multiply(groups, out, lengthy)
    groups = [([near], (0, 1, 0))]
    groups += [([*p, second[i]], (i + 1, 1, 0)) for i, p in enumerate(joined_near)]
    out = multiply(groups, out, brief)
    final = [
        finish(types, cap, packed[0][0], near_by, after(got, out))
        for near_by, got in zip(local, final)
    ]
    final_near = [side(f"far_near_{last}", p) for p in final]
    edge = starts[last]
    out = multiply([([p], (d, 0, edge)) for d, p in enumerate(final, 1)], out, brief)
    return multiply([([p], (d, 1, edge)) for d, p in enumerate(final_near, 1)], out, brief)


def solution(mesh):
    placed = (
        P(("parts", "cells"), "blk"),
        P(("parts", "cells")),
        P(("parts", "cells")),
        P(("parts", "blk")),
    )
    return jax.shard_map(
        shards,
        mesh=mesh,
        in_specs=placed,
        out_specs=P(("parts", "cells"), "blk", None),
        check_vma=False,
    )
```

```python
import functools

import jax
import jax.numpy as jnp
from jax import lax
from jax.experimental import pallas as pl
from jax.experimental.pallas import tpu as pltpu
from jax.sharding import PartitionSpec as P

dispersion = 100.0
epsilon = 1e-05
TILE = 16
VMEM = 16 * 1024 * 1024

brief = pl.CostEstimate(flops=1024, bytes_accessed=1024, transcendentals=0)
lengthy = pl.CostEstimate(flops=2 * 10**10, bytes_accessed=1024, transcendentals=0)
whole = pl.BlockSpec(memory_space=pltpu.VMEM)
anywhere = pl.BlockSpec(memory_space=pl.ANY)


def pack_kernel(types, cap, widths, type_ref, factor_ref, expr_ref, *outs):
    rows = expr_ref.shape[0]
    home = lax.axis_index("cells")
    kind = type_ref[...].reshape(1, rows)
    rel = jnp.bitwise_xor(kind, home)
    lines = max(types, 8)
    hot = lax.broadcasted_iota(jnp.int32, (lines, rows), 0) == rel
    hot_f = jnp.where(hot, 1.0, 0.0)
    upper = jnp.where(
        lax.broadcasted_iota(jnp.int32, (rows, rows), 0)
        <= lax.broadcasted_iota(jnp.int32, (rows, rows), 1),
        1.0,
        0.0,
    ).astype(jnp.bfloat16)
    running = jnp.dot(hot_f.astype(jnp.bfloat16), upper, preferred_element_type=jnp.float32)
    rank = jnp.sum(hot_f * running, axis=0, keepdims=True) - 1.0
    slot = rel * cap + rank.astype(jnp.int32)
    factor = factor_ref[...].astype(jnp.float32).reshape(1, rows)
    factor = jnp.broadcast_to(factor, (TILE, rows)).astype(jnp.bfloat16)
    values = expr_ref[...]
    for j in range(types):
        place = jnp.where(
            lax.broadcasted_iota(jnp.int32, (cap, rows), 0) + j * cap == slot, 1.0, 0.0
        ).astype(jnp.bfloat16)
        block = jnp.dot(place, values, preferred_element_type=jnp.float32).astype(jnp.bfloat16)
        start = 0
        for k, width in enumerate(widths):
            outs[k * types + j][0:cap, :] = block[:, start : start + width]
            start += width
        line = lax.dot_general(
            factor, place, (((1,), (1,)), ((), ())), preferred_element_type=jnp.float32
        )
        row = lax.broadcasted_iota(jnp.int32, (TILE, 1), 0)
        width = widths[0]
        tail = jnp.zeros((TILE, min(width, cap)), jnp.float32)
        for i in range(pl.cdiv(cap, width)):
            tail = jnp.where(row == i, line[:, i * width : min((i + 1) * width, cap)], tail)
        outs[j][cap : cap + TILE, 0 : min(width, cap)] = tail.astype(jnp.bfloat16)


def pack(types, cap, widths, cell_type, size_factor, expression):
    rows = expression.shape[0]
    shapes = [
        jax.ShapeDtypeStruct((cap + (TILE if k == 0 else 0), width), jnp.bfloat16)
        for k, width in enumerate(widths)
        for _ in range(types)
    ]
    flat = pl.pallas_call(
        functools.partial(pack_kernel, types, cap, widths),
        out_shape=shapes,
        in_specs=[whole] * 3,
        out_specs=[whole] * len(shapes),
        compiler_params=pltpu.CompilerParams(vmem_limit_bytes=VMEM),
        cost_estimate=brief,
        name="pack",
    )(cell_type, size_factor, expression)
    return [flat[k * types : (k + 1) * types] for k in range(len(widths))]


def factor_column(cap, lead, tail_ref, base):
    piece = min(lead, cap)
    column = jnp.zeros((cap, 1), jnp.float32)
    for i in range(pl.cdiv(cap, lead)):
        line = tail_ref[base : base + TILE, 0:piece].astype(jnp.float32)[i : i + 1, :]
        diagonal = (
            lax.broadcasted_iota(jnp.int32, (cap, piece), 0)
            == lax.broadcasted_iota(jnp.int32, (cap, piece), 1) + i * lead
        )
        column += jnp.sum(jnp.where(diagonal, line, 0.0), axis=1, keepdims=True)
    return column


def residuals(column, mean, levels):
    live = column > 0.0
    expected = jnp.where(live, column * mean, 1.0)
    return jnp.where(
        live,
        (levels.astype(jnp.float32) - expected)
        * lax.rsqrt(expected + expected * expected * (1.0 / dispersion)),
        0.0,
    )


def thirds(value):
    parts = []
    for _ in range(3):
        parts.append(value.astype(jnp.bfloat16).astype(jnp.float32))
        value = value - parts[-1]
    return parts


def standardize_kernel(types, cap, lead, separate, start, gathered, late, mean_ref, *refs):
    blocks = refs[:types]
    tails = refs[types : 2 * types] if separate else blocks
    base = 0 if separate else cap
    refs = refs[2 * types :] if separate else refs[types:]
    work, turned, sems = refs[-3:]
    more = (gathered[0] if gathered else 0) + (1 if late else 0)
    scaled_ref, turned_ref, count_ref, all_ref, *joined_refs = refs[-7 - more : -3]
    copies = []
    if gathered:
        sources = refs[: len(gathered[1])]
        for source, (joined, column) in zip(sources, gathered[1]):
            spot = joined_refs[joined].at[:, pl.ds(column, source.shape[1])]
            copies.append(pltpu.make_async_copy(source, spot, sems.at[2 + len(copies)]))
            copies[-1].start()
    width = work.shape[1]
    mean = mean_ref[0:1, start : start + width]
    total = jnp.zeros((1, width), jnp.float32)
    count = jnp.zeros((1, 1), jnp.float32)
    alive = []
    for j in range(types):
        column = factor_column(cap, lead, tails[j], base)
        live = column > 0.0
        alive.append(live)
        count += jnp.sum(jnp.where(live, 1.0, 0.0), axis=0, keepdims=True)
        residual = residuals(column, mean, blocks[j][0:cap, :])
        work[j * cap : (j + 1) * cap, :] = residual
        total += jnp.sum(residual, axis=0, keepdims=True)
    center = total / count
    square = jnp.zeros((1, width), jnp.float32)
    for j in range(types):
        centered = jnp.where(alive[j], work[j * cap : (j + 1) * cap, :] - center, 0.0)
        work[j * cap : (j + 1) * cap, :] = centered
        square += jnp.sum(centered * centered, axis=0, keepdims=True)
    scale = lax.rsqrt(square / count + epsilon)
    for j in range(types):
        scaled = work[j * cap : (j + 1) * cap, :] * scale
        scaled_ref[j * cap : (j + 1) * cap, :] = scaled.astype(jnp.bfloat16)
        work[j * cap : (j + 1) * cap, :] = scaled
    slots = types * cap
    columns = pl.ds(start, width)
    copies.append(pltpu.make_async_copy(scaled_ref, all_ref.at[:, columns], sems.at[0]))
    copies[-1].start()
    turned[...] = jnp.transpose(work[...]).astype(jnp.bfloat16)
    copies.append(pltpu.make_async_copy(turned, turned_ref.at[columns, :], sems.at[1]))
    copies[-1].start()
    if late:
        sent_ref = joined_refs[-1]
        sent_ref[0 : slots - cap, :] = scaled_ref[cap:slots, :]
        row = lax.broadcasted_iota(jnp.int32, (TILE, 1), 0)
        notes = jnp.zeros((TILE, width), jnp.float32)
        for i, part in enumerate(thirds(center) + thirds(scale) + thirds(mean)):
            notes = jnp.where(row == i, part, notes)
        sent_ref[slots - cap : slots - cap + TILE, :] = notes.astype(jnp.bfloat16)
    for copy in copies:
        copy.wait()
    count_ref[...] = jnp.broadcast_to(count, count_ref.shape)


def standardize(types, cap, mean, start, blocks, first, left, own, gather, late):
    lead, width = first[0].shape[1], blocks[0].shape[1]
    panel = mean.shape[1]
    separate = first is not blocks
    slots = types * cap
    specs = [whole] * (1 + types)
    args = [mean, *blocks]
    if separate:
        specs += [pl.BlockSpec((TILE, lead), lambda i: (cap // TILE, 0))] * types
        args += list(first)
    gathered, shapes = [], []
    for i, panels in enumerate(gather):
        column = 0
        for array in panels:
            gathered.append((i, column))
            column += array.shape[1]
            specs.append(whole)
            args.append(array)
        shapes.append(jax.ShapeDtypeStruct((slots, column), jnp.bfloat16))
    if late:
        shapes.append(jax.ShapeDtypeStruct((slots - cap + TILE, width), jnp.bfloat16))
    aliases = {}
    for value, output in ((left, 1), (own, 3)):
        if value is not None:
            aliases[len(args)] = output
            specs.append(anywhere)
            args.append(value)
    return pl.pallas_call(
        functools.partial(
            standardize_kernel,
            types,
            cap,
            lead,
            separate,
            start,
            (len(gather), gathered) if gathered else None,
            late,
        ),
        grid=(1,),
        out_shape=[
            jax.ShapeDtypeStruct((slots, width), jnp.bfloat16),
            jax.ShapeDtypeStruct((panel, slots), jnp.bfloat16),
            jax.ShapeDtypeStruct((8, 128), jnp.float32),
            jax.ShapeDtypeStruct((slots, panel), jnp.bfloat16),
            *shapes,
        ],
        in_specs=specs,
        out_specs=[whole, anywhere, whole, anywhere] + [whole] * len(shapes),
        scratch_shapes=[
            pltpu.VMEM((slots, width), jnp.float32),
            pltpu.VMEM((width, slots), jnp.bfloat16),
            pltpu.SemaphoreType.DMA((2 + len(gathered),)),
        ],
        input_output_aliases=aliases,
        compiler_params=pltpu.CompilerParams(vmem_limit_bytes=VMEM),
        cost_estimate=lengthy,
        name="standardize",
    )(*args)


def finish_kernel(cap, lead, sent_ref, local_ref, tail_ref, out_ref):
    rest = out_ref.shape[0] - cap
    out_ref[cap : cap + rest, :] = sent_ref[0:rest, :]
    notes = sent_ref[rest : rest + TILE, :].astype(jnp.float32)
    center, scale, mean = [
        notes[i : i + 1, :] + notes[i + 1 : i + 2, :] + notes[i + 2 : i + 3, :] for i in (0, 3, 6)
    ]
    column = factor_column(cap, lead, tail_ref, 0)
    residual = residuals(column, mean, local_ref[0:cap, :])
    centered = jnp.where(column > 0.0, residual - center, 0.0)
    out_ref[0:cap, :] = (centered * scale).astype(jnp.bfloat16)


def finish(types, cap, first, local, sent):
    lead, width = first.shape[1], sent.shape[1]
    return pl.pallas_call(
        functools.partial(finish_kernel, cap, lead),
        grid=(1,),
        out_shape=jax.ShapeDtypeStruct((types * cap, width), jnp.bfloat16),
        in_specs=[whole, whole, pl.BlockSpec((TILE, lead), lambda i: (cap // TILE, 0))],
        out_specs=whole,
        compiler_params=pltpu.CompilerParams(vmem_limit_bytes=VMEM),
        cost_estimate=brief,
        name="finish",
    )(sent, local, first)


def gram_kernel(blocks, cores, strip, groups, arrays, count_ref, left_ref, *refs):
    sources = refs[:arrays]
    out_ref, joined, tile, join_sems, sems = refs[-5:]
    rows, slots = left_ref.shape
    inverse = 1.0 / count_ref[0:1, 0:1]
    me = lax.axis_index("blk")

    joins, column = [], 0
    for panels, _ in groups:
        joins.append([])
        if len(panels) > 1:
            for index in panels:
                width = sources[index].shape[1]
                spot = joined.at[:, pl.ds(column, width)]
                joins[-1].append((column, sources[index], spot))
                column += width
    sent = 0
    for parts in joins:
        for _, source, spot in parts:
            pltpu.make_async_copy(source, spot, join_sems.at[sent]).start()
            sent += 1
    stores, sent = [], 0
    for (panels, (chip, flip, first, *part)), parts in zip(groups, joins):
        for _, source, spot in parts:
            pltpu.make_async_copy(source, spot, join_sems.at[sent]).wait()
            sent += 1
        width = part[0] if part else sum(sources[index].shape[1] for index in panels)
        low, high = part[1:] if part[1:] else (0, rows)
        owner = lax.rem(me + (blocks - chip * cores), blocks)
        owner = jnp.bitwise_xor(owner, flip)
        column = pl.multiple_of(owner * rows + first, 128)
        for row in range(low, high, strip):
            size = min(strip, high - row)
            slot = len(stores) % 2
            if len(stores) >= 2:
                stores[-2].wait()
            if parts:
                right = joined[:, parts[0][0] : parts[0][0] + width]
            else:
                skip = first if part else 0
                right = sources[panels[0]][:, skip : skip + width]
            product = jnp.dot(
                left_ref[row : row + size, :], right, preferred_element_type=jnp.float32
            )
            tile[slot, 0:size, 0:width] = (product * inverse).astype(jnp.bfloat16)
            stores.append(
                pltpu.make_async_copy(
                    tile.at[slot, pl.ds(0, size), pl.ds(0, width)],
                    out_ref.at[0, pl.ds(row, size), pl.ds(column, width)],
                    sems.at[slot],
                )
            )
            stores[-1].start()
    for store in stores[-2:]:
        store.wait()


def gram(blocks, cores, count, left, groups, before, cost):
    rows, slots = left.shape
    arrays, layout = [], []
    for panels, place in groups:
        layout.append((list(range(len(arrays), len(arrays) + len(panels))), place))
        arrays += panels
    joined = [array for panels, _ in groups if len(panels) > 1 for array in panels]
    widest = max(sum(array.shape[1] for array in panels) for panels, _ in groups)
    strip = min(rows, 512 if widest > 512 else 1024)
    args = [count, left, *arrays]
    specs = [whole] * len(args)
    if before is not None:
        args.append(before)
        specs.append(anywhere)
    return pl.pallas_call(
        functools.partial(gram_kernel, blocks, cores, strip, layout, len(arrays)),
        in_specs=specs,
        out_specs=anywhere,
        out_shape=jax.ShapeDtypeStruct((1, rows, rows * blocks), jnp.bfloat16),
        scratch_shapes=[
            pltpu.VMEM((slots, max(sum(array.shape[1] for array in joined), 128)), jnp.bfloat16),
            pltpu.VMEM((2, strip, widest), jnp.bfloat16),
            pltpu.SemaphoreType.DMA((max(len(joined), 1),)),
            pltpu.SemaphoreType.DMA((2,)),
        ],
        input_output_aliases={} if before is None else {len(args) - 1: 0},
        compiler_params=pltpu.CompilerParams(vmem_limit_bytes=VMEM),
        cost_estimate=cost,
        name="gram",
    )(*args)


def after(value, *others):
    return lax.optimization_barrier((value, *others))[0]


def shards(expression, cell_type, size_factor, gene_mean):
    types = lax.axis_size("cells")
    blocks = lax.axis_size("blk")
    shard_rows, panel = expression.shape
    cap = 2 * shard_rows // types
    assert types & (types - 1) == 0
    widths = [256] * (panel // 256)
    chunks = len(widths)
    starts = [sum(widths[:k]) for k in range(chunks)]
    cores = 2
    chips = blocks // cores
    window = 3

    packed = pack(types, cap, widths, cell_type, size_factor, expression)

    def swap(block, by):
        return lax.ppermute(block, "cells", [(s, s ^ by) for s in range(types)])

    def across(panel_, by):
        return lax.ppermute(panel_, "blk", [(b, (b + by * cores) % blocks) for b in range(blocks)])

    def side(name, panel_, *waits):
        with jax.named_scope(name):
            return lax.ppermute(after(panel_, *waits), "blk", [(b, b ^ 1) for b in range(blocks)])

    mean = jnp.broadcast_to(after(gene_mean, packed[0][0]), (8, panel))

    order = sorted(range(1, types), key=lambda j: (j == 3, j == 1, j))
    left, own, out, far, before = None, None, None, [], None
    for k in range(chunks):
        arrived = [packed[k][0]]
        for j in order:
            block = packed[k][j]
            if k:
                block = after(block, before[len(arrived)], *([mean] if k == 1 else []))
            with jax.named_scope(f"cells_{j}_chunk_{k}"):
                arrived.append(swap(block, j))
        before = list(arrived)
        if k == 1:
            with jax.named_scope("far_local"):
                local = [across(packed[-1][0], d) for d in range(1, chips)]
            arrived[0] = after(arrived[0], *local)
        if k >= 2:
            arrived[0] = after(arrived[0], *far[k - 2])
        if k == 0:
            first = arrived
        gather = []
        if k == chunks - 1 and k > 1:
            groups = [([own], (0, 0, 0, starts[k], 0, starts[k]))]
            out = gram(blocks, cores, count, left, groups, None, brief)
            arrived[0] = after(arrived[0], out)
            gather = [[got[d] for got in far[: k - 1]] for d in range(chips - 1)]
        scaled, left, count, own, *joined = standardize(
            types, cap, mean, starts[k], arrived, first, left, own, gather, k == chunks - 1
        )
        if k < chunks - 1:
            with jax.named_scope(f"far_{k}"):
                far.append([across(scaled, d) for d in range(1, chips)])

    multiply = functools.partial(gram, blocks, cores, count, left)
    last = chunks - 1
    near = side("near", own)
    sent = joined.pop()
    joined_near = [[side("far_near", p)] for p in joined] or [[]] * (chips - 1)
    joined = [[p] for p in joined] or [[]] * (chips - 1)
    if out is None:
        out = multiply([([own], (0, 0, 0))], None, brief)
    else:
        edge = starts[last]
        groups = [
            ([own], (0, 0, 0, panel, edge, panel)),
            ([own], (0, 0, edge, panel - edge, 0, edge)),
        ]
        out = multiply(groups, out, brief)
    final = [across(after(sent, out), d) for d in range(1, chips)]
    second = [side(f"far_near_{last - 1}", p, own) for p in far[last - 1]]
    groups = [([*p, far[last - 1][i]], (i + 1, 0, 0)) for i, p in enumerate(joined)]
    out = multiply(groups, out, lengthy)
    groups = [([near], (0, 1, 0))]
    groups += [([*p, second[i]], (i + 1, 1, 0)) for i, p in enumerate(joined_near)]
    out = multiply(groups, out, brief)
    final = [
        finish(types, cap, packed[0][0], near_by, after(got, out))
        for near_by, got in zip(local, final)
    ]
    final_near = [side(f"far_near_{last}", p) for p in final]
    edge = starts[last]
    out = multiply([([p], (d, 0, edge)) for d, p in enumerate(final, 1)], out, brief)
    return multiply([([p], (d, 1, edge)) for d, p in enumerate(final_near, 1)], out, brief)


def solution(mesh):
    placed = (
        P(("parts", "cells"), "blk"),
        P(("parts", "cells")),
        P(("parts", "cells")),
        P(("parts", "blk")),
    )
    return jax.shard_map(
        shards,
        mesh=mesh,
        in_specs=placed,
        out_specs=P(("parts", "cells"), "blk", None),
        check_vma=False,
    )
```

```python
import functools

import jax
import jax.numpy as jnp
from jax import lax
from jax.experimental import pallas as pl
from jax.experimental.pallas import tpu as pltpu
from jax.sharding import PartitionSpec as P

dispersion = 100.0
epsilon = 1e-05
TILE = 16
VMEM = 16 * 1024 * 1024

brief = pl.CostEstimate(flops=1024, bytes_accessed=1024, transcendentals=0)
lengthy = pl.CostEstimate(flops=2 * 10**10, bytes_accessed=1024, transcendentals=0)
whole = pl.BlockSpec(memory_space=pltpu.VMEM)
anywhere = pl.BlockSpec(memory_space=pl.ANY)


def pack_kernel(types, cap, widths, type_ref, factor_ref, expr_ref, *outs):
    rows = expr_ref.shape[0]
    home = lax.axis_index("cells")
    kind = type_ref[...].reshape(1, rows)
    rel = jnp.bitwise_xor(kind, home)
    lines = max(types, 8)
    hot = lax.broadcasted_iota(jnp.int32, (lines, rows), 0) == rel
    hot_f = jnp.where(hot, 1.0, 0.0)
    upper = jnp.where(
        lax.broadcasted_iota(jnp.int32, (rows, rows), 0)
        <= lax.broadcasted_iota(jnp.int32, (rows, rows), 1),
        1.0,
        0.0,
    ).astype(jnp.bfloat16)
    running = jnp.dot(hot_f.astype(jnp.bfloat16), upper, preferred_element_type=jnp.float32)
    rank = jnp.sum(hot_f * running, axis=0, keepdims=True) - 1.0
    slot = rel * cap + rank.astype(jnp.int32)
    factor = factor_ref[...].astype(jnp.float32).reshape(1, rows)
    factor = jnp.broadcast_to(factor, (TILE, rows)).astype(jnp.bfloat16)
    values = expr_ref[...]
    for j in range(types):
        place = jnp.where(
            lax.broadcasted_iota(jnp.int32, (cap, rows), 0) + j * cap == slot, 1.0, 0.0
        ).astype(jnp.bfloat16)
        block = jnp.dot(place, values, preferred_element_type=jnp.float32).astype(jnp.bfloat16)
        start = 0
        for k, width in enumerate(widths):
            outs[k * types + j][0:cap, :] = block[:, start : start + width]
            start += width
        line = lax.dot_general(
            factor, place, (((1,), (1,)), ((), ())), preferred_element_type=jnp.float32
        )
        row = lax.broadcasted_iota(jnp.int32, (TILE, 1), 0)
        width = widths[0]
        tail = jnp.zeros((TILE, min(width, cap)), jnp.float32)
        for i in range(pl.cdiv(cap, width)):
            tail = jnp.where(row == i, line[:, i * width : min((i + 1) * width, cap)], tail)
        outs[j][cap : cap + TILE, 0 : min(width, cap)] = tail.astype(jnp.bfloat16)


def pack(types, cap, widths, cell_type, size_factor, expression):
    rows = expression.shape[0]
    shapes = [
        jax.ShapeDtypeStruct((cap + (TILE if k == 0 else 0), width), jnp.bfloat16)
        for k, width in enumerate(widths)
        for _ in range(types)
    ]
    flat = pl.pallas_call(
        functools.partial(pack_kernel, types, cap, widths),
        out_shape=shapes,
        in_specs=[whole] * 3,
        out_specs=[whole] * len(shapes),
        compiler_params=pltpu.CompilerParams(vmem_limit_bytes=VMEM),
        cost_estimate=brief,
        name="pack",
    )(cell_type, size_factor, expression)
    return [flat[k * types : (k + 1) * types] for k in range(len(widths))]


def factor_column(cap, lead, tail_ref, base):
    piece = min(lead, cap)
    column = jnp.zeros((cap, 1), jnp.float32)
    for i in range(pl.cdiv(cap, lead)):
        line = tail_ref[base : base + TILE, 0:piece].astype(jnp.float32)[i : i + 1, :]
        diagonal = (
            lax.broadcasted_iota(jnp.int32, (cap, piece), 0)
            == lax.broadcasted_iota(jnp.int32, (cap, piece), 1) + i * lead
        )
        column += jnp.sum(jnp.where(diagonal, line, 0.0), axis=1, keepdims=True)
    return column


def residuals(column, mean, levels):
    live = column > 0.0
    expected = jnp.where(live, column * mean, 1.0)
    return jnp.where(
        live,
        (levels.astype(jnp.float32) - expected)
        * lax.rsqrt(expected + expected * expected * (1.0 / dispersion)),
        0.0,
    )


def thirds(value):
    parts = []
    for _ in range(3):
        parts.append(value.astype(jnp.bfloat16).astype(jnp.float32))
        value = value - parts[-1]
    return parts


def standardize_kernel(types, cap, lead, separate, start, gathered, late, counts, mean_ref, *refs):
    blocks = refs[:types]
    tails = refs[types : 2 * types] if separate else blocks
    base = 0 if separate else cap
    refs = refs[2 * types :] if separate else refs[types:]
    outputs = 3 + counts + (gathered[0] if gathered else 0)
    outs, scratch = list(refs[: len(refs) - (4 if late else 3)]), refs[-4 if late else -3 :]
    outs = outs[len(outs) - outputs :]
    turned_ref, all_ref = outs[:2]
    count_ref = outs[2] if counts else None
    joined_refs = outs[2 + counts : outputs - 1]
    if late:
        sent_ref, (work, turned, sems, scaled_ref) = outs[-1], scratch
    else:
        scaled_ref, (work, turned, sems) = outs[-1], scratch
    copies = []
    if gathered:
        sources = refs[: len(gathered[1])]
        for source, (joined, column) in zip(sources, gathered[1]):
            spot = joined_refs[joined].at[:, pl.ds(column, source.shape[1])]
            copies.append(pltpu.make_async_copy(source, spot, sems.at[2 + len(copies)]))
            copies[-1].start()
    width = work.shape[1]
    mean = mean_ref[0:1, start : start + width]
    total = jnp.zeros((1, width), jnp.float32)
    count = jnp.zeros((1, 1), jnp.float32)
    alive = []
    for j in range(types):
        column = factor_column(cap, lead, tails[j], base)
        live = column > 0.0
        alive.append(live)
        count += jnp.sum(jnp.where(live, 1.0, 0.0), axis=0, keepdims=True)
        residual = residuals(column, mean, blocks[j][0:cap, :])
        work[j * cap : (j + 1) * cap, :] = residual
        total += jnp.sum(residual, axis=0, keepdims=True)
    center = total / count
    square = jnp.zeros((1, width), jnp.float32)
    for j in range(types):
        centered = jnp.where(alive[j], work[j * cap : (j + 1) * cap, :] - center, 0.0)
        work[j * cap : (j + 1) * cap, :] = centered
        square += jnp.sum(centered * centered, axis=0, keepdims=True)
    scale = lax.rsqrt(square / count + epsilon)
    for j in range(types):
        scaled = work[j * cap : (j + 1) * cap, :] * scale
        scaled_ref[j * cap : (j + 1) * cap, :] = scaled.astype(jnp.bfloat16)
        work[j * cap : (j + 1) * cap, :] = scaled
    slots = types * cap
    columns = pl.ds(start, width)
    copies.append(pltpu.make_async_copy(scaled_ref, all_ref.at[:, columns], sems.at[0]))
    copies[-1].start()
    turned[...] = jnp.transpose(work[...]).astype(jnp.bfloat16)
    copies.append(pltpu.make_async_copy(turned, turned_ref.at[columns, :], sems.at[1]))
    copies[-1].start()
    if late:
        sent_ref[0 : slots - cap, :] = scaled_ref[cap:slots, :]
        row = lax.broadcasted_iota(jnp.int32, (TILE, 1), 0)
        notes = jnp.zeros((TILE, width), jnp.float32)
        for i, part in enumerate(thirds(center) + thirds(scale) + thirds(mean)):
            notes = jnp.where(row == i, part, notes)
        sent_ref[slots - cap : slots - cap + TILE, :] = notes.astype(jnp.bfloat16)
    for copy in copies:
        copy.wait()
    if counts:
        count_ref[...] = jnp.broadcast_to(count, count_ref.shape)


def standardize(types, cap, mean, start, blocks, first, left, own, gather, late, counts):
    lead, width = first[0].shape[1], blocks[0].shape[1]
    panel = mean.shape[1]
    separate = first is not blocks
    slots = types * cap
    specs = [whole] * (1 + types)
    args = [mean, *blocks]
    if separate:
        specs += [pl.BlockSpec((TILE, lead), lambda i: (cap // TILE, 0))] * types
        args += list(first)
    shapes = [
        jax.ShapeDtypeStruct((panel, slots), jnp.bfloat16),
        jax.ShapeDtypeStruct((slots, panel), jnp.bfloat16),
    ]
    if counts:
        shapes.append(jax.ShapeDtypeStruct((8, 128), jnp.float32))
    gathered = []
    for i, panels in enumerate(gather):
        column = 0
        for array in panels:
            gathered.append((i, column))
            column += array.shape[1]
            specs.append(whole)
            args.append(array)
        shapes.append(jax.ShapeDtypeStruct((slots, column), jnp.bfloat16))
    rows = slots - cap + TILE if late else slots
    shapes.append(jax.ShapeDtypeStruct((rows, width), jnp.bfloat16))
    aliases = {}
    for value, output in ((left, 0), (own, 1)):
        if value is not None:
            aliases[len(args)] = output
            specs.append(anywhere)
            args.append(value)
    scratch = [
        pltpu.VMEM((slots, width), jnp.float32),
        pltpu.VMEM((width, slots), jnp.bfloat16),
        pltpu.SemaphoreType.DMA((2 + len(gathered),)),
    ]
    if late:
        scratch.append(pltpu.VMEM((slots, width), jnp.bfloat16))
    return pl.pallas_call(
        functools.partial(
            standardize_kernel,
            types,
            cap,
            lead,
            separate,
            start,
            (len(gather), gathered) if gathered else None,
            late,
            int(counts),
        ),
        grid=(1,),
        out_shape=shapes,
        in_specs=specs,
        out_specs=[anywhere, anywhere] + [whole] * (len(shapes) - 2),
        scratch_shapes=scratch,
        input_output_aliases=aliases,
        compiler_params=pltpu.CompilerParams(vmem_limit_bytes=VMEM),
        cost_estimate=lengthy,
        name="standardize",
    )(*args)


def finish_kernel(cap, lead, sent_ref, local_ref, tail_ref, out_ref):
    rest = out_ref.shape[0] - cap
    out_ref[cap : cap + rest, :] = sent_ref[0:rest, :]
    notes = sent_ref[rest : rest + TILE, :].astype(jnp.float32)
    center, scale, mean = [
        notes[i : i + 1, :] + notes[i + 1 : i + 2, :] + notes[i + 2 : i + 3, :] for i in (0, 3, 6)
    ]
    column = factor_column(cap, lead, tail_ref, 0)
    residual = residuals(column, mean, local_ref[0:cap, :])
    centered = jnp.where(column > 0.0, residual - center, 0.0)
    out_ref[0:cap, :] = (centered * scale).astype(jnp.bfloat16)


def finish(types, cap, first, local, sent):
    lead, width = first.shape[1], sent.shape[1]
    return pl.pallas_call(
        functools.partial(finish_kernel, cap, lead),
        grid=(1,),
        out_shape=jax.ShapeDtypeStruct((types * cap, width), jnp.bfloat16),
        in_specs=[whole, whole, pl.BlockSpec((TILE, lead), lambda i: (cap // TILE, 0))],
        out_specs=whole,
        compiler_params=pltpu.CompilerParams(vmem_limit_bytes=VMEM),
        cost_estimate=brief,
        name="finish",
    )(sent, local, first)


def gram_kernel(blocks, cores, strip, groups, arrays, count_ref, left_ref, *refs):
    sources = refs[:arrays]
    out_ref, joined, tile, join_sems, sems = refs[-5:]
    rows, slots = left_ref.shape
    inverse = 1.0 / count_ref[0:1, 0:1]
    me = lax.axis_index("blk")

    joins, column = [], 0
    for panels, _ in groups:
        joins.append([])
        if len(panels) > 1:
            for index in panels:
                width = sources[index].shape[1]
                spot = joined.at[:, pl.ds(column, width)]
                joins[-1].append((column, sources[index], spot))
                column += width
    sent = 0
    for parts in joins:
        for _, source, spot in parts:
            pltpu.make_async_copy(source, spot, join_sems.at[sent]).start()
            sent += 1
    stores, sent = [], 0
    for (panels, (chip, flip, first, *part)), parts in zip(groups, joins):
        for _, source, spot in parts:
            pltpu.make_async_copy(source, spot, join_sems.at[sent]).wait()
            sent += 1
        width = part[0] if part else sum(sources[index].shape[1] for index in panels)
        low, high = part[1:] if part[1:] else (0, rows)
        owner = lax.rem(me + (blocks - chip * cores), blocks)
        owner = jnp.bitwise_xor(owner, flip)
        column = pl.multiple_of(owner * rows + first, 128)
        for row in range(low, high, strip):
            size = min(strip, high - row)
            slot = len(stores) % 2
            if len(stores) >= 2:
                stores[-2].wait()
            if parts:
                right = joined[:, parts[0][0] : parts[0][0] + width]
            else:
                skip = first if part else 0
                right = sources[panels[0]][:, skip : skip + width]
            product = jnp.dot(
                left_ref[row : row + size, :], right, preferred_element_type=jnp.float32
            )
            tile[slot, 0:size, 0:width] = (product * inverse).astype(jnp.bfloat16)
            stores.append(
                pltpu.make_async_copy(
                    tile.at[slot, pl.ds(0, size), pl.ds(0, width)],
                    out_ref.at[0, pl.ds(row, size), pl.ds(column, width)],
                    sems.at[slot],
                )
            )
            stores[-1].start()
    for store in stores[-2:]:
        store.wait()


def gram(blocks, cores, count, left, groups, before, cost):
    rows, slots = left.shape
    arrays, layout = [], []
    for panels, place in groups:
        layout.append((list(range(len(arrays), len(arrays) + len(panels))), place))
        arrays += panels
    joined = [array for panels, _ in groups if len(panels) > 1 for array in panels]
    widest = max(sum(array.shape[1] for array in panels) for panels, _ in groups)
    strip = min(rows, 512 if widest > 512 else 1024)
    args = [count, left, *arrays]
    specs = [whole] * len(args)
    if before is not None:
        args.append(before)
        specs.append(anywhere)
    return pl.pallas_call(
        functools.partial(gram_kernel, blocks, cores, strip, layout, len(arrays)),
        in_specs=specs,
        out_specs=anywhere,
        out_shape=jax.ShapeDtypeStruct((1, rows, rows * blocks), jnp.bfloat16),
        scratch_shapes=[
            pltpu.VMEM((slots, max(sum(array.shape[1] for array in joined), 128)), jnp.bfloat16),
            pltpu.VMEM((2, strip, widest), jnp.bfloat16),
            pltpu.SemaphoreType.DMA((max(len(joined), 1),)),
            pltpu.SemaphoreType.DMA((2,)),
        ],
        input_output_aliases={} if before is None else {len(args) - 1: 0},
        compiler_params=pltpu.CompilerParams(vmem_limit_bytes=VMEM),
        cost_estimate=cost,
        name="gram",
    )(*args)


def after(value, *others):
    return lax.optimization_barrier((value, *others))[0]


def shards(expression, cell_type, size_factor, gene_mean):
    types = lax.axis_size("cells")
    blocks = lax.axis_size("blk")
    shard_rows, panel = expression.shape
    cap = 2 * shard_rows // types
    assert types & (types - 1) == 0
    widths = [256] * (panel // 256)
    chunks = len(widths)
    starts = [sum(widths[:k]) for k in range(chunks)]
    cores = 2
    chips = blocks // cores
    window = 3

    packed = pack(types, cap, widths, cell_type, size_factor, expression)

    def swap(block, by):
        return lax.ppermute(block, "cells", [(s, s ^ by) for s in range(types)])

    def across(panel_, by):
        return lax.ppermute(panel_, "blk", [(b, (b + by * cores) % blocks) for b in range(blocks)])

    def side(name, panel_, *waits):
        with jax.named_scope(name):
            return lax.ppermute(after(panel_, *waits), "blk", [(b, b ^ 1) for b in range(blocks)])

    mean = jnp.broadcast_to(after(gene_mean, packed[0][0]), (8, panel))

    order = sorted(range(1, types), key=lambda j: (j == 2, j == 1, -j))
    left, own, out, far, before = None, None, None, [], None
    for k in range(chunks):
        arrived = [packed[k][0]]
        for j in order:
            block = packed[k][j]
            if k:
                block = after(block, before[len(arrived)], *([mean] if k == 1 else []))
            with jax.named_scope(f"cells_{j}_chunk_{k}"):
                arrived.append(swap(block, j))
        before = list(arrived)
        if k == 1:
            with jax.named_scope("far_local"):
                local = [across(packed[-1][0], d) for d in range(1, chips)]
            arrived[0] = after(arrived[0], *local)
        if k >= 2:
            arrived[0] = after(arrived[0], *far[k - 2])
        if k == 0:
            first = arrived
        gather = []
        if k == chunks - 1 and k > 1:
            groups = [([own], (0, 0, 0, starts[k], 0, starts[k]))]
            out = gram(blocks, cores, count, left, groups, None, brief)
            arrived[0] = after(arrived[0], out)
            gather = [[got[d] for got in far[: k - 1]] for d in range(chips - 1)]
        counts, late = k == chunks - 2, k == chunks - 1
        left, own, *rest = standardize(
            types, cap, mean, starts[k], arrived, first, left, own, gather, late, counts
        )
        if counts:
            count = rest.pop(0)
        scaled, joined = rest[-1], rest[:-1]
        if k < chunks - 1:
            with jax.named_scope(f"far_{k}"):
                far.append([across(scaled, d) for d in range(1, chips)])

    multiply = functools.partial(gram, blocks, cores, count, left)
    last = chunks - 1
    near = side("near", own)
    sent = scaled
    joined_near = [[side("far_near", p)] for p in joined] or [[]] * (chips - 1)
    joined = [[p] for p in joined] or [[]] * (chips - 1)
    if out is None:
        out = multiply([([own], (0, 0, 0))], None, brief)
    else:
        edge = starts[last]
        groups = [
            ([own], (0, 0, 0, panel, edge, panel)),
            ([own], (0, 0, edge, panel - edge, 0, edge)),
        ]
        out = multiply(groups, out, brief)
    final = [across(after(sent, out), d) for d in range(1, chips)]
    second = [side(f"far_near_{last - 1}", p, own) for p in far[last - 1]]
    groups = [([*p, far[last - 1][i]], (i + 1, 0, 0)) for i, p in enumerate(joined)]
    out = multiply(groups, out, lengthy)
    groups = [([near], (0, 1, 0))]
    groups += [([*p, second[i]], (i + 1, 1, 0)) for i, p in enumerate(joined_near)]
    out = multiply(groups, out, brief)
    final = [
        finish(types, cap, packed[0][0], near_by, after(got, out))
        for near_by, got in zip(local, final)
    ]
    final_near = [side(f"far_near_{last}", p) for p in final]
    edge = starts[last]
    out = multiply([([p], (d, 0, edge)) for d, p in enumerate(final, 1)], out, brief)
    return multiply([([p], (d, 1, edge)) for d, p in enumerate(final_near, 1)], out, brief)


def solution(mesh):
    placed = (
        P(("parts", "cells"), "blk"),
        P(("parts", "cells")),
        P(("parts", "cells")),
        P(("parts", "blk")),
    )
    return jax.shard_map(
        shards,
        mesh=mesh,
        in_specs=placed,
        out_specs=P(("parts", "cells"), "blk", None),
        check_vma=False,
    )
```

```python
import functools

import jax
import jax.numpy as jnp
from jax import lax
from jax.experimental import pallas as pl
from jax.experimental.pallas import tpu as pltpu
from jax.sharding import PartitionSpec as P

dispersion = 100.0
epsilon = 1e-05
TILE = 16
VMEM = 16 * 1024 * 1024

brief = pl.CostEstimate(flops=1024, bytes_accessed=1024, transcendentals=0)
lengthy = pl.CostEstimate(flops=2 * 10**10, bytes_accessed=1024, transcendentals=0)
whole = pl.BlockSpec(memory_space=pltpu.VMEM)
anywhere = pl.BlockSpec(memory_space=pl.ANY)


def pack_kernel(types, cap, widths, type_ref, factor_ref, expr_ref, *outs):
    rows = expr_ref.shape[0]
    home = lax.axis_index("cells")
    kind = type_ref[...].reshape(1, rows)
    rel = jnp.bitwise_xor(kind, home)
    lines = max(types, 8)
    hot = lax.broadcasted_iota(jnp.int32, (lines, rows), 0) == rel
    hot_f = jnp.where(hot, 1.0, 0.0)
    upper = jnp.where(
        lax.broadcasted_iota(jnp.int32, (rows, rows), 0)
        <= lax.broadcasted_iota(jnp.int32, (rows, rows), 1),
        1.0,
        0.0,
    ).astype(jnp.bfloat16)
    running = jnp.dot(hot_f.astype(jnp.bfloat16), upper, preferred_element_type=jnp.float32)
    rank = jnp.sum(hot_f * running, axis=0, keepdims=True) - 1.0
    slot = rel * cap + rank.astype(jnp.int32)
    factor = factor_ref[...].astype(jnp.float32).reshape(1, rows)
    factor = jnp.broadcast_to(factor, (TILE, rows)).astype(jnp.bfloat16)
    values = expr_ref[...]
    for j in range(types):
        place = jnp.where(
            lax.broadcasted_iota(jnp.int32, (cap, rows), 0) + j * cap == slot, 1.0, 0.0
        ).astype(jnp.bfloat16)
        block = jnp.dot(place, values, preferred_element_type=jnp.float32).astype(jnp.bfloat16)
        start = 0
        for k, width in enumerate(widths):
            outs[k * types + j][0:cap, :] = block[:, start : start + width]
            start += width
        line = lax.dot_general(
            factor, place, (((1,), (1,)), ((), ())), preferred_element_type=jnp.float32
        )
        row = lax.broadcasted_iota(jnp.int32, (TILE, 1), 0)
        width = widths[0]
        tail = jnp.zeros((TILE, min(width, cap)), jnp.float32)
        for i in range(pl.cdiv(cap, width)):
            tail = jnp.where(row == i, line[:, i * width : min((i + 1) * width, cap)], tail)
        outs[j][cap : cap + TILE, 0 : min(width, cap)] = tail.astype(jnp.bfloat16)


def pack(types, cap, widths, cell_type, size_factor, expression):
    rows = expression.shape[0]
    shapes = [
        jax.ShapeDtypeStruct((cap + (TILE if k == 0 else 0), width), jnp.bfloat16)
        for k, width in enumerate(widths)
        for _ in range(types)
    ]
    flat = pl.pallas_call(
        functools.partial(pack_kernel, types, cap, widths),
        out_shape=shapes,
        in_specs=[whole] * 3,
        out_specs=[whole] * len(shapes),
        compiler_params=pltpu.CompilerParams(vmem_limit_bytes=VMEM),
        cost_estimate=brief,
        name="pack",
    )(cell_type, size_factor, expression)
    return [flat[k * types : (k + 1) * types] for k in range(len(widths))]


def factor_column(cap, lead, tail_ref, base):
    piece = min(lead, cap)
    column = jnp.zeros((cap, 1), jnp.float32)
    for i in range(pl.cdiv(cap, lead)):
        line = tail_ref[base : base + TILE, 0:piece].astype(jnp.float32)[i : i + 1, :]
        diagonal = (
            lax.broadcasted_iota(jnp.int32, (cap, piece), 0)
            == lax.broadcasted_iota(jnp.int32, (cap, piece), 1) + i * lead
        )
        column += jnp.sum(jnp.where(diagonal, line, 0.0), axis=1, keepdims=True)
    return column


def residuals(column, mean, levels):
    live = column > 0.0
    expected = jnp.where(live, column * mean, 1.0)
    return jnp.where(
        live,
        (levels.astype(jnp.float32) - expected)
        * lax.rsqrt(expected + expected * expected * (1.0 / dispersion)),
        0.0,
    )


def thirds(value):
    parts = []
    for _ in range(3):
        parts.append(value.astype(jnp.bfloat16).astype(jnp.float32))
        value = value - parts[-1]
    return parts


def standardize_kernel(types, cap, lead, separate, start, gathered, late, counts, mean_ref, *refs):
    blocks = refs[:types]
    tails = refs[types : 2 * types] if separate else blocks
    base = 0 if separate else cap
    refs = refs[2 * types :] if separate else refs[types:]
    outputs = 3 + counts + (gathered[0] if gathered else 0)
    outs, scratch = list(refs[: len(refs) - (4 if late else 3)]), refs[-4 if late else -3 :]
    outs = outs[len(outs) - outputs :]
    turned_ref, all_ref = outs[:2]
    count_ref = outs[2] if counts else None
    joined_refs = outs[2 + counts : outputs - 1]
    if late:
        sent_ref, (work, turned, sems, scaled_ref) = outs[-1], scratch
    else:
        scaled_ref, (work, turned, sems) = outs[-1], scratch
    copies = []
    if gathered:
        sources = refs[: len(gathered[1])]
        for source, (joined, column) in zip(sources, gathered[1]):
            spot = joined_refs[joined].at[:, pl.ds(column, source.shape[1])]
            copies.append(pltpu.make_async_copy(source, spot, sems.at[2 + len(copies)]))
            copies[-1].start()
    width = work.shape[1]
    mean = mean_ref[0:1, start : start + width]
    total = jnp.zeros((1, width), jnp.float32)
    count = jnp.zeros((1, 1), jnp.float32)
    alive = []
    for j in range(types):
        column = factor_column(cap, lead, tails[j], base)
        live = column > 0.0
        alive.append(live)
        count += jnp.sum(jnp.where(live, 1.0, 0.0), axis=0, keepdims=True)
        residual = residuals(column, mean, blocks[j][0:cap, :])
        work[j * cap : (j + 1) * cap, :] = residual
        total += jnp.sum(residual, axis=0, keepdims=True)
    center = total / count
    square = jnp.zeros((1, width), jnp.float32)
    for j in range(types):
        centered = jnp.where(alive[j], work[j * cap : (j + 1) * cap, :] - center, 0.0)
        work[j * cap : (j + 1) * cap, :] = centered
        square += jnp.sum(centered * centered, axis=0, keepdims=True)
    scale = lax.rsqrt(square / count + epsilon)
    for j in range(types):
        scaled = work[j * cap : (j + 1) * cap, :] * scale
        scaled_ref[j * cap : (j + 1) * cap, :] = scaled.astype(jnp.bfloat16)
        work[j * cap : (j + 1) * cap, :] = scaled
    slots = types * cap
    columns = pl.ds(start, width)
    copies.append(pltpu.make_async_copy(scaled_ref, all_ref.at[:, columns], sems.at[0]))
    copies[-1].start()
    turned[...] = jnp.transpose(work[...]).astype(jnp.bfloat16)
    copies.append(pltpu.make_async_copy(turned, turned_ref.at[columns, :], sems.at[1]))
    copies[-1].start()
    if late:
        sent_ref[0 : slots - cap, :] = scaled_ref[cap:slots, :]
        row = lax.broadcasted_iota(jnp.int32, (TILE, 1), 0)
        notes = jnp.zeros((TILE, width), jnp.float32)
        for i, part in enumerate(thirds(center) + thirds(scale) + thirds(mean)):
            notes = jnp.where(row == i, part, notes)
        sent_ref[slots - cap : slots - cap + TILE, :] = notes.astype(jnp.bfloat16)
    for copy in copies:
        copy.wait()
    if counts:
        count_ref[...] = jnp.broadcast_to(count, count_ref.shape)


def standardize(types, cap, mean, start, blocks, first, left, own, gather, late, counts):
    lead, width = first[0].shape[1], blocks[0].shape[1]
    panel = mean.shape[1]
    separate = first is not blocks
    slots = types * cap
    specs = [whole] * (1 + types)
    args = [mean, *blocks]
    if separate:
        specs += [pl.BlockSpec((TILE, lead), lambda i: (cap // TILE, 0))] * types
        args += list(first)
    shapes = [
        jax.ShapeDtypeStruct((panel, slots), jnp.bfloat16),
        jax.ShapeDtypeStruct((slots, panel), jnp.bfloat16),
    ]
    if counts:
        shapes.append(jax.ShapeDtypeStruct((8, 128), jnp.float32))
    gathered = []
    for i, panels in enumerate(gather):
        column = 0
        for array in panels:
            gathered.append((i, column))
            column += array.shape[1]
            specs.append(whole)
            args.append(array)
        shapes.append(jax.ShapeDtypeStruct((slots, column), jnp.bfloat16))
    rows = slots - cap + TILE if late else slots
    shapes.append(jax.ShapeDtypeStruct((rows, width), jnp.bfloat16))
    aliases = {}
    for value, output in ((left, 0), (own, 1)):
        if value is not None:
            aliases[len(args)] = output
            specs.append(anywhere)
            args.append(value)
    scratch = [
        pltpu.VMEM((slots, width), jnp.float32),
        pltpu.VMEM((width, slots), jnp.bfloat16),
        pltpu.SemaphoreType.DMA((2 + len(gathered),)),
    ]
    if late:
        scratch.append(pltpu.VMEM((slots, width), jnp.bfloat16))
    return pl.pallas_call(
        functools.partial(
            standardize_kernel,
            types,
            cap,
            lead,
            separate,
            start,
            (len(gather), gathered) if gathered else None,
            late,
            int(counts),
        ),
        grid=(1,),
        out_shape=shapes,
        in_specs=specs,
        out_specs=[anywhere, anywhere] + [whole] * (len(shapes) - 2),
        scratch_shapes=scratch,
        input_output_aliases=aliases,
        compiler_params=pltpu.CompilerParams(vmem_limit_bytes=VMEM),
        cost_estimate=lengthy,
        name="standardize",
    )(*args)


def finish_kernel(cap, lead, sent_ref, local_ref, tail_ref, out_ref):
    rest = out_ref.shape[0] - cap
    out_ref[cap : cap + rest, :] = sent_ref[0:rest, :]
    notes = sent_ref[rest : rest + TILE, :].astype(jnp.float32)
    center, scale, mean = [
        notes[i : i + 1, :] + notes[i + 1 : i + 2, :] + notes[i + 2 : i + 3, :] for i in (0, 3, 6)
    ]
    column = factor_column(cap, lead, tail_ref, 0)
    residual = residuals(column, mean, local_ref[0:cap, :])
    centered = jnp.where(column > 0.0, residual - center, 0.0)
    out_ref[0:cap, :] = (centered * scale).astype(jnp.bfloat16)


def finish(types, cap, first, local, sent):
    lead, width = first.shape[1], sent.shape[1]
    return pl.pallas_call(
        functools.partial(finish_kernel, cap, lead),
        grid=(1,),
        out_shape=jax.ShapeDtypeStruct((types * cap, width), jnp.bfloat16),
        in_specs=[whole, whole, pl.BlockSpec((TILE, lead), lambda i: (cap // TILE, 0))],
        out_specs=whole,
        compiler_params=pltpu.CompilerParams(vmem_limit_bytes=VMEM),
        cost_estimate=brief,
        name="finish",
    )(sent, local, first)


def gram_kernel(blocks, cores, strip, groups, arrays, count_ref, left_ref, *refs):
    sources = refs[:arrays]
    out_ref, joined, tile, join_sems, sems = refs[-5:]
    rows, slots = left_ref.shape
    inverse = 1.0 / count_ref[0:1, 0:1]
    me = lax.axis_index("blk")

    joins, column = [], 0
    for panels, _ in groups:
        joins.append([])
        if len(panels) > 1:
            for index in panels:
                width = sources[index].shape[1]
                spot = joined.at[:, pl.ds(column, width)]
                joins[-1].append((column, sources[index], spot))
                column += width
    sent = 0
    for parts in joins:
        for _, source, spot in parts:
            pltpu.make_async_copy(source, spot, join_sems.at[sent]).start()
            sent += 1
    stores, sent = [], 0
    for (panels, (chip, flip, first, *part)), parts in zip(groups, joins):
        for _, source, spot in parts:
            pltpu.make_async_copy(source, spot, join_sems.at[sent]).wait()
            sent += 1
        width = part[0] if part else sum(sources[index].shape[1] for index in panels)
        low, high = part[1:] if part[1:] else (0, rows)
        owner = lax.rem(me + (blocks - chip * cores), blocks)
        owner = jnp.bitwise_xor(owner, flip)
        column = pl.multiple_of(owner * rows + first, 128)
        for row in range(low, high, strip):
            size = min(strip, high - row)
            slot = len(stores) % 2
            if len(stores) >= 2:
                stores[-2].wait()
            if parts:
                right = joined[:, parts[0][0] : parts[0][0] + width]
            else:
                skip = first if sources[panels[0]].shape[1] == rows else 0
                right = sources[panels[0]][:, skip : skip + width]
            product = jnp.dot(
                left_ref[row : row + size, :], right, preferred_element_type=jnp.float32
            )
            tile[slot, 0:size, 0:width] = (product * inverse).astype(jnp.bfloat16)
            stores.append(
                pltpu.make_async_copy(
                    tile.at[slot, pl.ds(0, size), pl.ds(0, width)],
                    out_ref.at[0, pl.ds(row, size), pl.ds(column, width)],
                    sems.at[slot],
                )
            )
            stores[-1].start()
    for store in stores[-2:]:
        store.wait()


def gram(blocks, cores, count, left, groups, before, cost):
    rows, slots = left.shape
    arrays, layout = [], []
    for panels, place in groups:
        layout.append((list(range(len(arrays), len(arrays) + len(panels))), place))
        arrays += panels
    joined = [array for panels, _ in groups if len(panels) > 1 for array in panels]
    widest = max(sum(array.shape[1] for array in panels) for panels, _ in groups)
    strip = min(rows, 512 if widest > 512 else 1024)
    args = [count, left, *arrays]
    specs = [whole] * len(args)
    if before is not None:
        args.append(before)
        specs.append(anywhere)
    return pl.pallas_call(
        functools.partial(gram_kernel, blocks, cores, strip, layout, len(arrays)),
        in_specs=specs,
        out_specs=anywhere,
        out_shape=jax.ShapeDtypeStruct((1, rows, rows * blocks), jnp.bfloat16),
        scratch_shapes=[
            pltpu.VMEM((slots, max(sum(array.shape[1] for array in joined), 128)), jnp.bfloat16),
            pltpu.VMEM((2, strip, widest), jnp.bfloat16),
            pltpu.SemaphoreType.DMA((max(len(joined), 1),)),
            pltpu.SemaphoreType.DMA((2,)),
        ],
        input_output_aliases={} if before is None else {len(args) - 1: 0},
        compiler_params=pltpu.CompilerParams(vmem_limit_bytes=VMEM),
        cost_estimate=cost,
        name="gram",
    )(*args)


def after(value, *others):
    return lax.optimization_barrier((value, *others))[0]


def shards(expression, cell_type, size_factor, gene_mean):
    types = lax.axis_size("cells")
    blocks = lax.axis_size("blk")
    shard_rows, panel = expression.shape
    cap = 2 * shard_rows // types
    assert types & (types - 1) == 0
    widths = [256] * (panel // 256)
    chunks = len(widths)
    starts = [sum(widths[:k]) for k in range(chunks)]
    cores = 2
    chips = blocks // cores
    window = 3

    packed = pack(types, cap, widths, cell_type, size_factor, expression)

    def swap(block, by):
        return lax.ppermute(block, "cells", [(s, s ^ by) for s in range(types)])

    def across(panel_, by):
        return lax.ppermute(panel_, "blk", [(b, (b + by * cores) % blocks) for b in range(blocks)])

    def side(name, panel_, *waits):
        with jax.named_scope(name):
            return lax.ppermute(after(panel_, *waits), "blk", [(b, b ^ 1) for b in range(blocks)])

    mean = jnp.broadcast_to(after(gene_mean, packed[0][0]), (8, panel))

    order = sorted(range(1, types), key=lambda j: (j == 2, j == 1, -j))
    left, own, out, far, before = None, None, None, [], None
    for k in range(chunks):
        arrived = [packed[k][0]]
        for j in order:
            block = packed[k][j]
            if k:
                waits = [mean] if k == 1 else [out] if out is not None and j == 2 else []
                block = after(block, before[len(arrived)], *waits)
            with jax.named_scope(f"cells_{j}_chunk_{k}"):
                arrived.append(swap(block, j))
        before = list(arrived)
        if k >= 2 and chunks == 4:
            low, high = starts[k - 1], starts[k]
            if k == 2:
                groups = [([own], (0, 0, 0, high, 0, high))]
                groups += [([p], (d, 0, 0, widths[0], 0, high)) for d, p in enumerate(far[0], 1)]
            else:
                groups = [([own], (0, 0, low, high - low, 0, high))]
                groups += [([own], (0, 0, 0, low, low, high))]
                for d in range(1, chips):
                    groups.append(([far[0][d - 1]], (d, 0, 0, widths[0], low, high)))
                    groups.append(([far[1][d - 1]], (d, 0, starts[1], widths[1], 0, high)))
            out = gram(blocks, cores, count, left, groups, out, brief)
            arrived[0] = after(arrived[0], out)
        if k == 1:
            with jax.named_scope("far_local"):
                local = [across(packed[-1][0], d) for d in range(1, chips)]
            arrived[0] = after(arrived[0], *local)
        if k >= 2:
            arrived[0] = after(arrived[0], *far[k - 2])
        if k == 0:
            first = arrived
        gather = []
        if k == chunks - 1 and k > 1:
            gather = [[got[d] for got in far[: k - 1]] for d in range(chips - 1)]
        counts, late = k == min(1, chunks - 2), k == chunks - 1
        left, own, *rest = standardize(
            types, cap, mean, starts[k], arrived, first, left, own, gather, late, counts
        )
        if counts:
            count = rest.pop(0)
        scaled, joined = rest[-1], rest[:-1]
        if k < chunks - 1:
            with jax.named_scope(f"far_{k}"):
                far.append([across(scaled, d) for d in range(1, chips)])

    multiply = functools.partial(gram, blocks, cores, count, left)
    last = chunks - 1
    near = side("near", own)
    sent = scaled
    joined_near = [[side("far_near", p)] for p in joined] or [[]] * (chips - 1)
    joined = [[p] for p in joined] or [[]] * (chips - 1)
    if out is None:
        out = multiply([([own], (0, 0, 0))], None, brief)
    else:
        edge = starts[last]
        groups = [
            ([own], (0, 0, 0, panel, edge, panel)),
            ([own], (0, 0, edge, panel - edge, 0, edge)),
        ]
        out = multiply(groups, out, brief)
    final = [across(after(sent, out), d) for d in range(1, chips)]
    second = [side(f"far_near_{last - 1}", p, own) for p in far[last - 1]]
    if chunks == 4:
        groups = []
        for i, p in enumerate(joined):
            groups.append((p, (i + 1, 0, 0, starts[2], starts[3], panel)))
            groups.append(([far[2][i]], (i + 1, 0, starts[2])))
    else:
        groups = [([*p, far[last - 1][i]], (i + 1, 0, 0)) for i, p in enumerate(joined)]
    out = multiply(groups, out, lengthy)
    groups = [([near], (0, 1, 0))]
    groups += [([*p, second[i]], (i + 1, 1, 0)) for i, p in enumerate(joined_near)]
    out = multiply(groups, out, brief)
    final = [
        finish(types, cap, packed[0][0], near_by, after(got, out))
        for near_by, got in zip(local, final)
    ]
    final_near = [side(f"far_near_{last}", p) for p in final]
    edge = starts[last]
    out = multiply([([p], (d, 0, edge)) for d, p in enumerate(final, 1)], out, brief)
    return multiply([([p], (d, 1, edge)) for d, p in enumerate(final_near, 1)], out, brief)


def solution(mesh):
    placed = (
        P(("parts", "cells"), "blk"),
        P(("parts", "cells")),
        P(("parts", "cells")),
        P(("parts", "blk")),
    )
    return jax.shard_map(
        shards,
        mesh=mesh,
        in_specs=placed,
        out_specs=P(("parts", "cells"), "blk", None),
        check_vma=False,
    )
```

```python
import functools

import jax
import jax.numpy as jnp
from jax import lax
from jax.experimental import pallas as pl
from jax.experimental.pallas import tpu as pltpu
from jax.sharding import PartitionSpec as P

dispersion = 100.0
epsilon = 1e-05
TILE = 16
VMEM = 16 * 1024 * 1024

brief = pl.CostEstimate(flops=1024, bytes_accessed=1024, transcendentals=0)
lengthy = pl.CostEstimate(flops=2 * 10**10, bytes_accessed=1024, transcendentals=0)
whole = pl.BlockSpec(memory_space=pltpu.VMEM)
anywhere = pl.BlockSpec(memory_space=pl.ANY)


def pack_kernel(types, cap, widths, type_ref, factor_ref, expr_ref, *outs):
    rows = expr_ref.shape[0]
    home = lax.axis_index("cells")
    kind = type_ref[...].reshape(1, rows)
    rel = jnp.bitwise_xor(kind, home)
    lines = max(types, 8)
    hot = lax.broadcasted_iota(jnp.int32, (lines, rows), 0) == rel
    hot_f = jnp.where(hot, 1.0, 0.0)
    upper = jnp.where(
        lax.broadcasted_iota(jnp.int32, (rows, rows), 0)
        <= lax.broadcasted_iota(jnp.int32, (rows, rows), 1),
        1.0,
        0.0,
    ).astype(jnp.bfloat16)
    running = jnp.dot(hot_f.astype(jnp.bfloat16), upper, preferred_element_type=jnp.float32)
    rank = jnp.sum(hot_f * running, axis=0, keepdims=True) - 1.0
    slot = rel * cap + rank.astype(jnp.int32)
    factor = factor_ref[...].astype(jnp.float32).reshape(1, rows)
    factor = jnp.broadcast_to(factor, (TILE, rows)).astype(jnp.bfloat16)
    values = expr_ref[...]
    for j in range(types):
        place = jnp.where(
            lax.broadcasted_iota(jnp.int32, (cap, rows), 0) + j * cap == slot, 1.0, 0.0
        ).astype(jnp.bfloat16)
        block = jnp.dot(place, values, preferred_element_type=jnp.float32).astype(jnp.bfloat16)
        start = 0
        for k, width in enumerate(widths):
            outs[k * types + j][0:cap, :] = block[:, start : start + width]
            start += width
        line = lax.dot_general(
            factor, place, (((1,), (1,)), ((), ())), preferred_element_type=jnp.float32
        )
        row = lax.broadcasted_iota(jnp.int32, (TILE, 1), 0)
        width = widths[0]
        tail = jnp.zeros((TILE, min(width, cap)), jnp.float32)
        for i in range(pl.cdiv(cap, width)):
            tail = jnp.where(row == i, line[:, i * width : min((i + 1) * width, cap)], tail)
        outs[j][cap : cap + TILE, 0 : min(width, cap)] = tail.astype(jnp.bfloat16)


def pack(types, cap, widths, cell_type, size_factor, expression):
    rows = expression.shape[0]
    shapes = [
        jax.ShapeDtypeStruct((cap + (TILE if k == 0 else 0), width), jnp.bfloat16)
        for k, width in enumerate(widths)
        for _ in range(types)
    ]
    flat = pl.pallas_call(
        functools.partial(pack_kernel, types, cap, widths),
        out_shape=shapes,
        in_specs=[whole] * 3,
        out_specs=[whole] * len(shapes),
        compiler_params=pltpu.CompilerParams(vmem_limit_bytes=VMEM),
        cost_estimate=brief,
        name="pack",
    )(cell_type, size_factor, expression)
    return [flat[k * types : (k + 1) * types] for k in range(len(widths))]


def factor_column(cap, lead, tail_ref, base):
    piece = min(lead, cap)
    column = jnp.zeros((cap, 1), jnp.float32)
    for i in range(pl.cdiv(cap, lead)):
        line = tail_ref[base : base + TILE, 0:piece].astype(jnp.float32)[i : i + 1, :]
        diagonal = (
            lax.broadcasted_iota(jnp.int32, (cap, piece), 0)
            == lax.broadcasted_iota(jnp.int32, (cap, piece), 1) + i * lead
        )
        column += jnp.sum(jnp.where(diagonal, line, 0.0), axis=1, keepdims=True)
    return column


def residuals(column, mean, levels):
    live = column > 0.0
    expected = jnp.where(live, column * mean, 1.0)
    return jnp.where(
        live,
        (levels.astype(jnp.float32) - expected)
        * lax.rsqrt(expected + expected * expected * (1.0 / dispersion)),
        0.0,
    )


def thirds(value):
    parts = []
    for _ in range(3):
        parts.append(value.astype(jnp.bfloat16).astype(jnp.float32))
        value = value - parts[-1]
    return parts


def standardize_kernel(types, cap, lead, separate, start, gathered, late, counts, mean_ref, *refs):
    blocks = refs[:types]
    tails = refs[types : 2 * types] if separate else blocks
    base = 0 if separate else cap
    refs = refs[2 * types :] if separate else refs[types:]
    outputs = 3 + counts + (gathered[0] if gathered else 0)
    outs, scratch = list(refs[: len(refs) - (4 if late else 3)]), refs[-4 if late else -3 :]
    outs = outs[len(outs) - outputs :]
    turned_ref, all_ref = outs[:2]
    count_ref = outs[2] if counts else None
    joined_refs = outs[2 + counts : outputs - 1]
    if late:
        sent_ref, (work, turned, sems, scaled_ref) = outs[-1], scratch
    else:
        scaled_ref, (work, turned, sems) = outs[-1], scratch
    copies = []
    if gathered:
        sources = refs[: len(gathered[1])]
        for source, (joined, column) in zip(sources, gathered[1]):
            spot = joined_refs[joined].at[:, pl.ds(column, source.shape[1])]
            copies.append(pltpu.make_async_copy(source, spot, sems.at[2 + len(copies)]))
            copies[-1].start()
    width = work.shape[1]
    mean = mean_ref[0:1, start : start + width]
    total = jnp.zeros((1, width), jnp.float32)
    count = jnp.zeros((1, 1), jnp.float32)
    alive = []
    for j in range(types):
        column = factor_column(cap, lead, tails[j], base)
        live = column > 0.0
        alive.append(live)
        count += jnp.sum(jnp.where(live, 1.0, 0.0), axis=0, keepdims=True)
        residual = residuals(column, mean, blocks[j][0:cap, :])
        work[j * cap : (j + 1) * cap, :] = residual
        total += jnp.sum(residual, axis=0, keepdims=True)
    center = total / count
    square = jnp.zeros((1, width), jnp.float32)
    for j in range(types):
        centered = jnp.where(alive[j], work[j * cap : (j + 1) * cap, :] - center, 0.0)
        work[j * cap : (j + 1) * cap, :] = centered
        square += jnp.sum(centered * centered, axis=0, keepdims=True)
    scale = lax.rsqrt(square / count + epsilon)
    for j in range(types):
        scaled = work[j * cap : (j + 1) * cap, :] * scale
        scaled_ref[j * cap : (j + 1) * cap, :] = scaled.astype(jnp.bfloat16)
        work[j * cap : (j + 1) * cap, :] = scaled
    slots = types * cap
    columns = pl.ds(start, width)
    copies.append(pltpu.make_async_copy(scaled_ref, all_ref.at[:, columns], sems.at[0]))
    copies[-1].start()
    turned[...] = jnp.transpose(work[...]).astype(jnp.bfloat16)
    copies.append(pltpu.make_async_copy(turned, turned_ref.at[columns, :], sems.at[1]))
    copies[-1].start()
    if late:
        sent_ref[0 : slots - cap, :] = scaled_ref[cap:slots, :]
        row = lax.broadcasted_iota(jnp.int32, (TILE, 1), 0)
        notes = jnp.zeros((TILE, width), jnp.float32)
        for i, part in enumerate(thirds(center) + thirds(scale) + thirds(mean)):
            notes = jnp.where(row == i, part, notes)
        sent_ref[slots - cap : slots - cap + TILE, :] = notes.astype(jnp.bfloat16)
    for copy in copies:
        copy.wait()
    if counts:
        count_ref[...] = jnp.broadcast_to(count, count_ref.shape)


def standardize(types, cap, mean, start, blocks, first, left, own, gather, late, counts):
    lead, width = first[0].shape[1], blocks[0].shape[1]
    panel = mean.shape[1]
    separate = first is not blocks
    slots = types * cap
    specs = [whole] * (1 + types)
    args = [mean, *blocks]
    if separate:
        specs += [pl.BlockSpec((TILE, lead), lambda i: (cap // TILE, 0))] * types
        args += list(first)
    shapes = [
        jax.ShapeDtypeStruct((panel, slots), jnp.bfloat16),
        jax.ShapeDtypeStruct((slots, panel), jnp.bfloat16),
    ]
    if counts:
        shapes.append(jax.ShapeDtypeStruct((8, 128), jnp.float32))
    gathered = []
    for i, panels in enumerate(gather):
        column = 0
        for array in panels:
            gathered.append((i, column))
            column += array.shape[1]
            specs.append(whole)
            args.append(array)
        shapes.append(jax.ShapeDtypeStruct((slots, column), jnp.bfloat16))
    rows = slots - cap + TILE if late else slots
    shapes.append(jax.ShapeDtypeStruct((rows, width), jnp.bfloat16))
    aliases = {}
    for value, output in ((left, 0), (own, 1)):
        if value is not None:
            aliases[len(args)] = output
            specs.append(anywhere)
            args.append(value)
    scratch = [
        pltpu.VMEM((slots, width), jnp.float32),
        pltpu.VMEM((width, slots), jnp.bfloat16),
        pltpu.SemaphoreType.DMA((2 + len(gathered),)),
    ]
    if late:
        scratch.append(pltpu.VMEM((slots, width), jnp.bfloat16))
    return pl.pallas_call(
        functools.partial(
            standardize_kernel,
            types,
            cap,
            lead,
            separate,
            start,
            (len(gather), gathered) if gathered else None,
            late,
            int(counts),
        ),
        grid=(1,),
        out_shape=shapes,
        in_specs=specs,
        out_specs=[anywhere, anywhere] + [whole] * (len(shapes) - 2),
        scratch_shapes=scratch,
        input_output_aliases=aliases,
        compiler_params=pltpu.CompilerParams(vmem_limit_bytes=VMEM),
        cost_estimate=lengthy,
        name="standardize",
    )(*args)


def finish_kernel(cap, lead, sent_ref, local_ref, tail_ref, out_ref):
    rest = out_ref.shape[0] - cap
    out_ref[cap : cap + rest, :] = sent_ref[0:rest, :]
    notes = sent_ref[rest : rest + TILE, :].astype(jnp.float32)
    center, scale, mean = [
        notes[i : i + 1, :] + notes[i + 1 : i + 2, :] + notes[i + 2 : i + 3, :] for i in (0, 3, 6)
    ]
    column = factor_column(cap, lead, tail_ref, 0)
    residual = residuals(column, mean, local_ref[0:cap, :])
    centered = jnp.where(column > 0.0, residual - center, 0.0)
    out_ref[0:cap, :] = (centered * scale).astype(jnp.bfloat16)


def finish(types, cap, first, local, sent):
    lead, width = first.shape[1], sent.shape[1]
    return pl.pallas_call(
        functools.partial(finish_kernel, cap, lead),
        grid=(1,),
        out_shape=jax.ShapeDtypeStruct((types * cap, width), jnp.bfloat16),
        in_specs=[whole, whole, pl.BlockSpec((TILE, lead), lambda i: (cap // TILE, 0))],
        out_specs=whole,
        compiler_params=pltpu.CompilerParams(vmem_limit_bytes=VMEM),
        cost_estimate=brief,
        name="finish",
    )(sent, local, first)


def strip_rows(width, rows):
    return rows if width <= 512 or rows <= 768 else 512


def gram_kernel(blocks, cores, groups, arrays, count_ref, left_ref, *refs):
    sources = refs[:arrays]
    out_ref, joined, tile, join_sems, sems = refs[-5:]
    rows, slots = left_ref.shape
    inverse = 1.0 / count_ref[0:1, 0:1]
    me = lax.axis_index("blk")

    joins, column = [], 0
    for panels, _ in groups:
        joins.append([])
        if len(panels) > 1:
            for index in panels:
                width = sources[index].shape[1]
                spot = joined.at[:, pl.ds(column, width)]
                joins[-1].append((column, sources[index], spot))
                column += width
    sent = 0
    for parts in joins:
        for _, source, spot in parts:
            pltpu.make_async_copy(source, spot, join_sems.at[sent]).start()
            sent += 1
    stores, sent = [], 0
    for (panels, (chip, flip, first, *part)), parts in zip(groups, joins):
        for _, source, spot in parts:
            pltpu.make_async_copy(source, spot, join_sems.at[sent]).wait()
            sent += 1
        width = part[0] if part else sum(sources[index].shape[1] for index in panels)
        low, high = part[1:] if part[1:] else (0, rows)
        owner = lax.rem(me + (blocks - chip * cores), blocks)
        owner = jnp.bitwise_xor(owner, flip)
        column = pl.multiple_of(owner * rows + first, 128)
        strip = strip_rows(width, high - low)
        for row in range(low, high, strip):
            size = min(strip, high - row)
            slot = len(stores) % 2
            if len(stores) >= 2:
                stores[-2].wait()
            if parts:
                right = joined[:, parts[0][0] : parts[0][0] + width]
            else:
                skip = first if part else 0
                right = sources[panels[0]][:, skip : skip + width]
            product = jnp.dot(
                left_ref[row : row + size, :], right, preferred_element_type=jnp.float32
            )
            tile[slot, 0:size, 0:width] = (product * inverse).astype(jnp.bfloat16)
            stores.append(
                pltpu.make_async_copy(
                    tile.at[slot, pl.ds(0, size), pl.ds(0, width)],
                    out_ref.at[0, pl.ds(row, size), pl.ds(column, width)],
                    sems.at[slot],
                )
            )
            stores[-1].start()
    for store in stores[-2:]:
        store.wait()


def gram(blocks, cores, count, left, groups, before, cost):
    rows, slots = left.shape
    arrays, layout = [], []
    for panels, place in groups:
        layout.append((list(range(len(arrays), len(arrays) + len(panels))), place))
        arrays += panels
    joined = [array for panels, _ in groups if len(panels) > 1 for array in panels]
    widest = max(sum(array.shape[1] for array in panels) for panels, _ in groups)
    args = [count, left, *arrays]
    specs = [whole] * len(args)
    if before is not None:
        args.append(before)
        specs.append(anywhere)
    return pl.pallas_call(
        functools.partial(gram_kernel, blocks, cores, layout, len(arrays)),
        in_specs=specs,
        out_specs=anywhere,
        out_shape=jax.ShapeDtypeStruct((1, rows, rows * blocks), jnp.bfloat16),
        scratch_shapes=[
            pltpu.VMEM((slots, max(sum(array.shape[1] for array in joined), 128)), jnp.bfloat16),
            pltpu.VMEM((2, rows, widest), jnp.bfloat16),
            pltpu.SemaphoreType.DMA((max(len(joined), 1),)),
            pltpu.SemaphoreType.DMA((2,)),
        ],
        input_output_aliases={} if before is None else {len(args) - 1: 0},
        compiler_params=pltpu.CompilerParams(vmem_limit_bytes=VMEM),
        cost_estimate=cost,
        name="gram",
    )(*args)


def after(value, *others):
    return lax.optimization_barrier((value, *others))[0]


def shards(expression, cell_type, size_factor, gene_mean):
    types = lax.axis_size("cells")
    blocks = lax.axis_size("blk")
    shard_rows, panel = expression.shape
    cap = 2 * shard_rows // types
    assert types & (types - 1) == 0
    widths = [256] * (panel // 256)
    chunks = len(widths)
    starts = [sum(widths[:k]) for k in range(chunks)]
    cores = 2
    chips = blocks // cores
    window = 3

    packed = pack(types, cap, widths, cell_type, size_factor, expression)

    def swap(block, by):
        return lax.ppermute(block, "cells", [(s, s ^ by) for s in range(types)])

    def across(panel_, by):
        return lax.ppermute(panel_, "blk", [(b, (b + by * cores) % blocks) for b in range(blocks)])

    def side(name, panel_, *waits):
        with jax.named_scope(name):
            return lax.ppermute(after(panel_, *waits), "blk", [(b, b ^ 1) for b in range(blocks)])

    mean = jnp.broadcast_to(after(gene_mean, packed[0][0]), (8, panel))

    order = sorted(range(1, types), key=lambda j: (j == 2, j == 1, -j))
    left, own, out, far, before = None, None, None, [], None
    for k in range(chunks):
        arrived = [packed[k][0]]
        for j in order:
            block = packed[k][j]
            if k:
                block = after(block, before[len(arrived)], *([mean] if k == 1 else []))
            with jax.named_scope(f"cells_{j}_chunk_{k}"):
                arrived.append(swap(block, j))
        before = list(arrived)
        if k == 1:
            with jax.named_scope("far_local"):
                local = [across(packed[-1][0], d) for d in range(1, chips)]
            arrived[0] = after(arrived[0], *local)
        if k >= 2:
            arrived[0] = after(arrived[0], *far[k - 2])
        if k == 0:
            first = arrived
        gather = []
        if k == chunks - 1 and k > 1:
            groups = [([own], (0, 0, 0, starts[k], 0, starts[k]))]
            out = gram(blocks, cores, count, left, groups, None, brief)
            arrived[0] = after(arrived[0], out)
            gather = [[got[d] for got in far[: k - 1]] for d in range(chips - 1)]
        counts, late = k == chunks - 2, k == chunks - 1
        left, own, *rest = standardize(
            types, cap, mean, starts[k], arrived, first, left, own, gather, late, counts
        )
        if counts:
            count = rest.pop(0)
        scaled, joined = rest[-1], rest[:-1]
        if k < chunks - 1:
            with jax.named_scope(f"far_{k}"):
                far.append([across(scaled, d) for d in range(1, chips)])

    multiply = functools.partial(gram, blocks, cores, count, left)
    last = chunks - 1
    near = side("near", own)
    sent = scaled
    joined_near = [[side("far_near", p)] for p in joined] or [[]] * (chips - 1)
    joined = [[p] for p in joined] or [[]] * (chips - 1)
    if out is None:
        out = multiply([([own], (0, 0, 0))], None, brief)
    else:
        edge = starts[last]
        groups = [
            ([own], (0, 0, 0, panel, edge, panel)),
            ([own], (0, 0, edge, panel - edge, 0, edge)),
        ]
        out = multiply(groups, out, brief)
    final = [across(after(sent, out), d) for d in range(1, chips)]
    second = [side(f"far_near_{last - 1}", p, own) for p in far[last - 1]]
    groups = [([*p, far[last - 1][i]], (i + 1, 0, 0)) for i, p in enumerate(joined)]
    out = multiply(groups, out, lengthy)
    groups = [([near], (0, 1, 0))]
    groups += [([*p, second[i]], (i + 1, 1, 0)) for i, p in enumerate(joined_near)]
    out = multiply(groups, out, brief)
    final = [
        finish(types, cap, packed[0][0], near_by, after(got, out))
        for near_by, got in zip(local, final)
    ]
    final_near = [side(f"far_near_{last}", p) for p in final]
    edge = starts[last]
    out = multiply([([p], (d, 0, edge)) for d, p in enumerate(final, 1)], out, brief)
    return multiply([([p], (d, 1, edge)) for d, p in enumerate(final_near, 1)], out, brief)


def solution(mesh):
    placed = (
        P(("parts", "cells"), "blk"),
        P(("parts", "cells")),
        P(("parts", "cells")),
        P(("parts", "blk")),
    )
    return jax.shard_map(
        shards,
        mesh=mesh,
        in_specs=placed,
        out_specs=P(("parts", "cells"), "blk", None),
        check_vma=False,
    )
```

```python
import functools

import jax
import jax.numpy as jnp
from jax import lax
from jax.experimental import pallas as pl
from jax.experimental.pallas import tpu as pltpu
from jax.sharding import PartitionSpec as P

dispersion = 100.0
epsilon = 1e-05
TILE = 16
VMEM = 16 * 1024 * 1024

brief = pl.CostEstimate(flops=1024, bytes_accessed=1024, transcendentals=0)
lengthy = pl.CostEstimate(flops=2 * 10**10, bytes_accessed=1024, transcendentals=0)
whole = pl.BlockSpec(memory_space=pltpu.VMEM)
anywhere = pl.BlockSpec(memory_space=pl.ANY)


def pack_kernel(types, cap, widths, type_ref, factor_ref, expr_ref, *outs):
    rows = expr_ref.shape[0]
    home = lax.axis_index("cells")
    kind = type_ref[...].reshape(1, rows)
    rel = jnp.bitwise_xor(kind, home)
    lines = max(types, 8)
    hot = lax.broadcasted_iota(jnp.int32, (lines, rows), 0) == rel
    hot_f = jnp.where(hot, 1.0, 0.0)
    upper = jnp.where(
        lax.broadcasted_iota(jnp.int32, (rows, rows), 0)
        <= lax.broadcasted_iota(jnp.int32, (rows, rows), 1),
        1.0,
        0.0,
    ).astype(jnp.bfloat16)
    running = jnp.dot(hot_f.astype(jnp.bfloat16), upper, preferred_element_type=jnp.float32)
    rank = jnp.sum(hot_f * running, axis=0, keepdims=True) - 1.0
    slot = rel * cap + rank.astype(jnp.int32)
    factor = factor_ref[...].astype(jnp.float32).reshape(1, rows)
    factor = jnp.broadcast_to(factor, (TILE, rows)).astype(jnp.bfloat16)
    values = expr_ref[...]
    for j in range(types):
        place = jnp.where(
            lax.broadcasted_iota(jnp.int32, (cap, rows), 0) + j * cap == slot, 1.0, 0.0
        ).astype(jnp.bfloat16)
        block = jnp.dot(place, values, preferred_element_type=jnp.float32).astype(jnp.bfloat16)
        start = 0
        for k, width in enumerate(widths):
            outs[k * types + j][0:cap, :] = block[:, start : start + width]
            start += width
        line = lax.dot_general(
            factor, place, (((1,), (1,)), ((), ())), preferred_element_type=jnp.float32
        )
        row = lax.broadcasted_iota(jnp.int32, (TILE, 1), 0)
        width = widths[0]
        tail = jnp.zeros((TILE, min(width, cap)), jnp.float32)
        for i in range(pl.cdiv(cap, width)):
            tail = jnp.where(row == i, line[:, i * width : min((i + 1) * width, cap)], tail)
        outs[j][cap : cap + TILE, 0 : min(width, cap)] = tail.astype(jnp.bfloat16)


def pack(types, cap, widths, cell_type, size_factor, expression):
    rows = expression.shape[0]
    shapes = [
        jax.ShapeDtypeStruct((cap + (TILE if k == 0 else 0), width), jnp.bfloat16)
        for k, width in enumerate(widths)
        for _ in range(types)
    ]
    flat = pl.pallas_call(
        functools.partial(pack_kernel, types, cap, widths),
        out_shape=shapes,
        in_specs=[whole] * 3,
        out_specs=[whole] * len(shapes),
        compiler_params=pltpu.CompilerParams(vmem_limit_bytes=VMEM),
        cost_estimate=brief,
        name="pack",
    )(cell_type, size_factor, expression)
    return [flat[k * types : (k + 1) * types] for k in range(len(widths))]


def factor_column(cap, lead, tail_ref, base):
    piece = min(lead, cap)
    column = jnp.zeros((cap, 1), jnp.float32)
    for i in range(pl.cdiv(cap, lead)):
        line = tail_ref[base : base + TILE, 0:piece].astype(jnp.float32)[i : i + 1, :]
        diagonal = (
            lax.broadcasted_iota(jnp.int32, (cap, piece), 0)
            == lax.broadcasted_iota(jnp.int32, (cap, piece), 1) + i * lead
        )
        column += jnp.sum(jnp.where(diagonal, line, 0.0), axis=1, keepdims=True)
    return column


def residuals(column, mean, levels):
    live = column > 0.0
    expected = jnp.where(live, column * mean, 1.0)
    return jnp.where(
        live,
        (levels.astype(jnp.float32) - expected)
        * lax.rsqrt(expected + expected * expected * (1.0 / dispersion)),
        0.0,
    )


def thirds(value):
    parts = []
    for _ in range(3):
        parts.append(value.astype(jnp.bfloat16).astype(jnp.float32))
        value = value - parts[-1]
    return parts


def standardize_kernel(types, cap, lead, separate, start, gathered, late, counts, mean_ref, *refs):
    blocks = refs[:types]
    tails = refs[types : 2 * types] if separate else blocks
    base = 0 if separate else cap
    refs = refs[2 * types :] if separate else refs[types:]
    outputs = 3 + counts + (gathered[0] if gathered else 0)
    outs, scratch = list(refs[: len(refs) - (4 if late else 3)]), refs[-4 if late else -3 :]
    outs = outs[len(outs) - outputs :]
    turned_ref, all_ref = outs[:2]
    count_ref = outs[2] if counts else None
    joined_refs = outs[2 + counts : outputs - 1]
    if late:
        sent_ref, (work, turned, sems, scaled_ref) = outs[-1], scratch
    else:
        scaled_ref, (work, turned, sems) = outs[-1], scratch
    copies = []
    if gathered:
        sources = refs[: len(gathered[1])]
        for source, (joined, column) in zip(sources, gathered[1]):
            spot = joined_refs[joined].at[:, pl.ds(column, source.shape[1])]
            copies.append(pltpu.make_async_copy(source, spot, sems.at[2 + len(copies)]))
            copies[-1].start()
    width = work.shape[1]
    mean = mean_ref[0:1, start : start + width]
    total = jnp.zeros((1, width), jnp.float32)
    count = jnp.zeros((1, 1), jnp.float32)
    alive = []
    for j in range(types):
        column = factor_column(cap, lead, tails[j], base)
        live = column > 0.0
        alive.append(live)
        count += jnp.sum(jnp.where(live, 1.0, 0.0), axis=0, keepdims=True)
        residual = residuals(column, mean, blocks[j][0:cap, :])
        work[j * cap : (j + 1) * cap, :] = residual
        total += jnp.sum(residual, axis=0, keepdims=True)
    center = total / count
    square = jnp.zeros((1, width), jnp.float32)
    for j in range(types):
        centered = jnp.where(alive[j], work[j * cap : (j + 1) * cap, :] - center, 0.0)
        work[j * cap : (j + 1) * cap, :] = centered
        square += jnp.sum(centered * centered, axis=0, keepdims=True)
    scale = lax.rsqrt(square / count + epsilon)
    for j in range(types):
        scaled = work[j * cap : (j + 1) * cap, :] * scale
        scaled_ref[j * cap : (j + 1) * cap, :] = scaled.astype(jnp.bfloat16)
        work[j * cap : (j + 1) * cap, :] = scaled
    slots = types * cap
    columns = pl.ds(start, width)
    copies.append(pltpu.make_async_copy(scaled_ref, all_ref.at[:, columns], sems.at[0]))
    copies[-1].start()
    turned[...] = jnp.transpose(work[...]).astype(jnp.bfloat16)
    copies.append(pltpu.make_async_copy(turned, turned_ref.at[columns, :], sems.at[1]))
    copies[-1].start()
    if late:
        sent_ref[0 : slots - cap, :] = scaled_ref[cap:slots, :]
        row = lax.broadcasted_iota(jnp.int32, (TILE, 1), 0)
        notes = jnp.zeros((TILE, width), jnp.float32)
        for i, part in enumerate(thirds(center) + thirds(scale) + thirds(mean)):
            notes = jnp.where(row == i, part, notes)
        sent_ref[slots - cap : slots - cap + TILE, :] = notes.astype(jnp.bfloat16)
    for copy in copies:
        copy.wait()
    if counts:
        count_ref[...] = jnp.broadcast_to(count, count_ref.shape)


def standardize(types, cap, mean, start, blocks, first, left, own, gather, late, counts):
    lead, width = first[0].shape[1], blocks[0].shape[1]
    panel = mean.shape[1]
    separate = first is not blocks
    slots = types * cap
    specs = [whole] * (1 + types)
    args = [mean, *blocks]
    if separate:
        specs += [pl.BlockSpec((TILE, lead), lambda i: (cap // TILE, 0))] * types
        args += list(first)
    shapes = [
        jax.ShapeDtypeStruct((panel, slots), jnp.bfloat16),
        jax.ShapeDtypeStruct((slots, panel), jnp.bfloat16),
    ]
    if counts:
        shapes.append(jax.ShapeDtypeStruct((8, 128), jnp.float32))
    gathered = []
    for i, panels in enumerate(gather):
        column = 0
        for array in panels:
            gathered.append((i, column))
            column += array.shape[1]
            specs.append(whole)
            args.append(array)
        shapes.append(jax.ShapeDtypeStruct((slots, column), jnp.bfloat16))
    rows = slots - cap + TILE if late else slots
    shapes.append(jax.ShapeDtypeStruct((rows, width), jnp.bfloat16))
    aliases = {}
    for value, output in ((left, 0), (own, 1)):
        if value is not None:
            aliases[len(args)] = output
            specs.append(anywhere)
            args.append(value)
    scratch = [
        pltpu.VMEM((slots, width), jnp.float32),
        pltpu.VMEM((width, slots), jnp.bfloat16),
        pltpu.SemaphoreType.DMA((2 + len(gathered),)),
    ]
    if late:
        scratch.append(pltpu.VMEM((slots, width), jnp.bfloat16))
    return pl.pallas_call(
        functools.partial(
            standardize_kernel,
            types,
            cap,
            lead,
            separate,
            start,
            (len(gather), gathered) if gathered else None,
            late,
            int(counts),
        ),
        grid=(1,),
        out_shape=shapes,
        in_specs=specs,
        out_specs=[anywhere, anywhere] + [whole] * (len(shapes) - 2),
        scratch_shapes=scratch,
        input_output_aliases=aliases,
        compiler_params=pltpu.CompilerParams(vmem_limit_bytes=VMEM),
        cost_estimate=lengthy,
        name="standardize",
    )(*args)


def finish_kernel(cap, lead, sent_ref, local_ref, tail_ref, out_ref):
    rest = out_ref.shape[0] - cap
    out_ref[cap : cap + rest, :] = sent_ref[0:rest, :]
    notes = sent_ref[rest : rest + TILE, :].astype(jnp.float32)
    center, scale, mean = [
        notes[i : i + 1, :] + notes[i + 1 : i + 2, :] + notes[i + 2 : i + 3, :] for i in (0, 3, 6)
    ]
    column = factor_column(cap, lead, tail_ref, 0)
    residual = residuals(column, mean, local_ref[0:cap, :])
    centered = jnp.where(column > 0.0, residual - center, 0.0)
    out_ref[0:cap, :] = (centered * scale).astype(jnp.bfloat16)


def finish(types, cap, first, local, sent):
    lead, width = first.shape[1], sent.shape[1]
    return pl.pallas_call(
        functools.partial(finish_kernel, cap, lead),
        grid=(1,),
        out_shape=jax.ShapeDtypeStruct((types * cap, width), jnp.bfloat16),
        in_specs=[whole, whole, pl.BlockSpec((TILE, lead), lambda i: (cap // TILE, 0))],
        out_specs=whole,
        compiler_params=pltpu.CompilerParams(vmem_limit_bytes=VMEM),
        cost_estimate=brief,
        name="finish",
    )(sent, local, first)


def strip_rows(width, rows):
    return rows if width <= 512 else 512


def gram_kernel(blocks, cores, groups, arrays, count_ref, left_ref, *refs):
    sources = refs[:arrays]
    out_ref, joined, tile, join_sems, sems = refs[-5:]
    rows, slots = left_ref.shape
    inverse = 1.0 / count_ref[0:1, 0:1]
    me = lax.axis_index("blk")

    joins, column = [], 0
    for panels, _ in groups:
        joins.append([])
        if len(panels) > 1:
            for index in panels:
                width = sources[index].shape[1]
                spot = joined.at[:, pl.ds(column, width)]
                joins[-1].append((column, sources[index], spot))
                column += width
    sent = 0
    for parts in joins:
        for _, source, spot in parts:
            pltpu.make_async_copy(source, spot, join_sems.at[sent]).start()
            sent += 1
    stores, sent = [], 0
    for (panels, (chip, flip, first, *part)), parts in zip(groups, joins):
        for _, source, spot in parts:
            pltpu.make_async_copy(source, spot, join_sems.at[sent]).wait()
            sent += 1
        width = part[0] if part else sum(sources[index].shape[1] for index in panels)
        low, high = part[1:] if part[1:] else (0, rows)
        owner = lax.rem(me + (blocks - chip * cores), blocks)
        owner = jnp.bitwise_xor(owner, flip)
        column = pl.multiple_of(owner * rows + first, 128)
        strip = strip_rows(width, high - low)
        for row in range(low, high, strip):
            size = min(strip, high - row)
            slot = len(stores) % 2
            if len(stores) >= 2:
                stores[-2].wait()
            if parts:
                right = joined[:, parts[0][0] : parts[0][0] + width]
            else:
                skip = first if part else 0
                right = sources[panels[0]][:, skip : skip + width]
            product = jnp.dot(
                left_ref[row : row + size, :], right, preferred_element_type=jnp.float32
            )
            tile[slot, 0:size, 0:width] = (product * inverse).astype(jnp.bfloat16)
            stores.append(
                pltpu.make_async_copy(
                    tile.at[slot, pl.ds(0, size), pl.ds(0, width)],
                    out_ref.at[0, pl.ds(row, size), pl.ds(column, width)],
                    sems.at[slot],
                )
            )
            stores[-1].start()
    for store in stores[-2:]:
        store.wait()


def gram(blocks, cores, count, left, groups, before, cost):
    rows, slots = left.shape
    arrays, layout = [], []
    for panels, place in groups:
        layout.append((list(range(len(arrays), len(arrays) + len(panels))), place))
        arrays += panels
    joined = [array for panels, _ in groups if len(panels) > 1 for array in panels]
    widest = max(sum(array.shape[1] for array in panels) for panels, _ in groups)
    args = [count, left, *arrays]
    specs = [whole] * len(args)
    if before is not None:
        args.append(before)
        specs.append(anywhere)
    return pl.pallas_call(
        functools.partial(gram_kernel, blocks, cores, layout, len(arrays)),
        in_specs=specs,
        out_specs=anywhere,
        out_shape=jax.ShapeDtypeStruct((1, rows, rows * blocks), jnp.bfloat16),
        scratch_shapes=[
            pltpu.VMEM((slots, max(sum(array.shape[1] for array in joined), 128)), jnp.bfloat16),
            pltpu.VMEM((2, rows, widest), jnp.bfloat16),
            pltpu.SemaphoreType.DMA((max(len(joined), 1),)),
            pltpu.SemaphoreType.DMA((2,)),
        ],
        input_output_aliases={} if before is None else {len(args) - 1: 0},
        compiler_params=pltpu.CompilerParams(vmem_limit_bytes=VMEM),
        cost_estimate=cost,
        name="gram",
    )(*args)


def after(value, *others):
    return lax.optimization_barrier((value, *others))[0]


def shards(expression, cell_type, size_factor, gene_mean):
    types = lax.axis_size("cells")
    blocks = lax.axis_size("blk")
    shard_rows, panel = expression.shape
    cap = 2 * shard_rows // types
    assert types & (types - 1) == 0
    widths = [256] * (panel // 256)
    chunks = len(widths)
    starts = [sum(widths[:k]) for k in range(chunks)]
    cores = 2
    chips = blocks // cores
    window = 3

    packed = pack(types, cap, widths, cell_type, size_factor, expression)

    def swap(block, by):
        return lax.ppermute(block, "cells", [(s, s ^ by) for s in range(types)])

    def across(panel_, by):
        return lax.ppermute(panel_, "blk", [(b, (b + by * cores) % blocks) for b in range(blocks)])

    def side(name, panel_, *waits):
        with jax.named_scope(name):
            return lax.ppermute(after(panel_, *waits), "blk", [(b, b ^ 1) for b in range(blocks)])

    mean = jnp.broadcast_to(after(gene_mean, packed[0][0]), (8, panel))

    order = sorted(range(1, types), key=lambda j: (j == 2, j == 1, -j))
    left, own, out, far, before = None, None, None, [], None
    for k in range(chunks):
        arrived = [packed[k][0]]
        for j in order:
            block = packed[k][j]
            if k:
                block = after(block, before[len(arrived)], *([mean] if k == 1 else []))
            with jax.named_scope(f"cells_{j}_chunk_{k}"):
                arrived.append(swap(block, j))
        before = list(arrived)
        if k == 1:
            with jax.named_scope("far_local"):
                local = [across(packed[-1][0], d) for d in range(1, chips)]
            arrived[0] = after(arrived[0], *local)
        if k >= 2:
            arrived[0] = after(arrived[0], *far[k - 2])
        if k == 0:
            first = arrived
        gather = []
        if k == chunks - 1 and k > 1:
            groups = [([own], (0, 0, 0, starts[k], 0, starts[k]))]
            out = gram(blocks, cores, count, left, groups, None, brief)
            arrived[0] = after(arrived[0], out)
            gather = [[got[d] for got in far[: k - 1]] for d in range(chips - 1)]
        counts, late = k == chunks - 2, k == chunks - 1
        left, own, *rest = standardize(
            types, cap, mean, starts[k], arrived, first, left, own, gather, late, counts
        )
        if counts:
            count = rest.pop(0)
        scaled, joined = rest[-1], rest[:-1]
        if k < chunks - 1:
            with jax.named_scope(f"far_{k}"):
                far.append([across(scaled, d) for d in range(1, chips)])

    multiply = functools.partial(gram, blocks, cores, count, left)
    last = chunks - 1
    near = side("near", own)
    sent = scaled
    joined_near = [[side("far_near", p)] for p in joined] or [[]] * (chips - 1)
    joined = [[p] for p in joined] or [[]] * (chips - 1)
    if out is None:
        out = multiply([([own], (0, 0, 0))], None, brief)
    else:
        edge = starts[last]
        groups = [
            ([own], (0, 0, 0, panel, edge, panel)),
            ([own], (0, 0, edge, panel - edge, 0, edge)),
        ]
        out = multiply(groups, out, brief)
    final = [across(after(sent, out), d) for d in range(1, chips)]
    second = [side(f"far_near_{last - 1}", p, own) for p in far[last - 1]]
    groups = [([*p, far[last - 1][i]], (i + 1, 0, 0)) for i, p in enumerate(joined)]
    out = multiply(groups, out, lengthy)
    groups = [([near], (0, 1, 0))]
    groups += [([*p, second[i]], (i + 1, 1, 0)) for i, p in enumerate(joined_near)]
    out = multiply(groups, out, brief)
    final = [
        finish(types, cap, packed[0][0], near_by, after(got, out))
        for near_by, got in zip(local, final)
    ]
    final_near = [side(f"far_near_{last}", p) for p in final]
    edge = starts[last]
    out = multiply([([p], (d, 0, edge)) for d, p in enumerate(final, 1)], out, brief)
    return multiply([([p], (d, 1, edge)) for d, p in enumerate(final_near, 1)], out, brief)


def solution(mesh):
    placed = (
        P(("parts", "cells"), "blk"),
        P(("parts", "cells")),
        P(("parts", "cells")),
        P(("parts", "blk")),
    )
    return jax.shard_map(
        shards,
        mesh=mesh,
        in_specs=placed,
        out_specs=P(("parts", "cells"), "blk", None),
        check_vma=False,
    )
```
